32 devices in a mesh: gx: 8 (over y, x, core), gy: 4 (over z).
Axes of the slice: x: 2, y: 2, z: 4, core: 2. Of those that a mesh axis runs over, the one named last changes fastest.
Arguments:
- waveforms: bfloat16 [64, 3, 1536], P(('gx', 'gy')), may hold values from -100 to 100
- templates: bfloat16 [1024, 8, 1536], P(('gx', 'gy')), may hold values from -100 to 100
- tpl_stations: int32 [1024, 8], P(('gx', 'gy')), may hold values from 0 to 63, all different within a row; in each aligned block of 32 rows (0 to 31, 32 to 63, ...) at most 8 rows name the same one
- det_station: int32 [2048], P(('gx', 'gy')), may hold values from 0 to 1
- det_time: int32 [2048], P(('gx', 'gy')), may hold values from 64 to 1216
- partner: int32 [2048, 4], P(('gx', 'gy')), may hold values from 0 to 63
Outputs:
- stack: float32 [1024, 1024], P(('gx', 'gy'))
- diffcc: float32 [2048, 4, 128], P(('gx', 'gy'))
The draws below stay inside these ranges and needn't reach their ends.
Inputs may be any that keep to these rules, and one draw needn't show every extreme that they name: `tpl_stations`: each row names 8 different stations; among the templates of one station group no station is named more than 8 times.
All inputs are finite; a program needn't handle non-finite values.
Results may differ from the reference program's by a relative error of at most 0.0007.
Values may be sent and summed in bfloat16 or wider, within the bound.
No kernel may reach another device: no remote copies, remote signals or barrier semaphores. Data moves between devices by JAX's collectives and lax.ppermute only.
A program may use at most 128 MiB of HBM per device.

```python
import math
import jax
import jax.numpy as jnp
import numpy as np
from jax import lax

STA_DEV = 2
TPL_DEV = 32
K = 8
TLEN = 512
NLAG = 1024
DET_DEV = 64
W = 256
DTLAG = 128
STATIONS = 64
TEMPLATES = 1024
DETECTIONS = 2048
SAMPLES = 1536
CAP = 8
N_GX = 8
N_GY = 4


def draw_waveforms(key, part):
    first, second = jax.random.split(key, 2)
    shape = (STATIONS, 3, SAMPLES)
    segments = (SAMPLES + 63) // 64
    envelope = jnp.exp(jax.random.uniform(second, (STATIONS, 3, segments), jnp.float32, 0.0, math.log(10.0)))
    envelope = jnp.repeat(envelope, 64, axis=2)[:, :, :SAMPLES]
    noise = jax.random.normal(first, shape, jnp.float32)
    return jnp.clip(noise * envelope, -100.0, 100.0).astype(jnp.bfloat16)


def draw_templates(key, part):
    first, second = jax.random.split(key, 2)
    shape = (TEMPLATES, K, 3, TLEN)
    scales = jnp.exp(jax.random.uniform(second, (TEMPLATES, K, 3, 1), jnp.float32, 0.0, math.log(10.0)))
    noise = jax.random.normal(first, shape, jnp.float32)
    return jnp.clip(noise * scales, -100.0, 100.0).reshape(TEMPLATES, K, 3 * TLEN).astype(jnp.bfloat16)


def place_ends(result, key, low, largest):
    spot = [jax.random.randint(jax.random.fold_in(key, axis), (), 0, length) for axis, length in enumerate(result.shape)]
    main_axis = result.shape.index(max(result.shape))
    neighbour = spot[:main_axis] + [(spot[main_axis] + 1) % result.shape[main_axis]] + spot[main_axis + 1:]
    return result.at[tuple(spot)].set(low).at[tuple(neighbour)].set(largest)


def routed_block(own_key, own, number, rows, amount, top, bound, skew):
    sequence = jax.random.permutation(own_key, amount)
    packed, ordinary = shares(amount, rows * top, bound, skew, True), shares(amount, rows * top, bound, skew, False)
    places = jnp.arange(amount)

    def named(lengths, rotation):
        used = int((lengths > 0).sum())
        fixed = max(1, used // 4)
        moved = fixed + (places - fixed + rotation * (used - fixed)) % max(1, amount - fixed)
        return jnp.zeros((amount,), jnp.int32).at[sequence[jnp.where(places < fixed, places, moved)]].set(jnp.asarray(lengths, jnp.int32))

    lengths = jnp.where(number % 4 == 0, named(packed, number // 4), named(ordinary, number - number // 4 - 1))
    mixed = jax.random.permutation(jax.random.fold_in(own, 3), amount)
    donor, taker = mixed[0:amount // 2 * 2:2], mixed[1:amount // 2 * 2:2]
    slack = jnp.minimum(lengths[donor] - 1, bound - lengths[taker]) // 2
    slack = jnp.where((donor == sequence[0]) | (taker == sequence[0]) | (lengths[taker] == 0), 0, jnp.maximum(slack, 0))
    moved = jax.random.randint(jax.random.fold_in(own, 4), (amount // 2,), 0, 1 << 20) % (slack + 1)
    lengths = lengths.at[donor].add(-moved).at[taker].add(moved)
    items = jnp.searchsorted(jnp.cumsum(lengths), jnp.arange(rows * top), side="right").astype(jnp.int32)
    listing = items.reshape(top, rows).T
    listing = listing[jax.random.permutation(jax.random.fold_in(own, 1), rows)]
    rotation = jax.random.randint(jax.random.fold_in(own, 2), (rows, 1), 0, top)
    return jnp.take_along_axis(listing, (jnp.arange(top)[None, :] + rotation) % top, axis=1)


def shares(count, total, most, slope, full):
    weights = [(1 << 20) // math.isqrt(rank ** slope) + 1 for rank in range(1, count + 1)]
    largest = most if full else min(most, max(-(-total // count), total * weights[0] // sum(weights)))
    least = 1 if total - largest >= count - 1 else 0
    counts, rest = [largest] + [least] * (count - 1), total - largest - least * (count - 1)
    while rest > 0:
        candidates = [i for i in range(1, count) if counts[i] < largest] or [i for i in range(1, count) if counts[i] < most]
        whole, remaining = sum([weights[i] for i in candidates]), rest
        for i in candidates:
            addition = min(most - counts[i], max(1, remaining * weights[i] // whole), rest)
            counts[i] = counts[i] + addition
            rest = rest - addition
    return np.array(counts)


def setup_inputs(seed: int = 0) -> dict:
    splits = jax.random.split(jax.random.key(seed), 7)
    waveforms = draw_waveforms(jax.random.fold_in(splits[6], 71), 0)
    templates = draw_templates(jax.random.fold_in(splits[6], 71), 0)
    tpl_stations_keys = jax.random.split(jax.random.fold_in(splits[2], 1), TEMPLATES // TPL_DEV)
    tpl_stations_turns = jax.random.permutation(jax.random.fold_in(splits[2], 3), TEMPLATES // TPL_DEV)
    tpl_stations = jax.vmap(lambda own, number: routed_block(jax.random.fold_in(splits[2], 2), own, number, TPL_DEV, STATIONS, K, CAP, 2))(tpl_stations_keys, tpl_stations_turns).reshape((TEMPLATES, K))
    det_station = place_ends(jax.random.randint(splits[3], (DETECTIONS,), 0, STA_DEV), jax.random.fold_in(splits[3], 1), 0, STA_DEV - 1).astype(jnp.int32)
    det_time = place_ends(jax.random.randint(splits[4], (DETECTIONS,), DTLAG // 2, SAMPLES - W - DTLAG // 2 + 1), jax.random.fold_in(splits[4], 1), DTLAG // 2, (SAMPLES - W - DTLAG // 2 + 1) - 1).astype(jnp.int32)
    partner = place_ends(jax.random.randint(splits[5], (DETECTIONS, 4), 0, DET_DEV), jax.random.fold_in(splits[5], 1), 0, DET_DEV - 1).astype(jnp.int32)
    return {"waveforms": waveforms, "templates": templates, "tpl_stations": tpl_stations, "det_station": det_station, "det_time": det_time, "partner": partner}


def correlate_block(block, data_freq, win_mean, nfft):
    tiles, ids = block
    tiles_f = tiles.astype(jnp.float32).reshape(tiles.shape[0], K, 3, TLEN)
    tile_mean = lax.optimization_barrier(jnp.mean(tiles_f * tiles_f, axis=(2, 3)))
    tile_freq = jnp.fft.rfft(tiles_f, n=nfft, axis=-1)
    product = lax.optimization_barrier(jnp.sum(data_freq[ids] * jnp.conj(tile_freq), axis=2))
    lagged = jnp.fft.irfft(product, n=nfft, axis=-1)[:, :, :NLAG]
    scaled = lagged / jnp.sqrt(3 * TLEN * (tile_mean[:, :, None] + 1e-06) * (win_mean[ids] + 1e-06))
    return lax.optimization_barrier(jnp.sum(scaled, axis=1)) / jnp.sqrt(jnp.float32(K))

def reference(waveforms, templates, tpl_stations, det_station, det_time, partner):
    data = waveforms.astype(jnp.float32)
    nfft = 1 << (SAMPLES - 1).bit_length()
    data_freq = jnp.fft.rfft(data, n=nfft, axis=-1)
    energy = lax.optimization_barrier(jnp.sum(data * data, axis=1))
    zero = jnp.zeros((), energy.dtype)
    window_sum = lax.reduce_window(energy, zero, lax.add, (1, TLEN), (1, 1), 'VALID')
    win_mean = window_sum[:, :NLAG] / (3 * TLEN)
    groups = N_GX * N_GY
    blocks = (templates.reshape(groups, TPL_DEV, K, 3 * TLEN), tpl_stations.reshape(groups, TPL_DEV, K))
    stack = lax.map(lambda blk: correlate_block(blk, data_freq, win_mean, nfft), blocks)
    stack = stack.reshape(TEMPLATES, NLAG)
    index = jnp.arange(DETECTIONS, dtype=jnp.int32)
    group = index // DET_DEV
    column = group // N_GY
    row = group % N_GY
    station = group * STA_DEV + det_station
    half = DTLAG // 2

    def cut(sta, start, size):
        return lax.dynamic_slice(data, (sta, jnp.int32(0), start), (1, 3, size))[0]
    local = jax.vmap(lambda s, t: cut(s, t, W))(station, det_time)
    wide = jax.vmap(lambda s, t: cut(s, t - half, W + DTLAG))(station, det_time - 0)
    wsize = W + DTLAG
    nwin = 1 << (wsize - 1).bit_length()
    local_freq = jnp.fft.rfft(local, n=nwin, axis=-1)
    local_mean = lax.optimization_barrier(jnp.mean(local * local, axis=(1, 2)))
    moves = ((1, 0), (-1, 0), (0, 1), (0, -1))
    outs = []
    for direction in range(4):
        nx = column + moves[direction][0]
        ny = row + moves[direction][1]
        valid = (nx >= 0) & (nx < N_GX) & (ny >= 0) & (ny < N_GY)
        other = jnp.clip(nx, 0, N_GX - 1) * N_GY + jnp.clip(ny, 0, N_GY - 1)
        target = other * DET_DEV + partner[:, direction]
        piece = wide[target] * valid.astype(jnp.float32)[:, None, None]
        piece_freq = jnp.fft.rfft(piece, n=nwin, axis=-1)
        lagged = jnp.fft.irfft(lax.optimization_barrier(jnp.sum(piece_freq * jnp.conj(local_freq), axis=1)), n=nwin, axis=-1)[:, :DTLAG]
        centre = piece[:, :, half:half + W]
        piece_mean = lax.optimization_barrier(jnp.mean(centre * centre, axis=(1, 2)))
        outs.append(lagged / jnp.sqrt(3 * W * (local_mean[:, None] + 1e-06) * (piece_mean[:, None] + 1e-06)))
    diffcc = jnp.stack(outs, axis=1)
    return (stack, diffcc)
```

```python
import functools

import jax
import jax.numpy as jnp
from jax import lax
from jax.experimental import pallas as pl
from jax.experimental.pallas import tpu as pltpu
from jax.sharding import PartitionSpec as P

LANES = 128
FINE = 8
COARSE = LANES // FINE
CHANNELS = 3
TAPS = 4
BLOCKS = 12
SLOTS = 16
W = 256
DTLAG = 128
HALF = DTLAG // 2
ROWS = CHANNELS * BLOCKS * 2
PACKED = ROWS + 8
EPS = 1e-06
F32 = jnp.float32
BF16 = jnp.bfloat16
NT = (((1,), (1,)), ((), ()))


def iota(shape, axis):
    return lax.broadcasted_iota(jnp.int32, shape, axis)


def rot(value, shift):
    shift = shift % LANES
    return pltpu.roll(value, shift, 1) if shift else value


def dot(a, b):
    return jnp.dot(a, b, preferred_element_type=F32)


def dot_nt(a, b):
    return lax.dot_general(a, b, NT, preferred_element_type=F32)


def pieces(value, count):
    out = []
    for _ in range(count - 1):
        high = value.astype(BF16)
        out.append(high)
        value = value - high.astype(F32)
    out.append(value.astype(BF16))
    return out


def lanes_before(lane, bound, first, second):
    if bound <= 0:
        return second
    if bound >= LANES:
        return first
    return jnp.where(lane < bound, first, second)


def column(row):
    n = row.shape[1]
    diagonal = iota((n, n), 0) == iota((n, n), 1)
    return jnp.sum(jnp.where(diagonal, row, 0), axis=1, keepdims=True)


def pack_kernel(wave_ref, time_ref, station_ref, out_ref, rows_ref):
    start = time_ref[...] - HALF
    row = 2 * (start // LANES) + station_ref[...]
    shift = start % LANES
    pad = jnp.zeros((1, LANES - row.shape[1]), F32)
    for c in range(CHANNELS):
        series = wave_ref[c].astype(F32)
        for block in range(BLOCKS):
            at = (c * BLOCKS + block) * 2
            rows_ref[at : at + 2, :] = series[:, block * LANES : (block + 1) * LANES]
    rows_ref[ROWS : ROWS + 1, :] = jnp.concatenate([row.astype(F32), pad], axis=1)
    rows_ref[ROWS + 1 : ROWS + 2, :] = jnp.concatenate([shift.astype(F32), pad], axis=1)
    rows_ref[ROWS + 2 : PACKED, :] = jnp.zeros((PACKED - ROWS - 2, LANES), F32)
    out_ref[...] = jnp.broadcast_to(rows_ref[...].astype(BF16)[None], out_ref.shape)


def tile_kernel(tiles_ref, station_ref, sorted_ref, scale_ref, owner_ref):
    tpl_dev, k_slots, row_len = tiles_ref.shape
    count = tpl_dev * k_slots
    total = sorted_ref.shape[0]
    station = station_ref[...].astype(F32).astype(BF16)
    home = (iota((count, tpl_dev), 0) // k_slots == iota((count, tpl_dev), 1)).astype(F32).astype(BF16)
    by_row = dot_nt(home, station)
    by_col = dot_nt(station, home)
    own_col = iota((count, k_slots), 0) % k_slots == iota((count, k_slots), 1)
    own_row = iota((k_slots, count), 1) % k_slots == iota((k_slots, count), 0)
    st_col = jnp.sum(jnp.where(own_col, by_row, 0.0), axis=1, keepdims=True)
    st_row = jnp.sum(jnp.where(own_row, by_col, 0.0), axis=0, keepdims=True)
    earlier = iota((count, count), 0) < iota((count, count), 1)
    rank = jnp.sum(jnp.where((st_col == st_row) & earlier, 1.0, 0.0), axis=0, keepdims=True)
    slot = (st_row * (SLOTS // 2) + rank).astype(jnp.int32)
    tiles = tiles_ref[...].reshape(count, row_len)
    step = 128
    for first in range(0, total, step):
        place = (iota((step, count), 0) + first == slot).astype(F32).astype(BF16)
        moved = dot(place, tiles)
        sorted_ref[first : first + step, :] = moved.astype(BF16)
        mean = jnp.sum(moved * moved, axis=1, keepdims=True) / row_len
        scale = lax.rsqrt(row_len * (mean + EPS))
        scale_ref[first : first + step, :] = jnp.broadcast_to(scale, (step, LANES))
        owner_ref[first : first + step, :] = dot(place, home).astype(BF16)


def main_kernel(
    ngx,
    ngy,
    data_ref,
    sorted_ref,
    scale_ref,
    owner_ref,
    time_ref,
    station_ref,
    partner_ref,
    stack_ref,
    diff_ref,
    x0_ref,
    x1_ref,
    w0_ref,
    w1_ref,
    win_ref,
    high_ref,
    low_ref,
    cut_ref,
    dc_ref,
):
    groups = ngx * ngy
    wide = COARSE * SLOTS
    lane16 = iota((SLOTS, LANES), 1)
    x_refs, w_refs = (x0_ref, x1_ref), (w0_ref, w1_ref)
    tlen = TAPS * LANES
    row_len = CHANNELS * tlen

    tri = jnp.concatenate(
        [
            iota((LANES, LANES), 0) >= iota((LANES, LANES), 1),
            iota((LANES, LANES), 0) < iota((LANES, LANES), 1),
            iota((LANES, LANES), 0) >= 0,
        ],
        axis=1,
    )
    tri = jnp.where(tri, 1.0, 0.0).astype(BF16)
    span = 2 * BLOCKS

    def windows(q, carry):
        x = data_ref[pl.ds(q * 8, 8)].astype(F32)
        energy = sum(x[:, span * c : span * (c + 1)] * x[:, span * c : span * (c + 1)] for c in range(CHANNELS))
        sums = sum(dot(part, tri) for part in pieces(energy.reshape(8 * span, LANES), 3))
        sums = sums.reshape(8, span, CHANNELS * LANES)
        mean = sums[:, 0:SLOTS, 0:LANES]
        for j in range(1, TAPS):
            mean = mean + sums[:, 2 * j : 2 * j + SLOTS, 2 * LANES :]
        mean = (mean + sums[:, 2 * TAPS : 2 * TAPS + SLOTS, LANES : 2 * LANES]) / row_len
        win_ref[q] = lax.rsqrt(mean + EPS).reshape(8 * SLOTS, LANES).T
        return carry

    lax.fori_loop(0, groups // 8, windows, 0)

    def shifted_left(get, blocks, shift):
        turned = [rot(get(j), -shift) for j in range(blocks)]
        return [lanes_before(lane16, LANES - shift, turned[j], turned[j + 1]) for j in range(blocks - 1)]

    def build_data(source, blocks, ref):
        keep = blocks - 1
        for a in range(COARSE):
            rows = slice(a * SLOTS, (a + 1) * SLOTS)
            tail = None
            for c in range(CHANNELS):
                turned = [rot(source[c][j], -FINE * a) for j in range(blocks)]
                for j in range(keep):
                    block = lanes_before(lane16, LANES - FINE * a, turned[j], turned[j + 1])
                    at = (c * keep + j) * LANES
                    ref[rows, at : at + LANES] = block
                end = rot(source[c][keep], FINE * (c - a))
                tail = end if tail is None else jnp.where(lane16 < FINE * c, tail, end)
            at = CHANNELS * keep * LANES
            ref[rows, at : at + LANES] = tail

    def build_taps(source, blocks, ref):
        zero = jnp.zeros((SLOTS, LANES), BF16)
        for b in range(FINE):
            rows = slice(b * SLOTS, (b + 1) * SLOTS)
            tail = zero
            for c in range(CHANNELS):
                before = zero
                for j in range(blocks):
                    turned = rot(source[c][j], b)
                    at = (c * blocks + j) * LANES
                    ref[rows, at : at + LANES] = lanes_before(lane16, b, before, turned)
                    before = turned
                if b:
                    end = rot(source[c][blocks - 1], b + FINE * c)
                    inside = (lane16 >= FINE * c) & (lane16 < FINE * c + b)
                    tail = jnp.where(inside, end, tail)
            at = CHANNELS * blocks * LANES
            ref[rows, at : at + LANES] = tail

    def build(g, which):
        x = data_ref[g].astype(F32)
        source = [
            [x[span * c + 2 * j : span * c + 2 * j + SLOTS].astype(BF16) for j in range(TAPS + 1)]
            for c in range(CHANNELS)
        ]
        build_data(source, TAPS + 1, x_refs[which])
        at = pl.ds(pl.multiple_of(g * SLOTS, SLOTS), SLOTS)
        tiles = sorted_ref[at, :]
        taps = [
            [tiles[:, (TAPS * c + j) * LANES : (TAPS * c + j + 1) * LANES] for j in range(TAPS)]
            for c in range(CHANNELS)
        ]
        build_taps(taps, TAPS, w_refs[which])

    own = (iota((SLOTS, wide), 0) // (SLOTS // 2)) == (iota((SLOTS, wide), 1) % 2)

    def correlate(g, which):
        raw = dot_nt(w_refs[which][...], x_refs[which][...])
        at = pl.ds(pl.multiple_of(g * SLOTS, SLOTS), SLOTS)
        scale = scale_ref[at, :]
        scale = jnp.concatenate([scale, scale], axis=1)
        turn = g % 8
        lane8 = iota((FINE, LANES), 1)
        halves = []
        for half in range(2):
            total = jnp.zeros((FINE, LANES), F32)
            for a in range(COARSE // 2):
                part = win_ref[g // 8, pl.ds((half * 8 + a) * FINE, FINE), :]
                part = pltpu.roll(part, (a - turn + 8) % 8 * SLOTS, 1)
                total = jnp.where(lane8 // SLOTS == a, part, total)
            halves.append(total)
        window = jnp.concatenate(halves, axis=1)
        for b in range(FINE):
            factor = jnp.where(own, window[b : b + 1], 0.0)
            value = raw[b * SLOTS : (b + 1) * SLOTS] * scale * factor
            high, low = pieces(value, 2)
            high_ref[b, at, :] = high
            low_ref[b, at, :] = low

    build(0, 0)

    def pair(i, carry):
        g = 2 * i
        correlate(g, 0)
        build(g + 1, 1)
        correlate(g + 1, 1)
        build(jnp.minimum(g + 2, groups - 1), 0)
        return carry

    lax.fori_loop(0, groups // 2, pair, 0)

    det_dev = time_ref.shape[1]
    lane = iota((det_dev, LANES), 1)
    row_iota = iota((det_dev, PACKED), 1)

    def cut(data, row, shift, blocks):
        picks = [row_iota == row + (span * c + 2 * j) for c in range(CHANNELS) for j in range(blocks)]
        picks = jnp.concatenate([jnp.where(pick, 1.0, 0.0) for pick in picks], axis=0).astype(BF16)
        found = dot(picks, data)
        found = [
            [found[(c * blocks + j) * det_dev : (c * blocks + j + 1) * det_dev] for j in range(blocks)]
            for c in range(CHANNELS)
        ]
        for bit in range(7):
            size = 1 << bit
            moves = (shift // size) % 2 == 1
            for c in range(CHANNELS):
                turned = [rot(found[c][j], -size) for j in range(blocks)]
                turned.append(turned[-1])
                found[c] = [
                    jnp.where(moves, jnp.where(lane < LANES - size, turned[j], turned[j + 1]), found[c][j])
                    for j in range(blocks)
                ]
        return [found[c][: blocks - 1] for c in range(CHANNELS)]

    def mean_square(blocks):
        return sum(jnp.sum(block * block, axis=1, keepdims=True) for block in blocks) / (CHANNELS * W)

    gx, gy = lax.axis_index("gx"), lax.axis_index("gy")
    start = column(time_ref[...])
    mine = cut(data_ref[gx * ngy + gy], 2 * (start // LANES) + column(station_ref[...]), start % LANES, 3)
    mine_scale = lax.rsqrt(CHANNELS * W * (mean_square([block for own_c in mine for block in own_c]) + EPS))
    diagonal = iota((SLOTS, wide), 0) == iota((SLOTS, wide), 1) % SLOTS
    parts = det_dev // SLOTS
    keep = W // LANES
    k_det = CHANNELS * keep * LANES + LANES

    scales = []
    for d, (dx, dy) in enumerate(((1, 0), (-1, 0), (0, 1), (0, -1))):
        x, y = gx + dx, gy + dy
        valid = (x >= 0) & (x < ngx) & (y >= 0) & (y < ngy)
        other = jnp.clip(x, 0, ngx - 1) * ngy + jnp.clip(y, 0, ngy - 1)
        data = data_ref[other]
        chosen = jnp.where(lane == column(partner_ref[d : d + 1, :]), 1.0, 0.0).astype(BF16)
        info = dot_nt(chosen, data[PACKED - 16 : PACKED, :])
        row = info[:, 8:9].astype(jnp.int32)
        shift = info[:, 9:10].astype(jnp.int32)
        piece = cut(data, row, shift, 4)
        centre = []
        for c in range(CHANNELS):
            centre += [
                jnp.where(lane >= HALF, piece[c][0], 0.0),
                piece[c][1],
                jnp.where(lane < HALF, piece[c][2], 0.0),
            ]
        scale = mine_scale * lax.rsqrt(mean_square(centre) + EPS)
        scales.append(jnp.where(valid, scale, 0.0))
        for c in range(CHANNELS):
            for j in range(keep + 1):
                cut_ref[d, c * (keep + 1) + j] = piece[c][j].astype(BF16)

    for q in range(parts):
        rows = slice(q * SLOTS, (q + 1) * SLOTS)
        build_taps([[mine[c][j][rows].astype(BF16) for j in range(keep)] for c in range(CHANNELS)], keep, w0_ref)
        taps = w0_ref[:, 0:k_det]
        for d in range(4):
            source = [
                [cut_ref[d, c * (keep + 1) + j, rows, :] for j in range(keep + 1)] for c in range(CHANNELS)
            ]
            ref = x_refs[d % 2]
            build_data(source, keep + 1, ref)
            raw = dot_nt(taps, ref[:, 0:k_det])
            at = d * det_dev + q * SLOTS
            for b in range(FINE):
                value = jnp.where(diagonal, raw[b * SLOTS : (b + 1) * SLOTS], 0.0)
                for n, part in enumerate(pieces(value, 2)):
                    dc_ref[n, b, at : at + SLOTS, :] = part

    tpl_dev = stack_ref.shape[0]
    block_of = (iota((tpl_dev, wide), 1) % SLOTS) // 2
    totals = jnp.zeros((BLOCKS - TAPS, tpl_dev, LANES), F32).reshape((BLOCKS - TAPS) * tpl_dev, LANES)
    lags = jnp.zeros((4 * det_dev, LANES), F32)
    for b in range(FINE):
        spread = iota((wide, LANES), 1) == (iota((wide, LANES), 0) // SLOTS) * FINE + b
        spread = jnp.where(spread, 1.0, 0.0).astype(BF16)
        contract = (((0,), (0,)), ((), ()))
        total = lax.dot_general(owner_ref[...], high_ref[b], contract, preferred_element_type=F32)
        total = total + lax.dot_general(owner_ref[...], low_ref[b], contract, preferred_element_type=F32)
        for n, part in enumerate(pieces(total, 2)):
            part = part.astype(F32)
            by_block = [jnp.where(block_of == block, part, 0.0) for block in range(BLOCKS - TAPS)]
            totals = totals + dot(jnp.concatenate(by_block, axis=0).astype(BF16), spread)
            lags = lags + dot(dc_ref[n, b], spread)
    for block in range(BLOCKS - TAPS):
        stack_ref[:, block * LANES : (block + 1) * LANES] = totals[block * tpl_dev : (block + 1) * tpl_dev] * (
            1.0 / 8.0**0.5
        )
    for d in range(4):
        diff_ref[pl.ds(d, det_dev, stride=4), :] = lags[d * det_dev : (d + 1) * det_dev] * scales[d]


def on_device(ngx, ngy, waveforms, templates, tpl_stations, det_station, det_time, partner):
    sta_dev, channels, samples = waveforms.shape
    tpl_dev, k_slots, row_len = templates.shape
    det_dev = det_station.shape[0]
    groups = ngx * ngy
    total = groups * SLOTS
    time_row, station_row = det_time.reshape(1, det_dev), det_station.reshape(1, det_dev)
    packed = pl.pallas_call(
        pack_kernel,
        out_shape=jax.ShapeDtypeStruct((groups, PACKED, LANES), BF16),
        scratch_shapes=[pltpu.VMEM((PACKED, LANES), F32)],
        name="pack",
    )(waveforms.transpose(1, 0, 2), time_row, station_row)
    data = lax.all_to_all(packed, ("gx", "gy"), split_axis=0, concat_axis=0, tiled=True)
    tiles, scale, owner = pl.pallas_call(
        tile_kernel,
        out_shape=(
            jax.ShapeDtypeStruct((total, row_len), BF16),
            jax.ShapeDtypeStruct((total, LANES), F32),
            jax.ShapeDtypeStruct((total, tpl_dev), BF16),
        ),
        compiler_params=pltpu.CompilerParams(vmem_limit_bytes=48 << 20),
        name="tiles",
    )(templates, tpl_stations.T)
    depth = row_len + LANES
    wide = COARSE * SLOTS
    stack, diff = pl.pallas_call(
        functools.partial(main_kernel, ngx, ngy),
        out_shape=(
            jax.ShapeDtypeStruct((tpl_dev, samples - row_len // CHANNELS), F32),
            jax.ShapeDtypeStruct((4 * det_dev, DTLAG), F32),
        ),
        scratch_shapes=[
            pltpu.VMEM((wide, depth), BF16),
            pltpu.VMEM((wide, depth), BF16),
            pltpu.VMEM((FINE * SLOTS, depth), BF16),
            pltpu.VMEM((FINE * SLOTS, depth), BF16),
            pltpu.VMEM((groups // 8, LANES, LANES), F32),
            pltpu.VMEM((FINE, total, wide), BF16),
            pltpu.VMEM((FINE, total, wide), BF16),
            pltpu.VMEM((4, 9, det_dev, LANES), BF16),
            pltpu.VMEM((2, FINE, 4 * det_dev, wide), BF16),
        ],
        compiler_params=pltpu.CompilerParams(vmem_limit_bytes=(12 << 20) + groups * (5 << 17)),
        name="correlate",
    )(data, tiles, scale, owner, time_row, station_row, partner.T)
    return stack, diff.reshape(det_dev, 4, DTLAG)


def solution(mesh):
    return jax.shard_map(
        functools.partial(on_device, mesh.shape["gx"], mesh.shape["gy"]),
        mesh=mesh,
        in_specs=(
            P(("gx", "gy"), None, None),
            P(("gx", "gy"), None, None),
            P(("gx", "gy"), None),
            P(("gx", "gy")),
            P(("gx", "gy")),
            P(("gx", "gy"), None),
        ),
        out_specs=(P(("gx", "gy"), None), P(("gx", "gy"), None, None)),
        check_vma=False,
    )
```

```python
import functools

import jax
import jax.numpy as jnp
from jax import lax
from jax.experimental import pallas as pl
from jax.experimental.pallas import tpu as pltpu
from jax.sharding import PartitionSpec as P

LANES = 128
CHANNELS = 3
STATIONS = 2
BLOCKS = 12
TAPS = 4
LAG_BLOCKS = BLOCKS - TAPS
SLOTS = 8
FINE = 8
COARSE = LANES // FINE
DET_FINE = 16
DET_COARSE = LANES // DET_FINE
DET_ROWS = 16
W = 256
DTLAG = 128
HALF = DTLAG // 2
KEEP = W // LANES
DET_DEPTH = CHANNELS * KEEP * LANES + LANES
SPAN = STATIONS * BLOCKS
ROWS = CHANNELS * SPAN
PACKED = ROWS + 8
EPS = 1e-06
F32 = jnp.float32
BF16 = jnp.bfloat16
NT = (((1,), (1,)), ((), ()))


def iota(shape, axis):
    return lax.broadcasted_iota(jnp.int32, shape, axis)


def rot(value, shift, axis=1):
    shift = shift % value.shape[axis]
    return pltpu.roll(value, shift, axis) if shift else value


def dot(a, b):
    return jnp.dot(a, b, preferred_element_type=F32)


def dot_nt(a, b):
    return lax.dot_general(a, b, NT, preferred_element_type=F32)


def ones_where(mask):
    return jnp.where(mask, 1.0, 0.0).astype(BF16)


def pieces(value, count):
    out = []
    for _ in range(count - 1):
        high = value.astype(BF16)
        out.append(high)
        value = value - high.astype(F32)
    out.append(value.astype(BF16))
    return out


def column(row):
    n = row.shape[1]
    diagonal = iota((n, n), 0) == iota((n, n), 1)
    return jnp.sum(jnp.where(diagonal, row, 0), axis=1, keepdims=True)


def pack_kernel(wave_ref, time_ref, station_ref, out_ref, rows_ref):
    start = time_ref[...] - HALF
    row = BLOCKS * station_ref[...] + start // LANES
    shift = start % LANES
    pad = jnp.zeros((1, LANES - row.shape[1]), F32)
    for c in range(CHANNELS):
        series = wave_ref[c].astype(F32)
        for s in range(STATIONS):
            for block in range(BLOCKS):
                at = c * SPAN + s * BLOCKS + block
                rows_ref[at : at + 1, :] = series[s : s + 1, block * LANES : (block + 1) * LANES]
    rows_ref[ROWS : ROWS + 1, :] = jnp.concatenate([row.astype(F32), pad], axis=1)
    rows_ref[ROWS + 1 : ROWS + 2, :] = jnp.concatenate([shift.astype(F32), pad], axis=1)
    rows_ref[ROWS + 2 : PACKED, :] = jnp.zeros((PACKED - ROWS - 2, LANES), F32)
    out_ref[...] = jnp.broadcast_to(rows_ref[...].astype(BF16)[None], out_ref.shape)


def tile_kernel(ngx, ngy, tiles_ref, station_ref, sorted_ref, scale_ref, owner_ref):
    tpl_dev, k_slots, row_len = tiles_ref.shape
    count = tpl_dev * k_slots
    total = sorted_ref.shape[0]
    station = station_ref[...].astype(F32).astype(BF16)
    home = ones_where(iota((count, tpl_dev), 0) // k_slots == iota((count, tpl_dev), 1))
    home_t = ones_where(iota((tpl_dev, count), 1) // k_slots == iota((tpl_dev, count), 0))
    by_row = dot_nt(home, station)
    by_col = dot(station, home_t)
    own_col = iota((count, k_slots), 0) % k_slots == iota((count, k_slots), 1)
    own_row = iota((k_slots, count), 1) % k_slots == iota((k_slots, count), 0)
    st_col = jnp.sum(jnp.where(own_col, by_row, 0.0), axis=1, keepdims=True)
    st_row = jnp.sum(jnp.where(own_row, by_col, 0.0), axis=0, keepdims=True)
    earlier = iota((count, count), 0) < iota((count, count), 1)
    rank = jnp.sum(jnp.where((st_col == st_row) & earlier, 1.0, 0.0), axis=0, keepdims=True)
    st = st_row.astype(jnp.int32)
    group = st // STATIONS
    x, y = group // ngy, group % ngy
    away = (x + lax.axis_index("gx")) % 2
    place_of = away * (ngx * ngy // 2) + x // 2 * ngy + y
    slot = (place_of * STATIONS + st % STATIONS) * SLOTS + rank.astype(jnp.int32)
    tiles = tiles_ref[...].reshape(count, row_len)
    step = 128
    for first in range(0, total, step):
        place = ones_where(iota((step, count), 0) + first == slot)
        moved = dot(place, tiles)
        sorted_ref[first : first + step, :] = moved.astype(BF16)
        mean = jnp.sum(moved * moved, axis=1, keepdims=True) / row_len
        scale = lax.rsqrt(row_len * (mean + EPS))
        scale_ref[first : first + step, :] = jnp.broadcast_to(scale, (step, LANES))
        owner_ref[:, first : first + step] = dot_nt(home_t, place).astype(BF16)


def window_scales(data_ref, rows_ref, win_ref):
    groups = data_ref.shape[0]
    step = min(8, groups)
    column_of = iota((LANES, LANES), 1)
    sample = FINE * (COARSE - 1 - column_of % COARSE) + column_of // COARSE
    row = iota((LANES, LANES), 0)
    sums_of = ones_where(jnp.concatenate([row >= sample, row < sample, row >= 0], axis=1))
    major, chunk = iota((step, FINE, LANES), 1), iota((step, FINE, LANES), 2) // COARSE

    def body(q, carry):
        x = data_ref[pl.ds(q * step, step)].astype(F32)
        rows_ref[pl.ds(q * step, step)] = x
        energy = sum(x[:, SPAN * c : SPAN * (c + 1)] * x[:, SPAN * c : SPAN * (c + 1)] for c in range(CHANNELS))
        sums = sum(dot(part, sums_of) for part in pieces(energy.reshape(step * SPAN, LANES), 3))
        sums = sums.reshape(step, SPAN, 3 * LANES)
        for s in range(STATIONS):
            at = BLOCKS * s
            mean = sums[:, at : at + LAG_BLOCKS, 0:LANES]
            for j in range(1, TAPS):
                mean = mean + sums[:, at + j : at + j + LAG_BLOCKS, 2 * LANES :]
            mean = (mean + sums[:, at + TAPS : at + TAPS + LAG_BLOCKS, LANES : 2 * LANES]) / (
                CHANNELS * TAPS * LANES
            )
            value = lax.rsqrt(mean + EPS)
            for bit in range(3):
                size = 1 << bit
                up = (major // size) % 2
                other = (chunk // size) % 2
                later = rot(rot(value, -size, 1), size * COARSE, 2)
                earlier = rot(rot(value, size, 1), -size * COARSE, 2)
                value = jnp.where(up == other, value, jnp.where(up == 0, later, earlier))
            win_ref[pl.ds(q * step, step), s] = value
        return carry

    lax.fori_loop(0, groups // step, body, 0)


def build_data(rows_ref, g, s, out_ref):
    lane = iota((COARSE, LANES), 1)
    bound = FINE * (iota((COARSE, LANES), 0) + 1)
    for c in range(CHANNELS):
        now = None
        for block in range(BLOCKS):
            at = SPAN * c + BLOCKS * s + block
            row = jnp.broadcast_to(rows_ref[g, at : at + 1, :], (COARSE, LANES))
            later = pltpu.roll(row, FINE, 1, stride=FINE, stride_axis=0).astype(BF16)
            if block:
                out_ref[(block - 1) * COARSE : block * COARSE, c * LANES : (c + 1) * LANES] = jnp.where(
                    lane < bound, now, later
                )
            now = later
        out_ref[(BLOCKS - 1) * COARSE : BLOCKS * COARSE, c * LANES : (c + 1) * LANES] = now


def build_taps(blocks_of, fine, height, out_ref, first, step):
    lane = iota((height, LANES), 1)
    zero = jnp.zeros((height, LANES), BF16)
    for b in range(fine):
        rows = slice(first + step * b, first + step * b + height)
        tail = zero
        at = 0
        for c, blocks in enumerate(blocks_of):
            before = zero
            for block in blocks:
                moved = rot(block, b)
                out_ref[rows, at : at + LANES] = jnp.where(lane < b, before, moved) if b else moved
                before = moved
                at += LANES
            if b:
                end = rot(blocks[-1], b + fine * c)
                tail = jnp.where((lane >= fine * c) & (lane < fine * c + b), end, tail)
        out_ref[rows, at : at + LANES] = tail


def taps_kernel(sorted_ref, out_ref):
    height = FINE * STATIONS * SLOTS
    per_step = out_ref.shape[0] // height
    rows = STATIONS * SLOTS
    lane = iota((rows, LANES), 1)
    zero = jnp.zeros((rows, LANES), BF16)

    def body(i, carry):
        at = (pl.program_id(0) * per_step + i) * rows
        tiles = sorted_ref[pl.ds(pl.multiple_of(at, rows), rows), :]
        out = out_ref.at[pl.ds(pl.multiple_of(i * height, height), height), :]
        for c in range(CHANNELS):
            blocks = [tiles[:, (TAPS * c + j) * LANES : (TAPS * c + j + 1) * LANES] for j in range(TAPS)]
            for b in range(FINE):
                before = zero
                for j in range(TAPS + 1):
                    moved = rot(blocks[j], b) if j < TAPS else zero
                    lanes = slice((c * (TAPS + 1) + j) * LANES, (c * (TAPS + 1) + j + 1) * LANES)
                    out[b * rows : (b + 1) * rows, lanes] = jnp.where(lane < b, before, moved) if b else moved
                    before = moved
        return carry

    lax.fori_loop(0, per_step, body, 0)


def correlate_kernel(call, data_ref, taps_ref, scale_ref, *refs):
    if call:
        owner_ref, first_high_ref, first_low_ref, stack_ref, high_ref, low_ref = refs[:6]
        refs = refs[6:]
    else:
        high_ref, low_ref = refs[:2]
        refs = refs[2:]
    rows_ref, win_ref = refs[:2]
    x_refs = (refs[2:4], refs[4:6])
    groups = data_ref.shape[0]
    rows = STATIONS * SLOTS
    height = FINE * rows
    per_step = taps_ref.shape[0] // height
    step = pl.program_id(0)

    def build(g, which):
        for s in range(STATIONS):
            build_data(rows_ref, g, s, x_refs[which][s])

    @pl.when(step == 0)
    def _():
        window_scales(data_ref, rows_ref, win_ref)
        build(0, 0)

    def lags(i, which):
        g = step * per_step + i
        taps = taps_ref[pl.ds(pl.multiple_of(i * height, height), height), :]
        data = [
            jnp.concatenate(
                [
                    ref[j * COARSE : j * COARSE + LANES, c * LANES : (c + 1) * LANES]
                    for c in range(CHANNELS)
                    for j in range(TAPS + 1)
                ],
                axis=1,
            )
            for ref in x_refs[which]
        ]
        raw = dot_nt(taps, jnp.concatenate(data, axis=0))
        scale = scale_ref[pl.ds(pl.multiple_of((call * groups + g) * rows, rows), rows), :]
        at = pl.ds(pl.multiple_of(g * rows, rows), rows)
        for b in range(FINE):
            value, window = [], []
            for s in range(STATIONS):
                first = b * rows + s * SLOTS
                value.append(raw[first : first + SLOTS, s * LANES : (s + 1) * LANES])
                window.append(jnp.broadcast_to(win_ref[g, s, b : b + 1, :], (SLOTS, LANES)))
            value = jnp.concatenate(value, axis=0) * scale * jnp.concatenate(window, axis=0)
            high, low = pieces(value, 2)
            high_ref[at, b * LANES : (b + 1) * LANES] = high
            low_ref[at, b * LANES : (b + 1) * LANES] = low

    def body(i, carry):
        g = step * per_step + 2 * i
        lags(2 * i, 0)
        build(g + 1, 1)
        lags(2 * i + 1, 1)
        build(jnp.minimum(g + 2, groups - 1), 0)
        return carry

    lax.fori_loop(0, per_step // 2, body, 0)

    if call:

        @pl.when(step == pl.num_programs(0) - 1)
        def _():
            half = groups * rows
            total = 0.0
            for first, second in ((first_high_ref, high_ref), (first_low_ref, low_ref)):
                total = total + dot(owner_ref[:, 0:half], first[...]) + dot(owner_ref[:, half:], second[...])
            stack_lags(total, stack_ref)


def stack_lags(total, stack_ref):
    tpl_dev = stack_ref.shape[0]
    block_of = iota((tpl_dev, FINE * LANES), 1) % LANES // COARSE
    place = iota((FINE * LANES, LANES), 0)
    spread = iota((FINE * LANES, LANES), 1) == FINE * (COARSE - 1 - place % COARSE) + place // LANES
    spread = ones_where(spread)
    out = 0.0
    for part in pieces(total, 2):
        part = part.astype(F32)
        masked = [jnp.where(block_of == block, part, 0.0) for block in range(LAG_BLOCKS)]
        out = out + dot(jnp.concatenate(masked, axis=0).astype(BF16), spread)
    for block in range(LAG_BLOCKS):
        rows = out[block * tpl_dev : (block + 1) * tpl_dev]
        stack_ref[:, block * LANES : (block + 1) * LANES] = rows * (1.0 / 8.0**0.5)


def cut(data, row, shift, blocks):
    det_dev = row.shape[0]
    row_iota, lane = iota((det_dev, PACKED), 1), iota((det_dev, LANES), 1)
    picks = [row_iota == row + (SPAN * c + j) for c in range(CHANNELS) for j in range(blocks)]
    picks = jnp.concatenate([jnp.where(pick, 1.0, 0.0) for pick in picks], axis=0).astype(BF16)
    found = dot(picks, data).astype(BF16)
    found = [
        [found[(c * blocks + j) * det_dev : (c * blocks + j + 1) * det_dev] for j in range(blocks)]
        for c in range(CHANNELS)
    ]
    shift = jnp.broadcast_to(shift, (det_dev, LANES))
    for bit in range(7):
        size = 1 << bit
        moves = (shift // size) % 2 == 1
        inner = lane < LANES - size
        for c in range(CHANNELS):
            turned = [rot(found[c][j], -size) for j in range(blocks)]
            turned.append(turned[-1])
            found[c] = [
                jnp.where(moves, jnp.where(inner, turned[j], turned[j + 1]), found[c][j]) for j in range(blocks)
            ]
    return [found[c][: blocks - 1] for c in range(CHANNELS)]


def mean_square(blocks):
    total = 0.0
    for block, mask in blocks:
        block = block.astype(F32)
        square = block * block
        total = total + (square if mask is None else jnp.where(mask, square, 0.0))
    return jnp.sum(total, axis=1, keepdims=True) / (CHANNELS * W)


def own_windows(data, time_ref, station_ref):
    start = column(time_ref[...])
    row = column(station_ref[...]) * BLOCKS + start // LANES
    mine = cut(data, row, start % LANES, KEEP + 1)
    scale = lax.rsqrt(CHANNELS * W * (mean_square([(block, None) for blocks in mine for block in blocks]) + EPS))
    return mine, scale


def partner_windows(data, chosen_row):
    det_dev = chosen_row.shape[1]
    lane = iota((det_dev, LANES), 1)
    info = dot_nt(ones_where(lane == column(chosen_row)), data[PACKED - 16 : PACKED, :])
    pieces_of = cut(data, info[:, 8:9].astype(jnp.int32), info[:, 9:10].astype(jnp.int32), KEEP + 2)
    centre = []
    for first, middle, last in pieces_of:
        centre += [(first, lane >= HALF), (middle, None), (last, lane < HALF)]
    return pieces_of, lax.rsqrt(mean_square(centre) + EPS)


def differential(mine, windows, x_ref, w_ref, parts_ref):
    count = len(windows)
    det_dev = mine[0][0].shape[0]
    height = count * DET_ROWS
    lane = iota((DET_ROWS, LANES), 1)
    wide = DET_FINE * DET_ROWS
    diagonal = iota((height, wide), 0) % DET_ROWS == iota((height, wide), 1) % DET_ROWS
    for q in range(det_dev // DET_ROWS):
        rows = slice(q * DET_ROWS, (q + 1) * DET_ROWS)
        build_taps([[block[rows] for block in blocks] for blocks in mine], DET_FINE, DET_ROWS, w_ref, 0, DET_ROWS)
        for d in range(count):
            source = [[block[rows] for block in blocks] for blocks in windows[d]]
            for a in range(DET_COARSE):
                shift = DET_FINE * a
                out = slice((a * count + d) * DET_ROWS, (a * count + d + 1) * DET_ROWS)
                tail = None
                for c in range(CHANNELS):
                    moved = [rot(block, -shift) for block in source[c]]
                    for j in range(KEEP):
                        block = jnp.where(lane < LANES - shift, moved[j], moved[j + 1]) if a else moved[j]
                        at = (c * KEEP + j) * LANES
                        x_ref[out, at : at + LANES] = block
                    end = rot(source[c][KEEP], DET_FINE * c - shift)
                    tail = end if tail is None else jnp.where(lane < DET_FINE * c, tail, end)
                x_ref[out, DET_DEPTH - LANES : DET_DEPTH] = tail
        raw = dot_nt(x_ref[0 : DET_COARSE * height, :], w_ref[...])
        for a in range(DET_COARSE):
            value = jnp.where(diagonal, raw[a * height : (a + 1) * height], 0.0)
            for n, part in enumerate(pieces(value, 2)):
                parts_ref[n, a, q * height : (q + 1) * height, :] = part
    place = iota((wide, LANES), 0)
    out = 0.0
    total = det_dev * count
    for a in range(DET_COARSE):
        spread = ones_where(iota((wide, LANES), 1) == DET_FINE * a + place // DET_ROWS)
        for n in range(2):
            out = out + dot(parts_ref[n, a, 0:total, :], spread)
    return out


def detect_kernel(
    ngx, ngy, near_ref, far_ref, time_ref, station_ref, partner_ref, diff_ref, x_ref, w_ref, parts_ref
):
    gx, gy = lax.axis_index("gx"), lax.axis_index("gy")
    mine, mine_scale = own_windows(near_ref[gx // 2 * ngy + gy], time_ref, station_ref)
    windows, scales = [], []
    for d, (dx, dy) in enumerate(((1, 0), (-1, 0), (0, 1), (0, -1))):
        x, y = gx + dx, gy + dy
        valid = (x >= 0) & (x < ngx) & (y >= 0) & (y < ngy)
        other = jnp.clip(x, 0, ngx - 1) // 2 * ngy + jnp.clip(y, 0, ngy - 1)
        data = (far_ref if dx else near_ref)[other]
        found, scale = partner_windows(data, partner_ref[d : d + 1, :])
        windows.append(found)
        scales.append(jnp.where(valid, mine_scale * scale, 0.0))
    out = differential(mine, windows, x_ref, w_ref, parts_ref)
    for q in range(time_ref.shape[1] // DET_ROWS):
        for d in range(4):
            at = (q * 4 + d) * DET_ROWS
            rows = slice(q * DET_ROWS, (q + 1) * DET_ROWS)
            diff_ref[pl.ds(q * DET_ROWS * 4 + d, DET_ROWS, stride=4), :] = (
                out[at : at + DET_ROWS] * scales[d][rows]
            )


def on_device(ngx, ngy, waveforms, templates, tpl_stations, det_station, det_time, partner):
    tpl_dev, k_slots, row_len = templates.shape
    det_dev = det_station.shape[0]
    groups = ngx * ngy
    half = groups // 2
    rows = STATIONS * SLOTS
    total = groups * rows
    time_row, station_row = det_time.reshape(1, det_dev), det_station.reshape(1, det_dev)
    packed = pl.pallas_call(
        pack_kernel,
        out_shape=jax.ShapeDtypeStruct((half, PACKED, LANES), BF16),
        scratch_shapes=[pltpu.VMEM((PACKED, LANES), F32)],
        name="pack",
    )(waveforms.transpose(1, 0, 2), time_row, station_row)
    members = [[x * ngy + y for x in range(parity, ngx, 2) for y in range(ngy)] for parity in range(2)]
    near = lax.all_to_all(
        packed, ("gx", "gy"), split_axis=0, concat_axis=0, axis_index_groups=members, tiled=True
    )
    tiles, scale, owner = pl.pallas_call(
        functools.partial(tile_kernel, ngx, ngy),
        out_shape=(
            jax.ShapeDtypeStruct((total, row_len), BF16),
            jax.ShapeDtypeStruct((total, LANES), F32),
            jax.ShapeDtypeStruct((tpl_dev, total), BF16),
        ),
        compiler_params=pltpu.CompilerParams(vmem_limit_bytes=24 << 20),
        name="tiles",
    )(templates, tpl_stations.T)
    steps = groups // 4
    height = 4 * FINE * rows
    depth = CHANNELS * (TAPS + 1) * LANES
    taps = pl.pallas_call(
        taps_kernel,
        grid=(steps,),
        in_specs=[pl.BlockSpec((total, row_len), lambda i: (0, 0))],
        out_specs=pl.BlockSpec((height, depth), lambda i: (i, 0)),
        out_shape=pltpu.HBM((steps * height, depth), BF16),
        compiler_params=pltpu.CompilerParams(vmem_limit_bytes=(8 << 20) + total * row_len * 4),
        name="taps",
    )(tiles)
    taps = pltpu.with_memory_space_constraint(taps, pltpu.HBM)
    far = lax.ppermute(near, "gx", [(x, x ^ 1) for x in range(ngx)])

    def whole(*shape):
        return pl.BlockSpec(shape, lambda i: (0,) * len(shape))

    sums = (half * rows, FINE * LANES)
    scratch = [
        pltpu.VMEM((half, PACKED, LANES), F32),
        pltpu.VMEM((half, STATIONS, FINE, LANES), F32),
    ] + [pltpu.VMEM((BLOCKS * COARSE, CHANNELS * LANES), BF16)] * 4
    params = pltpu.CompilerParams(vmem_limit_bytes=(16 << 20) + groups * (1 << 17))

    def specs(call):
        return [
            whole(half, PACKED, LANES),
            pl.BlockSpec((height, depth), lambda i: (call * steps // 2 + i, 0)),
            whole(*scale.shape),
        ]

    high, low = pl.pallas_call(
        functools.partial(correlate_kernel, 0),
        grid=(steps // 2,),
        in_specs=specs(0),
        out_specs=(whole(*sums), whole(*sums)),
        out_shape=(jax.ShapeDtypeStruct(sums, BF16),) * 2,
        scratch_shapes=scratch,
        compiler_params=params,
        name="correlate_near",
    )(near, taps, scale)
    stack = pl.pallas_call(
        functools.partial(correlate_kernel, 1),
        grid=(steps // 2,),
        in_specs=specs(1) + [whole(*owner.shape), whole(*sums), whole(*sums)],
        out_specs=whole(tpl_dev, LAG_BLOCKS * LANES),
        out_shape=jax.ShapeDtypeStruct((tpl_dev, LAG_BLOCKS * LANES), F32),
        scratch_shapes=[pltpu.VMEM(sums, BF16)] * 2 + scratch,
        compiler_params=params,
        name="correlate_far",
    )(far, taps, scale, owner, high, low)
    diff = pl.pallas_call(
        functools.partial(detect_kernel, ngx, ngy),
        out_shape=jax.ShapeDtypeStruct((4 * det_dev, DTLAG), F32),
        scratch_shapes=[
            pltpu.VMEM((4 * DET_COARSE * DET_ROWS, DET_DEPTH), BF16),
            pltpu.VMEM((DET_FINE * DET_ROWS, DET_DEPTH), BF16),
            pltpu.VMEM((2, DET_COARSE, 4 * det_dev, DET_FINE * DET_ROWS), BF16),
        ],
        compiler_params=pltpu.CompilerParams(vmem_limit_bytes=(16 << 20) + groups * (1 << 15)),
        name="detect",
    )(near, far, time_row, station_row, partner.T)
    return stack, diff.reshape(det_dev, 4, DTLAG)


def solution(mesh):
    return jax.shard_map(
        functools.partial(on_device, mesh.shape["gx"], mesh.shape["gy"]),
        mesh=mesh,
        in_specs=(
            P(("gx", "gy"), None, None),
            P(("gx", "gy"), None, None),
            P(("gx", "gy"), None),
            P(("gx", "gy")),
            P(("gx", "gy")),
            P(("gx", "gy"), None),
        ),
        out_specs=(P(("gx", "gy"), None), P(("gx", "gy"), None, None)),
        check_vma=False,
    )
```

```python
import functools

import jax
import jax.numpy as jnp
from jax import lax
from jax.experimental import pallas as pl
from jax.experimental.pallas import tpu as pltpu
from jax.sharding import PartitionSpec as P

LANES = 128
CHANNELS = 3
STATIONS = 2
BLOCKS = 12
TAPS = 4
LAG_BLOCKS = BLOCKS - TAPS
SLOTS = 8
FINE = 8
COARSE = LANES // FINE
DET_FINE = 16
DET_COARSE = LANES // DET_FINE
DET_ROWS = 16
W = 256
DTLAG = 128
HALF = DTLAG // 2
KEEP = W // LANES
DET_DEPTH = CHANNELS * KEEP * LANES + LANES
SPAN = STATIONS * BLOCKS
ROWS = CHANNELS * SPAN
PACKED = ROWS + 8
MXU = 256
PASSES = (CHANNELS * (TAPS + 1) + 1) // 2
SENT = 128
EPS = 1e-06
F32 = jnp.float32
BF16 = jnp.bfloat16
NT = (((1,), (1,)), ((), ()))


def iota(shape, axis):
    return lax.broadcasted_iota(jnp.int32, shape, axis)


def rot(value, shift, axis=1):
    shift = shift % value.shape[axis]
    return pltpu.roll(value, shift, axis) if shift else value


def dot(a, b):
    return jnp.dot(a, b, preferred_element_type=F32)


def dot_nt(a, b):
    return lax.dot_general(a, b, NT, preferred_element_type=F32)


def ones_where(mask):
    return jnp.where(mask, 1.0, 0.0).astype(BF16)


def pieces(value, count):
    out = []
    for _ in range(count - 1):
        high = value.astype(BF16)
        out.append(high)
        value = value - high.astype(F32)
    out.append(value.astype(BF16))
    return out


def column(row):
    n = row.shape[1]
    diagonal = iota((n, n), 0) == iota((n, n), 1)
    return jnp.sum(jnp.where(diagonal, row, 0), axis=1, keepdims=True)


def pack_kernel(wave_ref, time_ref, station_ref, out_ref, rows_ref):
    start = time_ref[...] - HALF
    row = BLOCKS * station_ref[...] + start // LANES
    shift = start % LANES
    pad = jnp.zeros((1, LANES - row.shape[1]), F32)
    for c in range(CHANNELS):
        series = wave_ref[c].astype(F32)
        for s in range(STATIONS):
            for block in range(BLOCKS):
                at = c * SPAN + s * BLOCKS + block
                rows_ref[at : at + 1, :] = series[s : s + 1, block * LANES : (block + 1) * LANES]
    rows_ref[ROWS : ROWS + 1, :] = jnp.concatenate([row.astype(F32), pad], axis=1)
    rows_ref[ROWS + 1 : ROWS + 2, :] = jnp.concatenate([shift.astype(F32), pad], axis=1)
    rows_ref[ROWS + 2 : PACKED, :] = jnp.zeros((PACKED - ROWS - 2, LANES), F32)
    count = out_ref.shape[0]
    out_ref[:, 0:PACKED] = jnp.broadcast_to(rows_ref[...].astype(BF16)[None], (count, PACKED, LANES))
    out_ref[:, PACKED:] = jnp.zeros((count, SENT - PACKED, LANES), BF16)


def tile_kernel(ngx, ngy, tiles_ref, station_ref, sorted_ref, scale_ref, owner_ref):
    tpl_dev, k_slots, row_len = tiles_ref.shape
    count = tpl_dev * k_slots
    total = sorted_ref.shape[0]
    station = station_ref[...].astype(F32).astype(BF16)
    home = ones_where(iota((count, tpl_dev), 0) // k_slots == iota((count, tpl_dev), 1))
    home_t = ones_where(iota((tpl_dev, count), 1) // k_slots == iota((tpl_dev, count), 0))
    by_row = dot_nt(home, station)
    by_col = dot(station, home_t)
    own_col = iota((count, k_slots), 0) % k_slots == iota((count, k_slots), 1)
    own_row = iota((k_slots, count), 1) % k_slots == iota((k_slots, count), 0)
    st_col = jnp.sum(jnp.where(own_col, by_row, 0.0), axis=1, keepdims=True)
    st_row = jnp.sum(jnp.where(own_row, by_col, 0.0), axis=0, keepdims=True)
    earlier = iota((count, count), 0) < iota((count, count), 1)
    rank = jnp.sum(jnp.where((st_col == st_row) & earlier, 1.0, 0.0), axis=0, keepdims=True)
    st = st_row.astype(jnp.int32)
    group = st // STATIONS
    x, y = group // ngy, group % ngy
    away = (x + lax.axis_index("gx")) % 2
    place_of = away * (ngx * ngy // 2) + x // 2 * ngy + y
    slot = (place_of * STATIONS + st % STATIONS) * SLOTS + rank.astype(jnp.int32)
    tiles = tiles_ref[...].reshape(count, row_len)
    step = 128
    for first in range(0, total, step):
        place = ones_where(iota((step, count), 0) + first == slot)
        moved = dot(place, tiles)
        sorted_ref[first : first + step, :] = moved.astype(BF16)
        mean = jnp.sum(moved * moved, axis=1, keepdims=True) / row_len
        scale = lax.rsqrt(row_len * (mean + EPS))
        scale_ref[first : first + step, :] = jnp.broadcast_to(scale, (step, LANES))
        owner_ref[:, first : first + step] = dot_nt(home_t, place).astype(BF16)


def windows_kernel(data_ref, rows_ref, win_ref):
    groups = data_ref.shape[0]
    step = min(8, groups)
    column_of = iota((LANES, LANES), 1)
    sample = FINE * (COARSE - 1 - column_of % COARSE) + column_of // COARSE
    row = iota((LANES, LANES), 0)
    sums_of = ones_where(jnp.concatenate([row >= sample, row < sample, row >= 0], axis=1))
    major, chunk = iota((step, FINE, LANES), 1), iota((step, FINE, LANES), 2) // COARSE

    def body(q, carry):
        x = data_ref[pl.ds(q * step, step), 0:PACKED].astype(F32)
        rows_ref[pl.ds(q * step, step)] = x
        energy = sum(x[:, SPAN * c : SPAN * (c + 1)] * x[:, SPAN * c : SPAN * (c + 1)] for c in range(CHANNELS))
        sums = sum(dot(part, sums_of) for part in pieces(energy.reshape(step * SPAN, LANES), 3))
        sums = sums.reshape(step, SPAN, 3 * LANES)
        for s in range(STATIONS):
            at = BLOCKS * s
            mean = sums[:, at : at + LAG_BLOCKS, 0:LANES]
            for j in range(1, TAPS):
                mean = mean + sums[:, at + j : at + j + LAG_BLOCKS, 2 * LANES :]
            mean = (mean + sums[:, at + TAPS : at + TAPS + LAG_BLOCKS, LANES : 2 * LANES]) / (
                CHANNELS * TAPS * LANES
            )
            value = lax.rsqrt(mean + EPS)
            for bit in range(3):
                size = 1 << bit
                up = (major // size) % 2
                other = (chunk // size) % 2
                later = rot(rot(value, -size, 1), size * COARSE, 2)
                earlier = rot(rot(value, size, 1), -size * COARSE, 2)
                value = jnp.where(up == other, value, jnp.where(up == 0, later, earlier))
            win_ref[pl.ds(q * step, step), s] = value
        return carry

    lax.fori_loop(0, groups // step, body, 0)


def build_data(rows_ref, g, s, c, out_ref):
    lane = iota((COARSE, LANES), 1)
    bound = FINE * (iota((COARSE, LANES), 0) + 1)
    now = None
    for block in range(BLOCKS):
        at = SPAN * c + BLOCKS * s + block
        row = jnp.broadcast_to(rows_ref[g, at : at + 1, :], (COARSE, LANES))
        later = pltpu.roll(row, FINE, 1, stride=FINE, stride_axis=0).astype(BF16)
        if block:
            out_ref[(block - 1) * COARSE : block * COARSE, c * LANES : (c + 1) * LANES] = jnp.where(
                lane < bound, now, later
            )
        now = later
    out_ref[(BLOCKS - 1) * COARSE : BLOCKS * COARSE, c * LANES : (c + 1) * LANES] = now


def build_taps(blocks_of, fine, height, out_ref, first, step):
    lane = iota((height, LANES), 1)
    zero = jnp.zeros((height, LANES), BF16)
    for b in range(fine):
        rows = slice(first + step * b, first + step * b + height)
        tail = zero
        at = 0
        for c, blocks in enumerate(blocks_of):
            before = zero
            for block in blocks:
                moved = rot(block, b)
                out_ref[rows, at : at + LANES] = jnp.where(lane < b, before, moved) if b else moved
                before = moved
                at += LANES
            if b:
                end = rot(blocks[-1], b + fine * c)
                tail = jnp.where((lane >= fine * c) & (lane < fine * c + b), end, tail)
        out_ref[rows, at : at + LANES] = tail


def taps_kernel(sorted_ref, out_ref):
    height = FINE * STATIONS * SLOTS
    per_step = out_ref.shape[0] // height
    rows = STATIONS * SLOTS
    lane = iota((rows, LANES), 1)
    zero = jnp.zeros((rows, LANES), BF16)

    def body(i, carry):
        at = (pl.program_id(0) * per_step + i) * rows
        tiles = sorted_ref[pl.ds(pl.multiple_of(at, rows), rows), :]
        out = out_ref.at[pl.ds(pl.multiple_of(i * height, height), height), :]
        for c in range(CHANNELS):
            blocks = [tiles[:, (TAPS * c + j) * LANES : (TAPS * c + j + 1) * LANES] for j in range(TAPS)]
            for b in range(FINE):
                before = zero
                for j in range(TAPS + 1):
                    moved = rot(blocks[j], b) if j < TAPS else zero
                    lanes = slice((c * (TAPS + 1) + j) * LANES, (c * (TAPS + 1) + j + 1) * LANES)
                    out[b * rows : (b + 1) * rows, lanes] = jnp.where(lane < b, before, moved) if b else moved
                    before = moved
        out[:, CHANNELS * (TAPS + 1) * LANES :] = jnp.zeros((height, LANES), BF16)
        return carry

    lax.fori_loop(0, per_step, body, 0)


def correlate_kernel(call, rows_ref, win_ref, taps_ref, scale_ref, high_ref, low_ref, *refs):
    x_refs = [[refs[4 * bank + 2 * n : 4 * bank + 2 * n + 2] for n in range(2)] for bank in range(2)]
    groups = rows_ref.shape[0]
    rows = STATIONS * SLOTS
    height = FINE * rows
    step = pl.program_id(0)
    parts = [(c, j) for c in range(CHANNELS) for j in range(TAPS + 1)]
    parts = parts + parts[:1]

    def builds(first, bank):
        for n in range(2):
            for s in range(STATIONS):
                for c in range(CHANNELS):
                    yield lambda n=n, s=s, c=c: build_data(rows_ref, first + n, s, c, x_refs[bank][n][s])

    @pl.when(step == 0)
    def _():
        for write in builds(0, 0):
            write()

    def store_lags(i, raw):
        g = step * 4 + i
        scale = scale_ref[pl.ds(pl.multiple_of((call * groups + g) * rows, rows), rows), :]
        at = pl.ds(pl.multiple_of(g * rows, rows), rows)
        for b in range(FINE):
            value, window = [], []
            for s in range(STATIONS):
                first = b * rows + s * SLOTS
                value.append(raw[first : first + SLOTS, s * LANES : (s + 1) * LANES])
                window.append(jnp.broadcast_to(win_ref[g, s, b : b + 1, :], (SLOTS, LANES)))
            value = jnp.concatenate(value, axis=0) * scale * jnp.concatenate(window, axis=0)
            high, low = pieces(value, 2)
            high_ref[at, b * LANES : (b + 1) * LANES] = high
            low_ref[at, b * LANES : (b + 1) * LANES] = low

    def multiply(accs, bank, writes):
        for t in range(PASSES):
            for n in range(2):
                data = [
                    jnp.concatenate(
                        [ref[j * COARSE : j * COARSE + LANES, c * LANES : (c + 1) * LANES] for c, j in parts[2 * t : 2 * t + 2]],
                        axis=1,
                    )
                    for ref in x_refs[bank][n]
                ]
                pltpu.matmul_push_rhs(jnp.concatenate(data, axis=0), t % 2, n, transpose=True)
                first = (2 * bank + n) * height
                taps = taps_ref[first : first + height, t * MXU : (t + 1) * MXU]
                pltpu.matmul_acc_lhs(accs[n], taps, load_staged_rhs=t % 2)
            for write in writes[t::PASSES]:
                write()

    def four_groups(*accs):
        multiply(accs[:2], 0, list(builds(step * 4 + 2, 1)))
        finish = [lambda n=n: store_lags(n, pltpu.matmul_pop(accs[n])) for n in range(2)]
        multiply(accs[2:], 1, list(builds(jnp.minimum(step * 4 + 4, groups - 2), 0)) + finish)
        for n in range(2):
            store_lags(2 + n, pltpu.matmul_pop(accs[2 + n]))

    pl.run_scoped(four_groups, *[pltpu.ACC(n % 2)((height, MXU), F32) for n in range(4)])


def stack_kernel(owner_ref, near_high_ref, near_low_ref, far_high_ref, far_low_ref, stack_ref):
    half = near_high_ref.shape[0]
    total = 0.0
    for near, far in ((near_high_ref, far_high_ref), (near_low_ref, far_low_ref)):
        total = total + dot(owner_ref[:, 0:half], near[...]) + dot(owner_ref[:, half:], far[...])
    tpl_dev = stack_ref.shape[0]
    block_of = iota((tpl_dev, FINE * LANES), 1) % LANES // COARSE
    place = iota((FINE * LANES, LANES), 0)
    spread = iota((FINE * LANES, LANES), 1) == FINE * (COARSE - 1 - place % COARSE) + place // LANES
    spread = ones_where(spread)
    out = 0.0
    for part in pieces(total, 2):
        part = part.astype(F32)
        masked = [jnp.where(block_of == block, part, 0.0) for block in range(LAG_BLOCKS)]
        out = out + dot(jnp.concatenate(masked, axis=0).astype(BF16), spread)
    for block in range(LAG_BLOCKS):
        rows = out[block * tpl_dev : (block + 1) * tpl_dev]
        stack_ref[:, block * LANES : (block + 1) * LANES] = rows * (1.0 / 8.0**0.5)


def cut(data, row, shift, blocks):
    det_dev = row.shape[0]
    row_iota, lane = iota((det_dev, PACKED), 1), iota((det_dev, LANES), 1)
    picks = [row_iota == row + (SPAN * c + j) for c in range(CHANNELS) for j in range(blocks)]
    picks = jnp.concatenate([jnp.where(pick, 1.0, 0.0) for pick in picks], axis=0).astype(BF16)
    found = dot(picks, data).astype(BF16)
    found = [
        [found[(c * blocks + j) * det_dev : (c * blocks + j + 1) * det_dev] for j in range(blocks)]
        for c in range(CHANNELS)
    ]
    shift = jnp.broadcast_to(shift, (det_dev, LANES))
    for bit in range(7):
        size = 1 << bit
        moves = (shift // size) % 2 == 1
        inner = lane < LANES - size
        for c in range(CHANNELS):
            turned = [rot(found[c][j], -size) for j in range(blocks)]
            turned.append(turned[-1])
            found[c] = [
                jnp.where(moves, jnp.where(inner, turned[j], turned[j + 1]), found[c][j]) for j in range(blocks)
            ]
    return [found[c][: blocks - 1] for c in range(CHANNELS)]


def mean_square(blocks):
    total = 0.0
    for block, mask in blocks:
        block = block.astype(F32)
        square = block * block
        total = total + (square if mask is None else jnp.where(mask, square, 0.0))
    return jnp.sum(total, axis=1, keepdims=True) / (CHANNELS * W)


def own_windows(data, time_ref, station_ref):
    start = column(time_ref[...])
    row = column(station_ref[...]) * BLOCKS + start // LANES
    mine = cut(data, row, start % LANES, KEEP + 1)
    scale = lax.rsqrt(CHANNELS * W * (mean_square([(block, None) for blocks in mine for block in blocks]) + EPS))
    return mine, scale


def partner_windows(data, chosen_row):
    det_dev = chosen_row.shape[1]
    lane = iota((det_dev, LANES), 1)
    info = dot_nt(ones_where(lane == column(chosen_row)), data[PACKED - 16 : PACKED, :])
    pieces_of = cut(data, info[:, 8:9].astype(jnp.int32), info[:, 9:10].astype(jnp.int32), KEEP + 2)
    centre = []
    for first, middle, last in pieces_of:
        centre += [(first, lane >= HALF), (middle, None), (last, lane < HALF)]
    return pieces_of, lax.rsqrt(mean_square(centre) + EPS)


def turn_over(block):
    n = block.shape[0]
    return dot(ones_where(iota((n, n), 0) + iota((n, n), 1) == n - 1), block).astype(BF16)


def differential(mine, windows, x_ref, w_ref, parts_ref):
    count = len(windows)
    det_dev = mine[0][0].shape[0]
    height = count * DET_ROWS
    lane = iota((DET_ROWS, LANES), 1)
    wide = DET_FINE * DET_ROWS
    sub_lane = iota((8, LANES), 1) % DET_ROWS
    for q in range(det_dev // DET_ROWS):
        rows = slice(q * DET_ROWS, (q + 1) * DET_ROWS)
        build_taps([[turn_over(block[rows]) for block in blocks] for blocks in mine], DET_FINE, DET_ROWS, w_ref, 0, DET_ROWS)
        for d in range(count):
            source = [[block[rows] for block in blocks] for blocks in windows[d]]
            for a in range(DET_COARSE):
                shift = DET_FINE * a
                out = slice((a * count + d) * DET_ROWS, (a * count + d + 1) * DET_ROWS)
                tail = None
                for c in range(CHANNELS):
                    moved = [rot(block, -shift) for block in source[c]]
                    for j in range(KEEP):
                        block = jnp.where(lane < LANES - shift, moved[j], moved[j + 1]) if a else moved[j]
                        at = (c * KEEP + j) * LANES
                        x_ref[out, at : at + LANES] = block
                    end = rot(source[c][KEEP], DET_FINE * c - shift)
                    tail = end if tail is None else jnp.where(lane < DET_FINE * c, tail, end)
                x_ref[out, DET_DEPTH - LANES : DET_DEPTH] = tail
        raw = dot_nt(x_ref[0 : DET_COARSE * height, :], w_ref[...])
        for half in range(2):
            for row in range(0, height, 8):
                upper = row % DET_ROWS // 8
                total = jnp.zeros((8, LANES), F32)
                for a in range(DET_COARSE):
                    part = raw[a * height + row : a * height + row + 8, half * LANES : (half + 1) * LANES]
                    base = a + 1 if upper else a + LANES - DET_ROWS + 1
                    part = pltpu.roll(part, base, 1, stride=1, stride_axis=0)
                    total = jnp.where(sub_lane == 8 * upper + a, part, total)
                parts_ref[q * height + row : q * height + row + 8, half * LANES : (half + 1) * LANES] = total
    place, to = iota((wide, LANES), 0), iota((wide, LANES), 1)
    order = ones_where((to // DET_FINE == place % DET_COARSE) & (to % DET_FINE == place // DET_ROWS))
    return sum(dot(part, order) for part in pieces(parts_ref[...], 2))


def detect_kernel(
    ngx, ngy, near_ref, far_ref, time_ref, station_ref, partner_ref, diff_ref, x_ref, w_ref, parts_ref
):
    gx, gy = lax.axis_index("gx"), lax.axis_index("gy")
    mine, mine_scale = own_windows(near_ref[gx // 2 * ngy + gy, 0:PACKED], time_ref, station_ref)
    windows, scales = [], []
    for d, (dx, dy) in enumerate(((1, 0), (-1, 0), (0, 1), (0, -1))):
        x, y = gx + dx, gy + dy
        valid = (x >= 0) & (x < ngx) & (y >= 0) & (y < ngy)
        other = jnp.clip(x, 0, ngx - 1) // 2 * ngy + jnp.clip(y, 0, ngy - 1)
        data = (far_ref if dx else near_ref)[other, 0:PACKED]
        found, scale = partner_windows(data, partner_ref[d : d + 1, :])
        windows.append(found)
        scales.append(jnp.where(valid, mine_scale * scale, 0.0))
    out = differential(mine, windows, x_ref, w_ref, parts_ref)
    for q in range(time_ref.shape[1] // DET_ROWS):
        for d in range(4):
            at = (q * 4 + d) * DET_ROWS
            rows = slice(q * DET_ROWS, (q + 1) * DET_ROWS)
            diff_ref[pl.ds(q * DET_ROWS * 4 + d, DET_ROWS, stride=4), :] = (
                out[at : at + DET_ROWS] * scales[d][rows]
            )


def on_device(ngx, ngy, waveforms, templates, tpl_stations, det_station, det_time, partner):
    tpl_dev, k_slots, row_len = templates.shape
    det_dev = det_station.shape[0]
    groups = ngx * ngy
    half = groups // 2
    rows = STATIONS * SLOTS
    total = groups * rows
    time_row, station_row = det_time.reshape(1, det_dev), det_station.reshape(1, det_dev)
    packed = pl.pallas_call(
        pack_kernel,
        out_shape=jax.ShapeDtypeStruct((half, SENT, LANES), BF16),
        scratch_shapes=[pltpu.VMEM((PACKED, LANES), F32)],
        name="pack",
    )(waveforms.transpose(1, 0, 2), time_row, station_row)
    members = [[x * ngy + y for x in range(parity, ngx, 2) for y in range(ngy)] for parity in range(2)]
    near = lax.all_to_all(
        packed, ("gx", "gy"), split_axis=0, concat_axis=0, axis_index_groups=members, tiled=True
    )
    tiles, scale, owner = pl.pallas_call(
        functools.partial(tile_kernel, ngx, ngy),
        out_shape=(
            jax.ShapeDtypeStruct((total, row_len), BF16),
            jax.ShapeDtypeStruct((total, LANES), F32),
            jax.ShapeDtypeStruct((tpl_dev, total), BF16),
        ),
        compiler_params=pltpu.CompilerParams(vmem_limit_bytes=24 << 20),
        name="tiles",
    )(templates, tpl_stations.T)
    steps = groups // 4
    height = 4 * FINE * rows
    depth = MXU * PASSES
    taps = pl.pallas_call(
        taps_kernel,
        grid=(steps,),
        in_specs=[pl.BlockSpec((total, row_len), lambda i: (0, 0))],
        out_specs=pl.BlockSpec((height, depth), lambda i: (i, 0)),
        out_shape=pltpu.HBM((steps * height, depth), BF16),
        compiler_params=pltpu.CompilerParams(vmem_limit_bytes=(8 << 20) + total * row_len * 4),
        name="taps",
    )(tiles)
    taps = pltpu.with_memory_space_constraint(taps, pltpu.HBM)
    far = lax.ppermute(near, "gx", [(x, x ^ 1) for x in range(ngx)])

    def whole(*shape):
        return pl.BlockSpec(shape, lambda i: (0,) * len(shape))

    sums = (half * rows, FINE * LANES)
    params = pltpu.CompilerParams(vmem_limit_bytes=(16 << 20) + groups * (1 << 17))

    def correlate(call, data):
        series, win = pl.pallas_call(
            windows_kernel,
            out_shape=(
                jax.ShapeDtypeStruct((half, PACKED, LANES), F32),
                jax.ShapeDtypeStruct((half, STATIONS, FINE, LANES), F32),
            ),
            compiler_params=params,
            name="windows",
        )(data)
        return pl.pallas_call(
            functools.partial(correlate_kernel, call),
            grid=(steps // 2,),
            in_specs=[
                whole(*series.shape),
                whole(*win.shape),
                pl.BlockSpec((height, depth), lambda i: (call * steps // 2 + i, 0)),
                whole(*scale.shape),
            ],
            out_specs=(whole(*sums), whole(*sums)),
            out_shape=(jax.ShapeDtypeStruct(sums, BF16),) * 2,
            scratch_shapes=[pltpu.VMEM((BLOCKS * COARSE, CHANNELS * LANES), BF16)] * 8,
            compiler_params=params,
            name="correlate",
        )(series, win, taps, scale)

    near_sums, far_sums = correlate(0, near), correlate(1, far)
    stack = pl.pallas_call(
        stack_kernel,
        out_shape=jax.ShapeDtypeStruct((tpl_dev, LAG_BLOCKS * LANES), F32),
        compiler_params=params,
        name="stack",
    )(owner, *near_sums, *far_sums)
    diff = pl.pallas_call(
        functools.partial(detect_kernel, ngx, ngy),
        out_shape=jax.ShapeDtypeStruct((4 * det_dev, DTLAG), F32),
        scratch_shapes=[
            pltpu.VMEM((4 * DET_COARSE * DET_ROWS, DET_DEPTH), BF16),
            pltpu.VMEM((DET_FINE * DET_ROWS, DET_DEPTH), BF16),
            pltpu.VMEM((4 * det_dev, DET_FINE * DET_ROWS), F32),
        ],
        compiler_params=pltpu.CompilerParams(vmem_limit_bytes=(16 << 20) + groups * (1 << 15)),
        name="detect",
    )(near, far, time_row, station_row, partner.T)
    return stack, diff.reshape(det_dev, 4, DTLAG)


def solution(mesh):
    return jax.shard_map(
        functools.partial(on_device, mesh.shape["gx"], mesh.shape["gy"]),
        mesh=mesh,
        in_specs=(
            P(("gx", "gy"), None, None),
            P(("gx", "gy"), None, None),
            P(("gx", "gy"), None),
            P(("gx", "gy")),
            P(("gx", "gy")),
            P(("gx", "gy"), None),
        ),
        out_specs=(P(("gx", "gy"), None), P(("gx", "gy"), None, None)),
        check_vma=False,
    )
```

```python
import functools

import jax
import jax.numpy as jnp
from jax import lax
from jax.experimental import pallas as pl
from jax.experimental.pallas import tpu as pltpu
from jax.sharding import PartitionSpec as P

LANES = 128
CHANNELS = 3
STATIONS = 2
BLOCKS = 12
TAPS = 4
LAG_BLOCKS = BLOCKS - TAPS
SLOTS = 8
FINE = 8
COARSE = LANES // FINE
DET_FINE = 16
DET_COARSE = LANES // DET_FINE
DET_ROWS = 16
W = 256
DTLAG = 128
HALF = DTLAG // 2
KEEP = W // LANES
DET_DEPTH = CHANNELS * KEEP * LANES + LANES
SPAN = STATIONS * BLOCKS
ROWS = CHANNELS * SPAN
PACKED = ROWS + 8
MXU = 256
RUNS = BLOCKS - 1
DEPTH = CHANNELS * LANES + LANES
EPS = 1e-06
F32 = jnp.float32
BF16 = jnp.bfloat16
NT = (((1,), (1,)), ((), ()))


def iota(shape, axis):
    return lax.broadcasted_iota(jnp.int32, shape, axis)


def rot(value, shift, axis=1):
    shift = shift % value.shape[axis]
    return pltpu.roll(value, shift, axis) if shift else value


def dot(a, b):
    return jnp.dot(a, b, preferred_element_type=F32)


def dot_nt(a, b):
    return lax.dot_general(a, b, NT, preferred_element_type=F32)


def ones_where(mask):
    return jnp.where(mask, 1.0, 0.0).astype(BF16)


def pieces(value, count):
    out = []
    for _ in range(count - 1):
        high = value.astype(BF16)
        out.append(high)
        value = value - high.astype(F32)
    out.append(value.astype(BF16))
    return out


def column(row):
    n = row.shape[1]
    diagonal = iota((n, n), 0) == iota((n, n), 1)
    return jnp.sum(jnp.where(diagonal, row, 0), axis=1, keepdims=True)


def pack_kernel(wave_ref, time_ref, station_ref, out_ref, rows_ref):
    start = time_ref[...] - HALF
    row = BLOCKS * station_ref[...] + start // LANES
    shift = start % LANES
    pad = jnp.zeros((1, LANES - row.shape[1]), F32)
    for c in range(CHANNELS):
        series = wave_ref[c].astype(F32)
        for s in range(STATIONS):
            for block in range(BLOCKS):
                at = c * SPAN + s * BLOCKS + block
                rows_ref[at : at + 1, :] = series[s : s + 1, block * LANES : (block + 1) * LANES]
    rows_ref[ROWS : ROWS + 1, :] = jnp.concatenate([row.astype(F32), pad], axis=1)
    rows_ref[ROWS + 1 : ROWS + 2, :] = jnp.concatenate([shift.astype(F32), pad], axis=1)
    rows_ref[ROWS + 2 : PACKED, :] = jnp.zeros((PACKED - ROWS - 2, LANES), F32)
    out_ref[...] = jnp.broadcast_to(rows_ref[...].astype(BF16)[None], out_ref.shape)


def tile_kernel(tiles_ref, station_ref, sorted_ref, scale_ref, owner_ref):
    tpl_dev, k_slots, row_len = tiles_ref.shape
    count = tpl_dev * k_slots
    total = scale_ref.shape[0]
    station = station_ref[...].astype(F32).astype(BF16)
    home = ones_where(iota((count, tpl_dev), 0) // k_slots == iota((count, tpl_dev), 1))
    home_t = ones_where(iota((tpl_dev, count), 1) // k_slots == iota((tpl_dev, count), 0))
    by_row = dot_nt(home, station)
    by_col = dot(station, home_t)
    own_col = iota((count, k_slots), 0) % k_slots == iota((count, k_slots), 1)
    own_row = iota((k_slots, count), 1) % k_slots == iota((k_slots, count), 0)
    st_col = jnp.sum(jnp.where(own_col, by_row, 0.0), axis=1, keepdims=True)
    st_row = jnp.sum(jnp.where(own_row, by_col, 0.0), axis=0, keepdims=True)
    earlier = iota((count, count), 0) < iota((count, count), 1)
    rank = jnp.sum(jnp.where((st_col == st_row) & earlier, 1.0, 0.0), axis=0, keepdims=True)
    slot = (st_row * SLOTS + rank).astype(jnp.int32)
    tiles = tiles_ref[...].reshape(count, row_len)
    step = 128
    for first in range(0, total, step):
        place = ones_where(iota((step, count), 0) + first == slot)
        moved = dot(place, tiles)
        mean = jnp.sum(moved * moved, axis=1, keepdims=True) / row_len
        scale = lax.rsqrt(row_len * (mean + EPS))
        scale_ref[first : first + step, :] = jnp.broadcast_to(scale, (step, LANES))
        owner_ref[:, first : first + step] = dot_nt(home_t, place).astype(BF16)
        moved = moved.reshape(step // SLOTS, SLOTS, row_len)
        for c in range(CHANNELS):
            parts = [moved[:, :, (TAPS * c + h) * LANES : (TAPS * c + h + 1) * LANES] for h in range(TAPS)]
            block = jnp.stack(parts, axis=1).reshape(step * TAPS, LANES)
            sorted_ref[first * TAPS : (first + step) * TAPS, c * LANES : (c + 1) * LANES] = block.astype(BF16)


def windows_kernel(data_ref, rows_ref, win_ref):
    groups = data_ref.shape[0]
    step = min(8, groups)
    column_of = iota((LANES, LANES), 1)
    sample = FINE * (COARSE - 1 - column_of % COARSE) + column_of // COARSE
    row = iota((LANES, LANES), 0)
    sums_of = ones_where(jnp.concatenate([row >= sample, row < sample, row >= 0], axis=1))
    major, chunk = iota((step, FINE, LANES), 1), iota((step, FINE, LANES), 2) // COARSE

    def body(q, carry):
        x = data_ref[pl.ds(q * step, step)].astype(F32)
        rows_ref[pl.ds(q * step, step)] = x
        energy = sum(x[:, SPAN * c : SPAN * (c + 1)] * x[:, SPAN * c : SPAN * (c + 1)] for c in range(CHANNELS))
        sums = sum(dot(part, sums_of) for part in pieces(energy.reshape(step * SPAN, LANES), 3))
        sums = sums.reshape(step, SPAN, 3 * LANES)
        for s in range(STATIONS):
            at = BLOCKS * s
            mean = sums[:, at : at + LAG_BLOCKS, 0:LANES]
            for j in range(1, TAPS):
                mean = mean + sums[:, at + j : at + j + LAG_BLOCKS, 2 * LANES :]
            mean = (mean + sums[:, at + TAPS : at + TAPS + LAG_BLOCKS, LANES : 2 * LANES]) / (
                CHANNELS * TAPS * LANES
            )
            value = lax.rsqrt(mean + EPS)
            for bit in range(3):
                size = 1 << bit
                up = (major // size) % 2
                other = (chunk // size) % 2
                later = rot(rot(value, -size, 1), size * COARSE, 2)
                earlier = rot(rot(value, size, 1), -size * COARSE, 2)
                value = jnp.where(up == other, value, jnp.where(up == 0, later, earlier))
            win_ref[pl.ds(q * step, step), s] = value
        return carry

    lax.fori_loop(0, groups // step, body, 0)


def build_data(rows_ref, group, s, out_ref):
    lane = iota((COARSE, LANES), 1)
    bound = FINE * (iota((COARSE, LANES), 0) + 1)

    def turned(c, block):
        at = SPAN * c + BLOCKS * s + block
        row = jnp.broadcast_to(rows_ref[group, at : at + 1, :], (COARSE, LANES))
        return pltpu.roll(row, FINE, 1, stride=FINE, stride_axis=0).astype(BF16)

    now = [turned(c, 0) for c in range(CHANNELS)]
    for run in range(RUNS):
        later = [turned(c, run + 1) for c in range(CHANNELS)]
        rows = slice(run * COARSE, (run + 1) * COARSE)
        for c in range(CHANNELS):
            out_ref[rows, c * LANES : (c + 1) * LANES] = jnp.where(lane < bound, now[c], later[c])
        tail = later[0]
        for c in range(1, CHANNELS):
            tail = jnp.where(lane < FINE * c, tail, rot(later[c], FINE * c))
        out_ref[rows, CHANNELS * LANES :] = tail
        now = later


def build_taps(blocks_of, fine, height, out_ref, first, step):
    lane = iota((height, LANES), 1)
    zero = jnp.zeros((height, LANES), BF16)
    for b in range(fine):
        rows = slice(first + step * b, first + step * b + height)
        tail = zero
        at = 0
        for c, blocks in enumerate(blocks_of):
            before = zero
            for block in blocks:
                moved = rot(block, b)
                out_ref[rows, at : at + LANES] = jnp.where(lane < b, before, moved) if b else moved
                before = moved
                at += LANES
            if b:
                end = rot(blocks[-1], b + fine * c)
                tail = jnp.where((lane >= fine * c) & (lane < fine * c + b), end, tail)
        out_ref[rows, at : at + LANES] = tail


def taps_kernel(sorted_ref, out_ref):
    height = FINE * TAPS * SLOTS
    stations = out_ref.shape[0] // height

    def body(i, carry):
        station = pl.program_id(0) * stations + i
        out = out_ref.at[pl.ds(pl.multiple_of(i * height, height), height), :]
        for pair in range(TAPS // 2):
            at = station * TAPS * SLOTS + pair * 2 * SLOTS
            tiles = sorted_ref[pl.ds(pl.multiple_of(at, 2 * SLOTS), 2 * SLOTS), :]
            blocks = [[tiles[:, c * LANES : (c + 1) * LANES]] for c in range(CHANNELS)]
            build_taps(blocks, FINE, 2 * SLOTS, out, pair * 2 * SLOTS, TAPS * SLOTS)
        return carry

    lax.fori_loop(0, stations, body, 0)


def correlate_kernel(rows_ref, win_ref, taps_ref, scale_ref, high_ref, low_ref, *x_refs):
    stations = rows_ref.shape[0] * STATIONS
    height = FINE * TAPS * SLOTS
    per_step = taps_ref.shape[0] // height
    base = pl.program_id(0) * per_step
    lane = iota((SLOTS, LANES), 1)

    def build(k):
        group = jnp.minimum((base + k) // STATIONS, stations // STATIONS - 1)
        build_data(rows_ref, group, k % STATIONS, x_refs[k % len(x_refs)])

    @pl.when(pl.program_id(0) == 0)
    def _():
        for ref in x_refs:
            ref[RUNS * COARSE :, :] = jnp.zeros((MXU - RUNS * COARSE, DEPTH), BF16)
        for k in range(2):
            build(k)

    def multiply(k, acc):
        data_ref = x_refs[k % len(x_refs)]
        for t in range(DEPTH // MXU):
            lanes = slice(t * MXU, (t + 1) * MXU)
            pltpu.matmul_push_rhs(data_ref[:, lanes], t % 2, k % 2, transpose=True)
            pltpu.matmul_acc_lhs(acc, taps_ref[k * height : (k + 1) * height, lanes], load_staged_rhs=t % 2)

    def lags(k, acc):
        raw = pltpu.matmul_pop(acc)
        st = base + k
        scale = scale_ref[pl.ds(pl.multiple_of(st * SLOTS, SLOTS), SLOTS), :]
        out = []
        for b in range(FINE):
            total = None
            for h in reversed(range(TAPS)):
                row = (b * TAPS + h) * SLOTS
                part = raw[row : row + SLOTS, 0:LANES]
                if h:
                    part = jnp.where(lane < h * COARSE, raw[row : row + SLOTS, LANES:], part)
                total = part if total is None else part + rot(total, -COARSE)
            out.append(total * scale * win_ref[st // STATIONS, k % STATIONS, b : b + 1, :])
        return out

    def run(*accs):
        done = []
        for k in range(per_step + 1):
            if k < per_step:
                multiply(k, accs[k % len(accs)])
                build(k + 2)
            if k:
                done.append(lags(k - 1, accs[(k - 1) % len(accs)]))
            if len(done) == STATIONS:
                at = pl.multiple_of((base + k - STATIONS) * SLOTS, STATIONS * SLOTS)
                for b in range(FINE):
                    high, low = pieces(jnp.concatenate([value[b] for value in done], axis=0), 2)
                    rows = pl.ds(at, STATIONS * SLOTS)
                    high_ref[rows, b * LANES : (b + 1) * LANES] = high
                    low_ref[rows, b * LANES : (b + 1) * LANES] = low
                done = []

    pl.run_scoped(run, *[pltpu.ACC(n % 2)((height, MXU), F32) for n in range(4)])


def stack_kernel(owner_ref, high_ref, low_ref, stack_ref):
    total = dot(owner_ref[...], high_ref[...]) + dot(owner_ref[...], low_ref[...])
    tpl_dev = stack_ref.shape[0]
    block_of = iota((tpl_dev, FINE * LANES), 1) % LANES // COARSE
    place = iota((FINE * LANES, LANES), 0)
    spread = iota((FINE * LANES, LANES), 1) == FINE * (COARSE - 1 - place % COARSE) + place // LANES
    spread = ones_where(spread)
    out = 0.0
    for part in pieces(total, 2):
        part = part.astype(F32)
        masked = [jnp.where(block_of == block, part, 0.0) for block in range(LAG_BLOCKS)]
        out = out + dot(jnp.concatenate(masked, axis=0).astype(BF16), spread)
    for block in range(LAG_BLOCKS):
        rows = out[block * tpl_dev : (block + 1) * tpl_dev]
        stack_ref[:, block * LANES : (block + 1) * LANES] = rows * (1.0 / 8.0**0.5)


def cut(data, row, shift, blocks):
    det_dev = row.shape[0]
    row_iota, lane = iota((det_dev, PACKED), 1), iota((det_dev, LANES), 1)
    picks = [row_iota == row + (SPAN * c + j) for c in range(CHANNELS) for j in range(blocks)]
    picks = jnp.concatenate([jnp.where(pick, 1.0, 0.0) for pick in picks], axis=0).astype(BF16)
    found = dot(picks, data).astype(BF16)
    found = [
        [found[(c * blocks + j) * det_dev : (c * blocks + j + 1) * det_dev] for j in range(blocks)]
        for c in range(CHANNELS)
    ]
    shift = jnp.broadcast_to(shift, (det_dev, LANES))
    for bit in range(7):
        size = 1 << bit
        moves = (shift & size) > 0
        found = [[jnp.where(moves, rot(block, -size), block) for block in row] for row in found]
    inside = lane < LANES - shift
    return [[jnp.where(inside, row[j], row[j + 1]) for j in range(blocks - 1)] for row in found]


def mean_square(blocks):
    total = 0.0
    for block, mask in blocks:
        block = block.astype(F32)
        square = block * block
        total = total + (square if mask is None else jnp.where(mask, square, 0.0))
    return jnp.sum(total, axis=1, keepdims=True) / (CHANNELS * W)


def own_windows(data, time_ref, station_ref):
    n = time_ref.shape[1]
    turned = iota((n, n), 0) ^ (DET_ROWS - 1) == iota((n, n), 1)
    start = jnp.sum(jnp.where(turned, time_ref[...], 0), axis=1, keepdims=True)
    station = jnp.sum(jnp.where(turned, station_ref[...], 0), axis=1, keepdims=True)
    mine = cut(data, station * BLOCKS + start // LANES, start % LANES, KEEP + 1)
    scale = lax.rsqrt(CHANNELS * W * (mean_square([(block, None) for blocks in mine for block in blocks]) + EPS))
    scale = jnp.sum(jnp.where(turned, scale, 0.0), axis=0, keepdims=True)
    return mine, column(scale)


def partner_windows(data, chosen_row):
    det_dev = chosen_row.shape[1]
    lane = iota((det_dev, LANES), 1)
    info = dot_nt(ones_where(lane == column(chosen_row)), data[PACKED - 16 : PACKED, :])
    pieces_of = cut(data, info[:, 8:9].astype(jnp.int32), info[:, 9:10].astype(jnp.int32), KEEP + 2)
    centre = []
    for first, middle, last in pieces_of:
        centre += [(first, lane >= HALF), (middle, None), (last, lane < HALF)]
    return pieces_of, lax.rsqrt(mean_square(centre) + EPS)


def differential(mine, windows, x_ref, w_ref, parts_ref):
    count = len(windows)
    det_dev = mine[0][0].shape[0]
    height = count * DET_ROWS
    lane = iota((DET_ROWS, LANES), 1)
    wide = DET_FINE * DET_ROWS
    sub_lane = iota((8, LANES), 1) % DET_ROWS
    for q in range(det_dev // DET_ROWS):
        rows = slice(q * DET_ROWS, (q + 1) * DET_ROWS)
        build_taps([[block[rows] for block in blocks] for blocks in mine], DET_FINE, DET_ROWS, w_ref, 0, DET_ROWS)
        for d in range(count):
            source = [[block[rows] for block in blocks] for blocks in windows[d]]
            ends = {}
            for a in range(DET_COARSE):
                shift = DET_FINE * a
                out = slice((a * count + d) * DET_ROWS, (a * count + d + 1) * DET_ROWS)
                tail = None
                for c in range(CHANNELS):
                    moved = [rot(block, -shift) for block in source[c]]
                    ends[c, a] = moved[KEEP]
                    for j in range(KEEP):
                        block = jnp.where(lane < LANES - shift, moved[j], moved[j + 1]) if a else moved[j]
                        at = (c * KEEP + j) * LANES
                        x_ref[out, at : at + LANES] = block
                    end = ends[c, a - c] if a >= c else rot(source[c][KEEP], DET_FINE * c - shift)
                    tail = end if tail is None else jnp.where(lane < DET_FINE * c, tail, end)
                x_ref[out, DET_DEPTH - LANES : DET_DEPTH] = tail
        raw = dot_nt(x_ref[0 : DET_COARSE * height, :], w_ref[...])
        for half in range(2):
            for row in range(0, height, 8):
                upper = row % DET_ROWS // 8
                total = jnp.zeros((8, LANES), F32)
                for a in range(DET_COARSE):
                    part = raw[a * height + row : a * height + row + 8, half * LANES : (half + 1) * LANES]
                    base = a + 1 if upper else a + LANES - DET_ROWS + 1
                    part = pltpu.roll(part, base, 1, stride=1, stride_axis=0)
                    total = jnp.where(sub_lane == 8 * upper + a, part, total)
                parts_ref[q * height + row : q * height + row + 8, half * LANES : (half + 1) * LANES] = total
    place, to = iota((wide, LANES), 0), iota((wide, LANES), 1)
    order = ones_where((to // DET_FINE == place % DET_COARSE) & (to % DET_FINE == place // DET_ROWS))
    return sum(dot(part, order) for part in pieces(parts_ref[...], 2))


def detect_kernel(
    ngx, ngy, data_ref, time_ref, station_ref, partner_ref, diff_ref, x_ref, w_ref, parts_ref
):
    gx, gy = lax.axis_index("gx"), lax.axis_index("gy")
    mine, mine_scale = own_windows(data_ref[gx * ngy + gy], time_ref, station_ref)
    windows, scales = [], []
    for d, (dx, dy) in enumerate(((1, 0), (-1, 0), (0, 1), (0, -1))):
        x, y = gx + dx, gy + dy
        valid = (x >= 0) & (x < ngx) & (y >= 0) & (y < ngy)
        data = data_ref[jnp.clip(x, 0, ngx - 1) * ngy + jnp.clip(y, 0, ngy - 1)]
        found, scale = partner_windows(data, partner_ref[d : d + 1, :])
        windows.append(found)
        scales.append(jnp.where(valid, mine_scale * scale, 0.0))
    out = differential(mine, windows, x_ref, w_ref, parts_ref)
    for q in range(time_ref.shape[1] // DET_ROWS):
        for d in range(4):
            at = (q * 4 + d) * DET_ROWS
            rows = slice(q * DET_ROWS, (q + 1) * DET_ROWS)
            diff_ref[pl.ds(q * DET_ROWS * 4 + d, DET_ROWS, stride=4), :] = (
                out[at : at + DET_ROWS] * scales[d][rows]
            )


def on_device(ngx, ngy, waveforms, templates, tpl_stations, det_station, det_time, partner):
    tpl_dev, k_slots, row_len = templates.shape
    det_dev = det_station.shape[0]
    groups = ngx * ngy
    stations = groups * STATIONS
    total = stations * SLOTS
    time_row, station_row = det_time.reshape(1, det_dev), det_station.reshape(1, det_dev)
    params = pltpu.CompilerParams(vmem_limit_bytes=(16 << 20) + groups * (1 << 17))
    packed = pl.pallas_call(
        pack_kernel,
        out_shape=jax.ShapeDtypeStruct((groups, PACKED, LANES), BF16),
        scratch_shapes=[pltpu.VMEM((PACKED, LANES), F32)],
        name="pack",
    )(waveforms.transpose(1, 0, 2), time_row, station_row)
    data = lax.all_to_all(packed, ("gx", "gy"), split_axis=0, concat_axis=0, tiled=True)
    tiles, scale, owner = pl.pallas_call(
        tile_kernel,
        out_shape=(
            jax.ShapeDtypeStruct((total * TAPS, CHANNELS * LANES), BF16),
            jax.ShapeDtypeStruct((total, LANES), F32),
            jax.ShapeDtypeStruct((tpl_dev, total), BF16),
        ),
        compiler_params=params,
        name="tiles",
    )(templates, tpl_stations.T)
    steps = groups // 4
    height = 4 * STATIONS * FINE * TAPS * SLOTS

    def whole(*shape):
        return pl.BlockSpec(shape, lambda i: (0,) * len(shape))

    def piece(*shape):
        return pl.BlockSpec(shape, lambda i: (i,) + (0,) * (len(shape) - 1))

    taps = pl.pallas_call(
        taps_kernel,
        grid=(steps,),
        in_specs=[whole(*tiles.shape)],
        out_specs=piece(height, DEPTH),
        out_shape=pltpu.HBM((steps * height, DEPTH), BF16),
        compiler_params=params,
        name="taps",
    )(tiles)
    taps = pltpu.with_memory_space_constraint(taps, pltpu.HBM)
    series, win = pl.pallas_call(
        windows_kernel,
        out_shape=(
            jax.ShapeDtypeStruct((groups, PACKED, LANES), F32),
            jax.ShapeDtypeStruct((groups, STATIONS, FINE, LANES), F32),
        ),
        compiler_params=params,
        name="windows",
    )(data)
    sums = (total, FINE * LANES)
    high, low = pl.pallas_call(
        correlate_kernel,
        grid=(steps,),
        in_specs=[whole(*series.shape), whole(*win.shape), piece(height, DEPTH), whole(*scale.shape)],
        out_specs=(whole(*sums), whole(*sums)),
        out_shape=(jax.ShapeDtypeStruct(sums, BF16),) * 2,
        scratch_shapes=[pltpu.VMEM((MXU, DEPTH), BF16)] * 4,
        compiler_params=params,
        name="correlate",
    )(series, win, taps, scale)
    stack = pl.pallas_call(
        stack_kernel,
        out_shape=jax.ShapeDtypeStruct((tpl_dev, LAG_BLOCKS * LANES), F32),
        compiler_params=params,
        name="stack",
    )(owner, high, low)
    diff = pl.pallas_call(
        functools.partial(detect_kernel, ngx, ngy),
        out_shape=jax.ShapeDtypeStruct((4 * det_dev, DTLAG), F32),
        scratch_shapes=[
            pltpu.VMEM((4 * DET_COARSE * DET_ROWS, DET_DEPTH), BF16),
            pltpu.VMEM((DET_FINE * DET_ROWS, DET_DEPTH), BF16),
            pltpu.VMEM((4 * det_dev, DET_FINE * DET_ROWS), F32),
        ],
        compiler_params=params,
        name="detect",
    )(data, time_row, station_row, partner.T)
    return stack, diff.reshape(det_dev, 4, DTLAG)


def solution(mesh):
    return jax.shard_map(
        functools.partial(on_device, mesh.shape["gx"], mesh.shape["gy"]),
        mesh=mesh,
        in_specs=(
            P(("gx", "gy"), None, None),
            P(("gx", "gy"), None, None),
            P(("gx", "gy"), None),
            P(("gx", "gy")),
            P(("gx", "gy")),
            P(("gx", "gy"), None),
        ),
        out_specs=(P(("gx", "gy"), None), P(("gx", "gy"), None, None)),
        check_vma=False,
    )
```

```python
import functools

import jax
import jax.numpy as jnp
from jax import lax
from jax.experimental import pallas as pl
from jax.experimental.pallas import tpu as pltpu
from jax.sharding import PartitionSpec as P

LANES = 128
CHANNELS = 3
STATIONS = 2
BLOCKS = 12
TAPS = 4
LAG_BLOCKS = BLOCKS - TAPS
SLOTS = 8
FINE = 8
COARSE = LANES // FINE
DET_FINE = 16
DET_COARSE = LANES // DET_FINE
DET_ROWS = 16
W = 256
DTLAG = 128
HALF = DTLAG // 2
KEEP = W // LANES
DET_DEPTH = CHANNELS * KEEP * LANES + LANES
SPAN = STATIONS * BLOCKS
ROWS = CHANNELS * SPAN
PACKED = ROWS + 8
MXU = 256
PASSES = (CHANNELS * (TAPS + 1) + 1) // 2
EPS = 1e-06
F32 = jnp.float32
BF16 = jnp.bfloat16
NT = (((1,), (1,)), ((), ()))


def iota(shape, axis):
    return lax.broadcasted_iota(jnp.int32, shape, axis)


def rot(value, shift, axis=1):
    shift = shift % value.shape[axis]
    return pltpu.roll(value, shift, axis) if shift else value


def dot(a, b):
    return jnp.dot(a, b, preferred_element_type=F32)


def dot_nt(a, b):
    return lax.dot_general(a, b, NT, preferred_element_type=F32)


def ones_where(mask):
    return jnp.where(mask, 1.0, 0.0).astype(BF16)


def pieces(value, count):
    out = []
    for _ in range(count - 1):
        high = value.astype(BF16)
        out.append(high)
        value = value - high.astype(F32)
    out.append(value.astype(BF16))
    return out


def column(row):
    n = row.shape[1]
    diagonal = iota((n, n), 0) == iota((n, n), 1)
    return jnp.sum(jnp.where(diagonal, row, 0), axis=1, keepdims=True)


def pack_kernel(wave_ref, time_ref, station_ref, out_ref, rows_ref):
    start = time_ref[...] - HALF
    row = BLOCKS * station_ref[...] + start // LANES
    shift = start % LANES
    pad = jnp.zeros((1, LANES - row.shape[1]), F32)
    for c in range(CHANNELS):
        series = wave_ref[c].astype(F32)
        for s in range(STATIONS):
            for block in range(BLOCKS):
                at = c * SPAN + s * BLOCKS + block
                rows_ref[at : at + 1, :] = series[s : s + 1, block * LANES : (block + 1) * LANES]
    rows_ref[ROWS : ROWS + 1, :] = jnp.concatenate([row.astype(F32), pad], axis=1)
    rows_ref[ROWS + 1 : ROWS + 2, :] = jnp.concatenate([shift.astype(F32), pad], axis=1)
    rows_ref[ROWS + 2 : PACKED, :] = jnp.zeros((PACKED - ROWS - 2, LANES), F32)
    out_ref[0] = rows_ref[...].astype(BF16)


def join_kernel(near_ref, other_ref, after_ref, out_ref):
    half = near_ref.shape[0]
    out_ref[0:half] = near_ref[...]
    out_ref[half:] = other_ref[...]


def rounds(ngx, ngy):
    masks = []
    for axis, size in (("gy", ngy), ("gx", ngx)):
        while size > 1:
            size //= 2
            masks.append((axis, size))
    return masks


def position(ngx, ngy, x, y):
    away = {"gx": x ^ lax.axis_index("gx"), "gy": y ^ lax.axis_index("gy")}
    return sum(((away[axis] // mask) & 1) << n for n, (axis, mask) in enumerate(rounds(ngx, ngy)))


def tile_kernel(ngx, ngy, tiles_ref, station_ref, sorted_ref, scale_ref, owner_ref):
    tpl_dev, k_slots, row_len = tiles_ref.shape
    count = tpl_dev * k_slots
    total = sorted_ref.shape[0]
    station = station_ref[...].astype(F32).astype(BF16)
    home = ones_where(iota((count, tpl_dev), 0) // k_slots == iota((count, tpl_dev), 1))
    home_t = ones_where(iota((tpl_dev, count), 1) // k_slots == iota((tpl_dev, count), 0))
    by_row = dot_nt(home, station)
    by_col = dot(station, home_t)
    own_col = iota((count, k_slots), 0) % k_slots == iota((count, k_slots), 1)
    own_row = iota((k_slots, count), 1) % k_slots == iota((k_slots, count), 0)
    st_col = jnp.sum(jnp.where(own_col, by_row, 0.0), axis=1, keepdims=True)
    st_row = jnp.sum(jnp.where(own_row, by_col, 0.0), axis=0, keepdims=True)
    earlier = iota((count, count), 0) < iota((count, count), 1)
    rank = jnp.sum(jnp.where((st_col == st_row) & earlier, 1.0, 0.0), axis=0, keepdims=True)
    st = st_row.astype(jnp.int32)
    group = st // STATIONS
    place_of = position(ngx, ngy, group // ngy, group % ngy)
    slot = (place_of * STATIONS + st % STATIONS) * SLOTS + rank.astype(jnp.int32)
    tiles = tiles_ref[...].reshape(count, row_len)
    step = 128
    for first in range(0, total, step):
        place = ones_where(iota((step, count), 0) + first == slot)
        moved = dot(place, tiles)
        sorted_ref[first : first + step, :] = moved.astype(BF16)
        mean = jnp.sum(moved * moved, axis=1, keepdims=True) / row_len
        scale = lax.rsqrt(row_len * (mean + EPS))
        scale_ref[first : first + step, :] = jnp.broadcast_to(scale, (step, LANES))
        owner_ref[:, first : first + step] = dot_nt(home_t, place).astype(BF16)


def windows_kernel(data_ref, rows_ref, win_ref):
    groups = data_ref.shape[0]
    step = min(8, groups)
    column_of = iota((LANES, LANES), 1)
    sample = FINE * (COARSE - 1 - column_of % COARSE) + column_of // COARSE
    row = iota((LANES, LANES), 0)
    sums_of = ones_where(jnp.concatenate([row >= sample, row < sample, row >= 0], axis=1))
    major, chunk = iota((step, FINE, LANES), 1), iota((step, FINE, LANES), 2) // COARSE

    def body(q, carry):
        x = data_ref[pl.ds(q * step, step)].astype(F32)
        rows_ref[pl.ds(q * step, step)] = x
        energy = sum(x[:, SPAN * c : SPAN * (c + 1)] * x[:, SPAN * c : SPAN * (c + 1)] for c in range(CHANNELS))
        sums = sum(dot(part, sums_of) for part in pieces(energy.reshape(step * SPAN, LANES), 3))
        sums = sums.reshape(step, SPAN, 3 * LANES)
        for s in range(STATIONS):
            at = BLOCKS * s
            mean = sums[:, at : at + LAG_BLOCKS, 0:LANES]
            for j in range(1, TAPS):
                mean = mean + sums[:, at + j : at + j + LAG_BLOCKS, 2 * LANES :]
            mean = (mean + sums[:, at + TAPS : at + TAPS + LAG_BLOCKS, LANES : 2 * LANES]) / (
                CHANNELS * TAPS * LANES
            )
            value = lax.rsqrt(mean + EPS)
            for bit in range(3):
                size = 1 << bit
                up = (major // size) % 2
                other = (chunk // size) % 2
                later = rot(rot(value, -size, 1), size * COARSE, 2)
                earlier = rot(rot(value, size, 1), -size * COARSE, 2)
                value = jnp.where(up == other, value, jnp.where(up == 0, later, earlier))
            win_ref[pl.ds(q * step, step), s] = value
        return carry

    lax.fori_loop(0, groups // step, body, 0)


def build_data(rows_ref, g, s, c, out_ref):
    lane = iota((COARSE, LANES), 1)
    bound = FINE * (iota((COARSE, LANES), 0) + 1)
    now = None
    for block in range(BLOCKS):
        at = SPAN * c + BLOCKS * s + block
        row = rows_ref[g, pl.ds(at, FINE, stride=0), :]
        turned = [
            pltpu.roll(row, FINE * (1 + first), 1, stride=FINE, stride_axis=0) for first in range(0, COARSE, FINE)
        ]
        later = jnp.concatenate(turned, axis=0).astype(BF16)
        if block:
            out_ref[(block - 1) * COARSE : block * COARSE, c * LANES : (c + 1) * LANES] = jnp.where(
                lane < bound, now, later
            )
        now = later
    out_ref[(BLOCKS - 1) * COARSE : BLOCKS * COARSE, c * LANES : (c + 1) * LANES] = now


def build_taps(blocks_of, fine, height, out_ref, first, step):
    lane = iota((height, LANES), 1)
    zero = jnp.zeros((height, LANES), BF16)
    for b in range(fine):
        rows = slice(first + step * b, first + step * b + height)
        tail = zero
        at = 0
        for c, blocks in enumerate(blocks_of):
            before = zero
            for block in blocks:
                moved = rot(block, b)
                out_ref[rows, at : at + LANES] = jnp.where(lane < b, before, moved) if b else moved
                before = moved
                at += LANES
            if b:
                end = rot(blocks[-1], b + fine * c)
                tail = jnp.where((lane >= fine * c) & (lane < fine * c + b), end, tail)
        out_ref[rows, at : at + LANES] = tail


def taps_kernel(first, sorted_ref, after_ref, out_ref):
    height = FINE * STATIONS * SLOTS
    per_step = out_ref.shape[0] // height
    rows = STATIONS * SLOTS
    lane = iota((rows, LANES), 1)
    zero = jnp.zeros((rows, LANES), BF16)

    def body(i, carry):
        at = (first() * per_step + i) * rows
        tiles = sorted_ref[pl.ds(pl.multiple_of(at, rows), rows), :]
        out = out_ref.at[pl.ds(pl.multiple_of(i * height, height), height), :]
        for c in range(CHANNELS):
            blocks = [tiles[:, (TAPS * c + j) * LANES : (TAPS * c + j + 1) * LANES] for j in range(TAPS)]
            for b in range(FINE):
                before = zero
                for j in range(TAPS + 1):
                    moved = rot(blocks[j], b) if j < TAPS else zero
                    lanes = slice((c * (TAPS + 1) + j) * LANES, (c * (TAPS + 1) + j + 1) * LANES)
                    out[b * rows : (b + 1) * rows, lanes] = jnp.where(lane < b, before, moved) if b else moved
                    before = moved
        out[:, CHANNELS * (TAPS + 1) * LANES :] = jnp.zeros((height, LANES), BF16)
        return carry

    lax.fori_loop(0, per_step, body, 0)


def correlate_kernel(call, rows_ref, win_ref, taps_ref, scale_ref, high_ref, low_ref, *refs):
    x_refs = [[refs[4 * bank + 2 * n : 4 * bank + 2 * n + 2] for n in range(2)] for bank in range(2)]
    groups = rows_ref.shape[0]
    rows = STATIONS * SLOTS
    height = FINE * rows
    step = pl.program_id(0)
    parts = [(c, j) for c in range(CHANNELS) for j in range(TAPS + 1)]
    parts = parts + parts[:1]

    def builds(first, bank):
        for n in range(2):
            for s in range(STATIONS):
                for c in range(CHANNELS):
                    yield lambda n=n, s=s, c=c: build_data(rows_ref, first + n, s, c, x_refs[bank][n][s])

    @pl.when(step == 0)
    def _():
        for write in builds(0, 0):
            write()

    def store_lags(i, raw):
        g = step * 4 + i
        scale = scale_ref[pl.ds(pl.multiple_of((call * groups + g) * rows, rows), rows), :]
        at = pl.ds(pl.multiple_of(g * rows, rows), rows)
        for b in range(FINE):
            value, window = [], []
            for s in range(STATIONS):
                first = b * rows + s * SLOTS
                value.append(raw[first : first + SLOTS, s * LANES : (s + 1) * LANES])
                window.append(jnp.broadcast_to(win_ref[g, s, b : b + 1, :], (SLOTS, LANES)))
            value = jnp.concatenate(value, axis=0) * scale * jnp.concatenate(window, axis=0)
            high, low = pieces(value, 2)
            high_ref[at, b * LANES : (b + 1) * LANES] = high
            low_ref[at, b * LANES : (b + 1) * LANES] = low

    def multiply(accs, bank, writes):
        for t in range(PASSES):
            for n in range(2):
                data = [
                    jnp.concatenate(
                        [ref[j * COARSE : j * COARSE + LANES, c * LANES : (c + 1) * LANES] for c, j in parts[2 * t : 2 * t + 2]],
                        axis=1,
                    )
                    for ref in x_refs[bank][n]
                ]
                pltpu.matmul_push_rhs(jnp.concatenate(data, axis=0), t % 2, n, transpose=True)
                first = (2 * bank + n) * height
                taps = taps_ref[first : first + height, t * MXU : (t + 1) * MXU]
                pltpu.matmul_acc_lhs(accs[n], taps, load_staged_rhs=t % 2)
            for write in writes[t::PASSES]:
                write()

    def four_groups(*accs):
        multiply(accs[:2], 0, list(builds(step * 4 + 2, 1)))
        finish = [lambda n=n: store_lags(n, pltpu.matmul_pop(accs[n])) for n in range(2)]
        multiply(accs[2:], 1, list(builds(jnp.minimum(step * 4 + 4, groups - 2), 0)) + finish)
        for n in range(2):
            store_lags(2 + n, pltpu.matmul_pop(accs[2 + n]))

    pl.run_scoped(four_groups, *[pltpu.ACC(n % 2)((height, MXU), F32) for n in range(4)])


def stack_kernel(owner_ref, near_high_ref, near_low_ref, far_high_ref, far_low_ref, stack_ref):
    half = near_high_ref.shape[0]
    total = 0.0
    for near, far in ((near_high_ref, far_high_ref), (near_low_ref, far_low_ref)):
        total = total + dot(owner_ref[:, 0:half], near[...]) + dot(owner_ref[:, half:], far[...])
    tpl_dev = stack_ref.shape[0]
    block_of = iota((tpl_dev, FINE * LANES), 1) % LANES // COARSE
    place = iota((FINE * LANES, LANES), 0)
    spread = iota((FINE * LANES, LANES), 1) == FINE * (COARSE - 1 - place % COARSE) + place // LANES
    spread = ones_where(spread)
    out = 0.0
    for part in pieces(total, 2):
        part = part.astype(F32)
        masked = [jnp.where(block_of == block, part, 0.0) for block in range(LAG_BLOCKS)]
        out = out + dot(jnp.concatenate(masked, axis=0).astype(BF16), spread)
    for block in range(LAG_BLOCKS):
        rows = out[block * tpl_dev : (block + 1) * tpl_dev]
        stack_ref[:, block * LANES : (block + 1) * LANES] = rows * (1.0 / 8.0**0.5)


def cut(data, row, shift, blocks):
    det_dev = row.shape[0]
    row_iota, lane = iota((det_dev, PACKED), 1), iota((det_dev, LANES), 1)
    picks = [row_iota == row + (SPAN * c + j) for c in range(CHANNELS) for j in range(blocks)]
    picks = jnp.concatenate([jnp.where(pick, 1.0, 0.0) for pick in picks], axis=0).astype(BF16)
    found = dot(picks, data).astype(BF16)
    found = [
        [found[(c * blocks + j) * det_dev : (c * blocks + j + 1) * det_dev] for j in range(blocks)]
        for c in range(CHANNELS)
    ]
    shift = jnp.broadcast_to(shift, (det_dev, LANES))
    for bit in range(7):
        size = 1 << bit
        moves = (shift & size) > 0
        found = [[jnp.where(moves, rot(block, -size), block) for block in row] for row in found]
    inside = lane < LANES - shift
    return [[jnp.where(inside, row[j], row[j + 1]) for j in range(blocks - 1)] for row in found]


def mean_square(blocks):
    total = 0.0
    for block, mask in blocks:
        block = block.astype(F32)
        square = block * block
        total = total + (square if mask is None else jnp.where(mask, square, 0.0))
    return jnp.sum(total, axis=1, keepdims=True) / (CHANNELS * W)


def own_windows(data, time_ref, station_ref):
    n = time_ref.shape[1]
    turned = iota((n, n), 0) ^ (DET_ROWS - 1) == iota((n, n), 1)
    start = jnp.sum(jnp.where(turned, time_ref[...], 0), axis=1, keepdims=True)
    station = jnp.sum(jnp.where(turned, station_ref[...], 0), axis=1, keepdims=True)
    mine = cut(data, station * BLOCKS + start // LANES, start % LANES, KEEP + 1)
    scale = lax.rsqrt(CHANNELS * W * (mean_square([(block, None) for blocks in mine for block in blocks]) + EPS))
    scale = jnp.sum(jnp.where(turned, scale, 0.0), axis=0, keepdims=True)
    return mine, column(scale)


def partner_windows(data, chosen_row):
    det_dev = chosen_row.shape[1]
    lane = iota((det_dev, LANES), 1)
    info = dot_nt(ones_where(lane == column(chosen_row)), data[PACKED - 16 : PACKED, :])
    pieces_of = cut(data, info[:, 8:9].astype(jnp.int32), info[:, 9:10].astype(jnp.int32), KEEP + 2)
    centre = []
    for first, middle, last in pieces_of:
        centre += [(first, lane >= HALF), (middle, None), (last, lane < HALF)]
    return pieces_of, lax.rsqrt(mean_square(centre) + EPS)


def differential(taps_ref, windows, x_ref, parts_ref):
    count = len(windows)
    height = count * DET_ROWS
    lane = iota((DET_ROWS, LANES), 1)
    wide = DET_FINE * DET_ROWS
    sub_lane = iota((8, LANES), 1) % DET_ROWS
    for q in range(taps_ref.shape[0]):
        rows = slice(q * DET_ROWS, (q + 1) * DET_ROWS)
        for d in range(count):
            source = [[block[rows] for block in blocks] for blocks in windows[d]]
            ends = {}
            for a in range(DET_COARSE):
                shift = DET_FINE * a
                out = slice((a * count + d) * DET_ROWS, (a * count + d + 1) * DET_ROWS)
                tail = None
                for c in range(CHANNELS):
                    moved = [rot(block, -shift) for block in source[c]]
                    ends[c, a] = moved[KEEP]
                    for j in range(KEEP):
                        block = jnp.where(lane < LANES - shift, moved[j], moved[j + 1]) if a else moved[j]
                        at = (c * KEEP + j) * LANES
                        x_ref[out, at : at + LANES] = block
                    end = ends[c, a - c] if a >= c else rot(source[c][KEEP], DET_FINE * c - shift)
                    tail = end if tail is None else jnp.where(lane < DET_FINE * c, tail, end)
                x_ref[out, DET_DEPTH - LANES : DET_DEPTH] = tail
        raw = dot_nt(x_ref[0 : DET_COARSE * height, :], taps_ref[q])
        for half in range(2):
            for row in range(0, height, 8):
                upper = row % DET_ROWS // 8
                total = jnp.zeros((8, LANES), F32)
                for a in range(DET_COARSE):
                    part = raw[a * height + row : a * height + row + 8, half * LANES : (half + 1) * LANES]
                    base = a + 1 if upper else a + LANES - DET_ROWS + 1
                    part = pltpu.roll(part, base, 1, stride=1, stride_axis=0)
                    total = jnp.where(sub_lane == 8 * upper + a, part, total)
                parts_ref[q * height + row : q * height + row + 8, half * LANES : (half + 1) * LANES] = total
    place, to = iota((wide, LANES), 0), iota((wide, LANES), 1)
    order = ones_where((to // DET_FINE == place % DET_COARSE) & (to % DET_FINE == place // DET_ROWS))
    return sum(dot(part, order) for part in pieces(parts_ref[...], 2))


def own_kernel(data_ref, time_ref, station_ref, after_ref, taps_ref, scale_ref):
    mine, scale = own_windows(data_ref[0], time_ref, station_ref)
    scale_ref[...] = jnp.broadcast_to(scale, scale_ref.shape)
    for q in range(taps_ref.shape[0]):
        rows = slice(q * DET_ROWS, (q + 1) * DET_ROWS)
        blocks = [[block[rows] for block in channel] for channel in mine]
        build_taps(blocks, DET_FINE, DET_ROWS, taps_ref.at[q], 0, DET_ROWS)


def cuts_kernel(ngx, ngy, near_ref, far_ref, scale_ref, partner_ref, windows_ref, scales_ref):
    gx, gy = lax.axis_index("gx"), lax.axis_index("gy")
    for d, (dx, dy) in enumerate(((1, 0), (-1, 0), (0, 1), (0, -1))):
        x, y = gx + dx, gy + dy
        valid = (x >= 0) & (x < ngx) & (y >= 0) & (y < ngy)
        at = position(ngx, ngy, jnp.clip(x, 0, ngx - 1), jnp.clip(y, 0, ngy - 1)) % near_ref.shape[0]
        data = (far_ref if dx else near_ref)[at]
        found, scale = partner_windows(data, partner_ref[d : d + 1, :])
        for c in range(CHANNELS):
            for j in range(KEEP + 1):
                windows_ref[d, c, j] = found[c][j]
        scales_ref[d] = jnp.where(valid, scale_ref[...] * scale, 0.0)


def detect_kernel(taps_ref, windows_ref, scales_ref, diff_ref, x_ref, parts_ref):
    windows = [[[windows_ref[d, c, j] for j in range(KEEP + 1)] for c in range(CHANNELS)] for d in range(4)]
    out = differential(taps_ref, windows, x_ref, parts_ref)
    for q in range(taps_ref.shape[0]):
        for d in range(4):
            at = (q * 4 + d) * DET_ROWS
            rows = slice(q * DET_ROWS, (q + 1) * DET_ROWS)
            diff_ref[pl.ds(q * DET_ROWS * 4 + d, DET_ROWS, stride=4), :] = (
                out[at : at + DET_ROWS] * scales_ref[d, rows, :]
            )


def on_device(ngx, ngy, waveforms, templates, tpl_stations, det_station, det_time, partner):
    tpl_dev, k_slots, row_len = templates.shape
    det_dev = det_station.shape[0]
    groups = ngx * ngy
    half = groups // 2
    rows = STATIONS * SLOTS
    total = groups * rows
    time_row, station_row = det_time.reshape(1, det_dev), det_station.reshape(1, det_dev)
    packed = pl.pallas_call(
        pack_kernel,
        out_shape=jax.ShapeDtypeStruct((1, PACKED, LANES), BF16),
        scratch_shapes=[pltpu.VMEM((PACKED, LANES), F32)],
        name="pack",
    )(waveforms.transpose(1, 0, 2), time_row, station_row)

    def swap(value, axis, mask):
        size = {"gx": ngx, "gy": ngy}[axis]
        return lax.ppermute(value, axis, [(n, n ^ mask) for n in range(size)])

    vmem, after = pl.BlockSpec(memory_space=pltpu.VMEM), pl.BlockSpec(memory_space=pl.ANY)
    tiles, scale, owner = pl.pallas_call(
        functools.partial(tile_kernel, ngx, ngy),
        out_shape=(
            jax.ShapeDtypeStruct((total, row_len), BF16),
            jax.ShapeDtypeStruct((total, LANES), F32),
            jax.ShapeDtypeStruct((tpl_dev, total), BF16),
        ),
        compiler_params=pltpu.CompilerParams(vmem_limit_bytes=24 << 20),
        name="tiles",
    )(templates, tpl_stations.T)
    steps = groups // 4
    height = 4 * FINE * rows
    depth = MXU * PASSES
    def shifted(call, near):
        shape = (steps // 2 * height, depth)
        limit = pltpu.CompilerParams(vmem_limit_bytes=(8 << 20) + total * row_len * 4)
        if groups <= 32:
            taps = pl.pallas_call(
                functools.partial(taps_kernel, lambda: call),
                in_specs=[vmem, after],
                out_specs=vmem,
                out_shape=pltpu.VMEM(shape, BF16),
                compiler_params=limit,
                name="taps",
            )(tiles, near)
            return pltpu.with_memory_space_constraint(taps, pltpu.VMEM)
        taps = pl.pallas_call(
            functools.partial(taps_kernel, lambda: pl.program_id(0)),
            grid=(steps // 2,),
            in_specs=[pl.BlockSpec((total // 2, row_len), lambda i: (call, 0)), after],
            out_specs=pl.BlockSpec((height, depth), lambda i: (i, 0)),
            out_shape=pltpu.HBM(shape, BF16),
            compiler_params=limit,
            name="taps",
        )(tiles, near)
        return pltpu.with_memory_space_constraint(taps, pltpu.HBM)

    parts = det_dev // DET_ROWS

    def own_detections(near):
        return pl.pallas_call(
            own_kernel,
            out_shape=(
                jax.ShapeDtypeStruct((parts, DET_FINE * DET_ROWS, DET_DEPTH), BF16),
                jax.ShapeDtypeStruct((det_dev, LANES), F32),
            ),
            in_specs=[vmem, vmem, vmem, after],
            compiler_params=pltpu.CompilerParams(vmem_limit_bytes=16 << 20),
            name="own",
        )(packed, time_row, station_row, near)

    near, taps = packed, []
    *first, last = rounds(ngx, ngy)
    for n, (axis, mask) in enumerate(first):
        other = swap(near, axis, mask)
        beside = near
        if n == 0:
            beside = scale
        elif n <= 2:
            taps.append(shifted(n - 1, near))
            beside = taps[-1]
        elif n == len(first) - 1:
            mine, mine_scale = own_detections(near)
            beside = mine_scale
        near = pl.pallas_call(
            join_kernel,
            out_shape=jax.ShapeDtypeStruct((2 * near.shape[0], PACKED, LANES), BF16),
            in_specs=[vmem, vmem, after],
            compiler_params=pltpu.CompilerParams(vmem_limit_bytes=16 << 20),
            name="join",
        )(near, other, beside)
    far = swap(near, *last)

    def whole(*shape):
        return pl.BlockSpec(shape, lambda i: (0,) * len(shape))

    sums = (half * rows, FINE * LANES)
    params = pltpu.CompilerParams(vmem_limit_bytes=(16 << 20) + groups * (1 << 17))

    def correlate(call, data):
        series, win = pl.pallas_call(
            windows_kernel,
            out_shape=(
                jax.ShapeDtypeStruct((half, PACKED, LANES), F32),
                jax.ShapeDtypeStruct((half, STATIONS, FINE, LANES), F32),
            ),
            compiler_params=params,
            name="windows",
        )(data)
        return pl.pallas_call(
            functools.partial(correlate_kernel, call),
            grid=(steps // 2,),
            in_specs=[
                whole(*series.shape),
                whole(*win.shape),
                pl.BlockSpec((height, depth), lambda i: (i, 0)),
                whole(*scale.shape),
            ],
            out_specs=(whole(*sums), whole(*sums)),
            out_shape=(jax.ShapeDtypeStruct(sums, BF16),) * 2,
            scratch_shapes=[pltpu.VMEM((BLOCKS * COARSE, CHANNELS * LANES), BF16)] * 8,
            compiler_params=params,
            name="correlate",
        )(series, win, taps[call], scale)

    near_sums, far_sums = correlate(0, near), correlate(1, far)
    stack = pl.pallas_call(
        stack_kernel,
        out_shape=jax.ShapeDtypeStruct((tpl_dev, LAG_BLOCKS * LANES), F32),
        compiler_params=params,
        name="stack",
    )(owner, *near_sums, *far_sums)
    cuts = pl.pallas_call(
        functools.partial(cuts_kernel, ngx, ngy),
        out_shape=(
            jax.ShapeDtypeStruct((4, CHANNELS, KEEP + 1, det_dev, LANES), BF16),
            jax.ShapeDtypeStruct((4, det_dev, LANES), F32),
        ),
        compiler_params=params,
        name="cuts",
    )(near, far, mine_scale, partner.T)
    diff = pl.pallas_call(
        detect_kernel,
        out_shape=jax.ShapeDtypeStruct((4 * det_dev, DTLAG), F32),
        scratch_shapes=[
            pltpu.VMEM((4 * DET_COARSE * DET_ROWS, DET_DEPTH), BF16),
            pltpu.VMEM((4 * det_dev, DET_FINE * DET_ROWS), F32),
        ],
        compiler_params=params,
        name="detect",
    )(mine, *cuts)
    return stack, diff.reshape(det_dev, 4, DTLAG)


def solution(mesh):
    return jax.shard_map(
        functools.partial(on_device, mesh.shape["gx"], mesh.shape["gy"]),
        mesh=mesh,
        in_specs=(
            P(("gx", "gy"), None, None),
            P(("gx", "gy"), None, None),
            P(("gx", "gy"), None),
            P(("gx", "gy")),
            P(("gx", "gy")),
            P(("gx", "gy"), None),
        ),
        out_specs=(P(("gx", "gy"), None), P(("gx", "gy"), None, None)),
        check_vma=False,
    )
```

```python
import functools

import jax
import jax.numpy as jnp
from jax import lax
from jax.experimental import pallas as pl
from jax.experimental.pallas import tpu as pltpu
from jax.sharding import PartitionSpec as P

LANES = 128
CHANNELS = 3
STATIONS = 2
BLOCKS = 12
TAPS = 4
LAG_BLOCKS = BLOCKS - TAPS
SLOTS = 8
FINE = 8
COARSE = LANES // FINE
DET_FINE = 16
DET_COARSE = LANES // DET_FINE
DET_ROWS = 16
W = 256
DTLAG = 128
HALF = DTLAG // 2
KEEP = W // LANES
DET_DEPTH = CHANNELS * KEEP * LANES + LANES
SPAN = STATIONS * BLOCKS
ROWS = CHANNELS * SPAN
PACKED = ROWS + 8
MXU = 256
PASSES = (CHANNELS * (TAPS + 1) + 1) // 2
EPS = 1e-06
F32 = jnp.float32
BF16 = jnp.bfloat16
NT = (((1,), (1,)), ((), ()))


def iota(shape, axis):
    return lax.broadcasted_iota(jnp.int32, shape, axis)


def rot(value, shift, axis=1):
    shift = shift % value.shape[axis]
    return pltpu.roll(value, shift, axis) if shift else value


def dot(a, b):
    return jnp.dot(a, b, preferred_element_type=F32)


def dot_nt(a, b):
    return lax.dot_general(a, b, NT, preferred_element_type=F32)


def ones_where(mask):
    return jnp.where(mask, 1.0, 0.0).astype(BF16)


def pieces(value, count):
    out = []
    for _ in range(count - 1):
        high = value.astype(BF16)
        out.append(high)
        value = value - high.astype(F32)
    out.append(value.astype(BF16))
    return out


def column(row):
    n = row.shape[1]
    diagonal = iota((n, n), 0) == iota((n, n), 1)
    return jnp.sum(jnp.where(diagonal, row, 0), axis=1, keepdims=True)


def pack_kernel(wave_ref, *refs):
    small_refs, out_ref, copy_refs, rows_ref = refs[:4], refs[4], refs[5:9], refs[9]
    for source_ref, copy_ref in zip(small_refs, copy_refs):
        copy_ref[...] = source_ref[...]
    time_ref, station_ref = small_refs[:2]
    start = time_ref[...] - HALF
    row = BLOCKS * station_ref[...] + start // LANES
    shift = start % LANES
    pad = jnp.zeros((1, LANES - row.shape[1]), F32)
    for c in range(CHANNELS):
        series = wave_ref[c].astype(F32)
        for s in range(STATIONS):
            for block in range(BLOCKS):
                at = c * SPAN + s * BLOCKS + block
                rows_ref[at : at + 1, :] = series[s : s + 1, block * LANES : (block + 1) * LANES]
    rows_ref[ROWS : ROWS + 1, :] = jnp.concatenate([row.astype(F32), pad], axis=1)
    rows_ref[ROWS + 1 : ROWS + 2, :] = jnp.concatenate([shift.astype(F32), pad], axis=1)
    rows_ref[ROWS + 2 : PACKED, :] = jnp.zeros((PACKED - ROWS - 2, LANES), F32)
    out_ref[0] = rows_ref[...].astype(BF16)


def join_kernel(near_ref, other_ref, *refs):
    out_ref = refs[-1]
    half = near_ref.shape[0]
    out_ref[0:half] = near_ref[...]
    out_ref[half:] = other_ref[...]


def rounds(ngx, ngy):
    masks = []
    for axis, size in (("gy", ngy), ("gx", ngx)):
        while size > 1:
            size //= 2
            masks.append((axis, size))
    return masks


def position(ngx, ngy, x, y):
    away = {"gx": x ^ lax.axis_index("gx"), "gy": y ^ lax.axis_index("gy")}
    return sum(((away[axis] // mask) & 1) << n for n, (axis, mask) in enumerate(rounds(ngx, ngy)))


def tile_kernel(ngx, ngy, templates_ref, station_ref, sorted_ref, scale_ref, owner_ref, tiles_ref, semaphore):
    copy = pltpu.make_async_copy(templates_ref, tiles_ref, semaphore)
    copy.start()
    tpl_dev, k_slots, row_len = tiles_ref.shape
    count = tpl_dev * k_slots
    total = sorted_ref.shape[0]
    station = station_ref[...].astype(F32).astype(BF16)
    home = ones_where(iota((count, tpl_dev), 0) // k_slots == iota((count, tpl_dev), 1))
    home_t = ones_where(iota((tpl_dev, count), 1) // k_slots == iota((tpl_dev, count), 0))
    by_row = dot_nt(home, station)
    by_col = dot(station, home_t)
    own_col = iota((count, k_slots), 0) % k_slots == iota((count, k_slots), 1)
    own_row = iota((k_slots, count), 1) % k_slots == iota((k_slots, count), 0)
    st_col = jnp.sum(jnp.where(own_col, by_row, 0.0), axis=1, keepdims=True)
    st_row = jnp.sum(jnp.where(own_row, by_col, 0.0), axis=0, keepdims=True)
    earlier = iota((count, count), 0) < iota((count, count), 1)
    rank = jnp.sum(jnp.where((st_col == st_row) & earlier, 1.0, 0.0), axis=0, keepdims=True)
    st = st_row.astype(jnp.int32)
    group = st // STATIONS
    place_of = position(ngx, ngy, group // ngy, group % ngy)
    slot = (place_of * STATIONS + st % STATIONS) * SLOTS + rank.astype(jnp.int32)
    copy.wait()
    tiles = tiles_ref[...].reshape(count, row_len)
    step = 128
    for first in range(0, total, step):
        place = ones_where(iota((step, count), 0) + first == slot)
        moved = dot(place, tiles)
        sorted_ref[first : first + step, :] = moved.astype(BF16)
        mean = jnp.sum(moved * moved, axis=1, keepdims=True) / row_len
        scale = lax.rsqrt(row_len * (mean + EPS))
        scale_ref[first : first + step, :] = jnp.broadcast_to(scale, (step, LANES))
        owner_ref[:, first : first + step] = dot_nt(home_t, place).astype(BF16)


def windows_kernel(data_ref, rows_ref, win_ref):
    groups = data_ref.shape[0]
    step = min(8, groups)
    column_of = iota((LANES, LANES), 1)
    sample = FINE * (COARSE - 1 - column_of % COARSE) + column_of // COARSE
    row = iota((LANES, LANES), 0)
    sums_of = ones_where(jnp.concatenate([row >= sample, row < sample, row >= 0], axis=1))
    major, chunk = iota((step, FINE, LANES), 1), iota((step, FINE, LANES), 2) // COARSE

    def body(q, carry):
        x = data_ref[pl.ds(q * step, step)].astype(F32)
        rows_ref[pl.ds(q * step, step)] = x
        energy = sum(x[:, SPAN * c : SPAN * (c + 1)] * x[:, SPAN * c : SPAN * (c + 1)] for c in range(CHANNELS))
        sums = sum(dot(part, sums_of) for part in pieces(energy.reshape(step * SPAN, LANES), 3))
        sums = sums.reshape(step, SPAN, 3 * LANES)
        for s in range(STATIONS):
            at = BLOCKS * s
            mean = sums[:, at : at + LAG_BLOCKS, 0:LANES]
            for j in range(1, TAPS):
                mean = mean + sums[:, at + j : at + j + LAG_BLOCKS, 2 * LANES :]
            mean = (mean + sums[:, at + TAPS : at + TAPS + LAG_BLOCKS, LANES : 2 * LANES]) / (
                CHANNELS * TAPS * LANES
            )
            value = lax.rsqrt(mean + EPS)
            for bit in range(3):
                size = 1 << bit
                up = (major // size) % 2
                other = (chunk // size) % 2
                later = rot(rot(value, -size, 1), size * COARSE, 2)
                earlier = rot(rot(value, size, 1), -size * COARSE, 2)
                value = jnp.where(up == other, value, jnp.where(up == 0, later, earlier))
            win_ref[pl.ds(q * step, step), s] = value
        return carry

    lax.fori_loop(0, groups // step, body, 0)


def build_data(rows_ref, g, s, c, out_ref):
    lane = iota((COARSE, LANES), 1)
    bound = FINE * (iota((COARSE, LANES), 0) + 1)
    now = None
    for block in range(BLOCKS):
        at = SPAN * c + BLOCKS * s + block
        row = rows_ref[g, pl.ds(at, FINE, stride=0), :]
        turned = [
            pltpu.roll(row, FINE * (1 + first), 1, stride=FINE, stride_axis=0) for first in range(0, COARSE, FINE)
        ]
        later = jnp.concatenate(turned, axis=0).astype(BF16)
        if block:
            out_ref[(block - 1) * COARSE : block * COARSE, c * LANES : (c + 1) * LANES] = jnp.where(
                lane < bound, now, later
            )
        now = later
    out_ref[(BLOCKS - 1) * COARSE : BLOCKS * COARSE, c * LANES : (c + 1) * LANES] = now


def build_taps(blocks_of, fine, height, out_ref, first, step):
    lane = iota((height, LANES), 1)
    zero = jnp.zeros((height, LANES), BF16)
    for b in range(fine):
        rows = slice(first + step * b, first + step * b + height)
        tail = zero
        at = 0
        for c, blocks in enumerate(blocks_of):
            before = zero
            for block in blocks:
                moved = rot(block, b)
                out_ref[rows, at : at + LANES] = jnp.where(lane < b, before, moved) if b else moved
                before = moved
                at += LANES
            if b:
                end = rot(blocks[-1], b + fine * c)
                tail = jnp.where((lane >= fine * c) & (lane < fine * c + b), end, tail)
        out_ref[rows, at : at + LANES] = tail


def taps_kernel(first, sorted_ref, after_ref, out_ref):
    height = FINE * STATIONS * SLOTS
    per_step = out_ref.shape[0] // height
    rows = STATIONS * SLOTS
    lane = iota((rows, LANES), 1)
    zero = jnp.zeros((rows, LANES), BF16)

    def body(i, carry):
        at = (first() * per_step + i) * rows
        tiles = sorted_ref[pl.ds(pl.multiple_of(at, rows), rows), :]
        out = out_ref.at[pl.ds(pl.multiple_of(i * height, height), height), :]
        for c in range(CHANNELS):
            blocks = [tiles[:, (TAPS * c + j) * LANES : (TAPS * c + j + 1) * LANES] for j in range(TAPS)]
            for b in range(FINE):
                before = zero
                for j in range(TAPS + 1):
                    moved = rot(blocks[j], b) if j < TAPS else zero
                    lanes = slice((c * (TAPS + 1) + j) * LANES, (c * (TAPS + 1) + j + 1) * LANES)
                    out[b * rows : (b + 1) * rows, lanes] = jnp.where(lane < b, before, moved) if b else moved
                    before = moved
        out[:, CHANNELS * (TAPS + 1) * LANES :] = jnp.zeros((height, LANES), BF16)
        return carry

    lax.fori_loop(0, per_step, body, 0)


def correlate_kernel(start, rows_ref, win_ref, taps_ref, scale_ref, high_ref, low_ref, *refs):
    x_refs = [[refs[4 * bank + 2 * n : 4 * bank + 2 * n + 2] for n in range(2)] for bank in range(2)]
    groups = rows_ref.shape[0]
    rows = STATIONS * SLOTS
    height = FINE * rows
    step = pl.program_id(0)
    parts = [(c, j) for c in range(CHANNELS) for j in range(TAPS + 1)]
    parts = parts + parts[:1]

    def builds(first, bank):
        for n in range(2):
            for s in range(STATIONS):
                for c in range(CHANNELS):
                    yield lambda n=n, s=s, c=c: build_data(rows_ref, first + n, s, c, x_refs[bank][n][s])

    @pl.when(step == 0)
    def _():
        for write in builds(0, 0):
            write()

    def store_lags(i, raw):
        g = step * 4 + i
        scale = scale_ref[pl.ds(pl.multiple_of((start + g) * rows, rows), rows), :]
        at = pl.ds(pl.multiple_of(g * rows, rows), rows)
        for b in range(FINE):
            value, window = [], []
            for s in range(STATIONS):
                first = b * rows + s * SLOTS
                value.append(raw[first : first + SLOTS, s * LANES : (s + 1) * LANES])
                window.append(win_ref[g, s, pl.ds(b, SLOTS, stride=0), :])
            value = jnp.concatenate(value, axis=0) * scale * jnp.concatenate(window, axis=0)
            high, low = pieces(value, 2)
            high_ref[at, b * LANES : (b + 1) * LANES] = high
            low_ref[at, b * LANES : (b + 1) * LANES] = low

    def multiply(accs, bank, writes):
        for t in range(PASSES):
            for n in range(2):
                data = [
                    jnp.concatenate(
                        [ref[j * COARSE : j * COARSE + LANES, c * LANES : (c + 1) * LANES] for c, j in parts[2 * t : 2 * t + 2]],
                        axis=1,
                    )
                    for ref in x_refs[bank][n]
                ]
                pltpu.matmul_push_rhs(jnp.concatenate(data, axis=0), t % 2, n, transpose=True)
                first = (2 * bank + n) * height
                taps = taps_ref[first : first + height, t * MXU : (t + 1) * MXU]
                pltpu.matmul_acc_lhs(accs[n], taps, load_staged_rhs=t % 2)
            for write in writes[t::PASSES]:
                write()

    def four_groups(*accs):
        multiply(accs[:2], 0, list(builds(step * 4 + 2, 1)))
        finish = [lambda n=n: store_lags(n, pltpu.matmul_pop(accs[n])) for n in range(2)]
        multiply(accs[2:], 1, list(builds(jnp.minimum(step * 4 + 4, groups - 2), 0)) + finish)
        for n in range(2):
            store_lags(2 + n, pltpu.matmul_pop(accs[2 + n]))

    pl.run_scoped(four_groups, *[pltpu.ACC(n % 2)((height, MXU), F32) for n in range(4)])


def stack_kernel(owner_ref, *refs):
    stack_ref = refs[-1]
    total, first = 0.0, 0
    for high_ref, low_ref in zip(refs[0:-1:2], refs[1:-1:2]):
        owner = owner_ref[:, first : first + high_ref.shape[0]]
        total = total + dot(owner, high_ref[...]) + dot(owner, low_ref[...])
        first += high_ref.shape[0]
    tpl_dev = stack_ref.shape[0]
    block_of = iota((tpl_dev, FINE * LANES), 1) % LANES // COARSE
    place = iota((FINE * LANES, LANES), 0)
    spread = iota((FINE * LANES, LANES), 1) == FINE * (COARSE - 1 - place % COARSE) + place // LANES
    spread = ones_where(spread)
    out = 0.0
    for part in pieces(total, 2):
        part = part.astype(F32)
        masked = [jnp.where(block_of == block, part, 0.0) for block in range(LAG_BLOCKS)]
        out = out + dot(jnp.concatenate(masked, axis=0).astype(BF16), spread)
    for block in range(LAG_BLOCKS):
        rows = out[block * tpl_dev : (block + 1) * tpl_dev]
        stack_ref[:, block * LANES : (block + 1) * LANES] = rows * (1.0 / 8.0**0.5)


def cut(data, row, shift, blocks):
    det_dev = row.shape[0]
    row_iota, lane = iota((det_dev, PACKED), 1), iota((det_dev, LANES), 1)
    picks = [row_iota == row + (SPAN * c + j) for c in range(CHANNELS) for j in range(blocks)]
    picks = jnp.concatenate([jnp.where(pick, 1.0, 0.0) for pick in picks], axis=0).astype(BF16)
    found = dot(picks, data).astype(BF16)
    found = [
        [found[(c * blocks + j) * det_dev : (c * blocks + j + 1) * det_dev] for j in range(blocks)]
        for c in range(CHANNELS)
    ]
    shift = jnp.broadcast_to(shift, (det_dev, LANES))
    for bit in range(7):
        size = 1 << bit
        moves = (shift & size) > 0
        found = [[jnp.where(moves, rot(block, -size), block) for block in row] for row in found]
    inside = lane < LANES - shift
    return [[jnp.where(inside, row[j], row[j + 1]) for j in range(blocks - 1)] for row in found]


def mean_square(blocks):
    total = 0.0
    for block, mask in blocks:
        block = block.astype(F32)
        square = block * block
        total = total + (square if mask is None else jnp.where(mask, square, 0.0))
    return jnp.sum(total, axis=1, keepdims=True) / (CHANNELS * W)


def own_windows(data, time_ref, station_ref):
    n = time_ref.shape[1]
    turned = iota((n, n), 0) ^ (DET_ROWS - 1) == iota((n, n), 1)
    start = jnp.sum(jnp.where(turned, time_ref[...], 0), axis=1, keepdims=True)
    station = jnp.sum(jnp.where(turned, station_ref[...], 0), axis=1, keepdims=True)
    mine = cut(data, station * BLOCKS + start // LANES, start % LANES, KEEP + 1)
    scale = lax.rsqrt(CHANNELS * W * (mean_square([(block, None) for blocks in mine for block in blocks]) + EPS))
    scale = jnp.sum(jnp.where(turned, scale, 0.0), axis=0, keepdims=True)
    return mine, column(scale)


def partner_windows(data, chosen_row):
    det_dev = chosen_row.shape[1]
    lane = iota((det_dev, LANES), 1)
    info = dot_nt(ones_where(lane == column(chosen_row)), data[PACKED - 16 : PACKED, :])
    pieces_of = cut(data, info[:, 8:9].astype(jnp.int32), info[:, 9:10].astype(jnp.int32), KEEP + 2)
    centre = []
    for first, middle, last in pieces_of:
        centre += [(first, lane >= HALF), (middle, None), (last, lane < HALF)]
    return pieces_of, lax.rsqrt(mean_square(centre) + EPS)


def differential(taps_ref, windows, x_ref, parts_ref):
    count = len(windows)
    height = count * DET_ROWS
    lane = iota((DET_ROWS, LANES), 1)
    wide = DET_FINE * DET_ROWS
    sub_lane = iota((8, LANES), 1) % DET_ROWS
    for q in range(taps_ref.shape[0]):
        rows = slice(q * DET_ROWS, (q + 1) * DET_ROWS)
        for d in range(count):
            source = [[block[rows] for block in blocks] for blocks in windows[d]]
            ends = {}
            for a in range(DET_COARSE):
                shift = DET_FINE * a
                out = slice((a * count + d) * DET_ROWS, (a * count + d + 1) * DET_ROWS)
                tail = None
                for c in range(CHANNELS):
                    moved = [rot(block, -shift) for block in source[c]]
                    ends[c, a] = moved[KEEP]
                    for j in range(KEEP):
                        block = jnp.where(lane < LANES - shift, moved[j], moved[j + 1]) if a else moved[j]
                        at = (c * KEEP + j) * LANES
                        x_ref[out, at : at + LANES] = block
                    end = ends[c, a - c] if a >= c else rot(source[c][KEEP], DET_FINE * c - shift)
                    tail = end if tail is None else jnp.where(lane < DET_FINE * c, tail, end)
                x_ref[out, DET_DEPTH - LANES : DET_DEPTH] = tail
        raw = dot_nt(x_ref[0 : DET_COARSE * height, :], taps_ref[q])
        for half in range(2):
            for row in range(0, height, 8):
                upper = row % DET_ROWS // 8
                total = jnp.zeros((8, LANES), F32)
                for a in range(DET_COARSE):
                    part = raw[a * height + row : a * height + row + 8, half * LANES : (half + 1) * LANES]
                    base = a + 1 if upper else a + LANES - DET_ROWS + 1
                    part = pltpu.roll(part, base, 1, stride=1, stride_axis=0)
                    total = jnp.where(sub_lane == 8 * upper + a, part, total)
                parts_ref[q * height + row : q * height + row + 8, half * LANES : (half + 1) * LANES] = total
    place, to = iota((wide, LANES), 0), iota((wide, LANES), 1)
    order = ones_where((to // DET_FINE == place % DET_COARSE) & (to % DET_FINE == place // DET_ROWS))
    return sum(dot(part, order) for part in pieces(parts_ref[...], 2))


def own_kernel(data_ref, time_ref, station_ref, after_ref, taps_ref, scale_ref):
    mine, scale = own_windows(data_ref[0], time_ref, station_ref)
    scale_ref[...] = jnp.broadcast_to(scale, scale_ref.shape)
    for q in range(taps_ref.shape[0]):
        rows = slice(q * DET_ROWS, (q + 1) * DET_ROWS)
        blocks = [[block[rows] for block in channel] for channel in mine]
        build_taps(blocks, DET_FINE, DET_ROWS, taps_ref.at[q], 0, DET_ROWS)


def cuts_kernel(ngx, ngy, near_ref, far_ref, scale_ref, partner_ref, windows_ref, scales_ref):
    gx, gy = lax.axis_index("gx"), lax.axis_index("gy")
    for d, (dx, dy) in enumerate(((1, 0), (-1, 0), (0, 1), (0, -1))):
        x, y = gx + dx, gy + dy
        valid = (x >= 0) & (x < ngx) & (y >= 0) & (y < ngy)
        at = position(ngx, ngy, jnp.clip(x, 0, ngx - 1), jnp.clip(y, 0, ngy - 1)) % near_ref.shape[0]
        data = (far_ref if dx else near_ref)[at]
        found, scale = partner_windows(data, partner_ref[d : d + 1, :])
        for c in range(CHANNELS):
            for j in range(KEEP + 1):
                windows_ref[d, c, j] = found[c][j]
        scales_ref[d] = jnp.where(valid, scale_ref[...] * scale, 0.0)


def detect_kernel(taps_ref, windows_ref, scales_ref, diff_ref, x_ref, parts_ref):
    windows = [[[windows_ref[d, c, j] for j in range(KEEP + 1)] for c in range(CHANNELS)] for d in range(4)]
    out = differential(taps_ref, windows, x_ref, parts_ref)
    for q in range(taps_ref.shape[0]):
        for d in range(4):
            at = (q * 4 + d) * DET_ROWS
            rows = slice(q * DET_ROWS, (q + 1) * DET_ROWS)
            diff_ref[pl.ds(q * DET_ROWS * 4 + d, DET_ROWS, stride=4), :] = (
                out[at : at + DET_ROWS] * scales_ref[d, rows, :]
            )


def on_device(ngx, ngy, waveforms, templates, tpl_stations, det_station, det_time, partner):
    tpl_dev, k_slots, row_len = templates.shape
    det_dev = det_station.shape[0]
    groups = ngx * ngy
    half = groups // 2
    rows = STATIONS * SLOTS
    total = groups * rows
    time_row, station_row = det_time.reshape(1, det_dev), det_station.reshape(1, det_dev)
    small = (time_row, station_row, partner.T, tpl_stations.T)
    packed, time_row, station_row, partners, tile_stations = pl.pallas_call(
        pack_kernel,
        out_shape=(jax.ShapeDtypeStruct((1, PACKED, LANES), BF16),)
        + tuple(pltpu.VMEM(value.shape, value.dtype) for value in small),
        scratch_shapes=[pltpu.VMEM((PACKED, LANES), F32)],
        name="pack",
    )(waveforms.transpose(1, 0, 2), *small)

    def swap(value, axis, mask):
        size = {"gx": ngx, "gy": ngy}[axis]
        return lax.ppermute(value, axis, [(n, n ^ mask) for n in range(size)])

    vmem, after = pl.BlockSpec(memory_space=pltpu.VMEM), pl.BlockSpec(memory_space=pl.ANY)
    tiles, scale, owner = pl.pallas_call(
        functools.partial(tile_kernel, ngx, ngy),
        out_shape=(
            jax.ShapeDtypeStruct((total, row_len), BF16),
            jax.ShapeDtypeStruct((total, LANES), F32),
            jax.ShapeDtypeStruct((tpl_dev, total), BF16),
        ),
        in_specs=[after, vmem],
        scratch_shapes=[pltpu.VMEM(templates.shape, BF16), pltpu.SemaphoreType.DMA],
        compiler_params=pltpu.CompilerParams(vmem_limit_bytes=24 << 20),
        name="tiles",
    )(pltpu.with_memory_space_constraint(templates, pltpu.HBM), tile_stations)
    steps = groups // 4
    height = 4 * FINE * rows
    depth = MXU * PASSES
    def shifted(call, near):
        shape = (steps // 2 * height, depth)
        limit = pltpu.CompilerParams(vmem_limit_bytes=(8 << 20) + total * row_len * 4)
        if groups <= 32:
            taps = pl.pallas_call(
                functools.partial(taps_kernel, lambda: call),
                in_specs=[vmem, after],
                out_specs=vmem,
                out_shape=pltpu.VMEM(shape, BF16),
                compiler_params=limit,
                name="taps",
            )(tiles, near)
            return pltpu.with_memory_space_constraint(taps, pltpu.VMEM)
        taps = pl.pallas_call(
            functools.partial(taps_kernel, lambda: pl.program_id(0)),
            grid=(steps // 2,),
            in_specs=[pl.BlockSpec((total // 2, row_len), lambda i: (call, 0)), after],
            out_specs=pl.BlockSpec((height, depth), lambda i: (i, 0)),
            out_shape=pltpu.HBM(shape, BF16),
            compiler_params=limit,
            name="taps",
        )(tiles, near)
        return pltpu.with_memory_space_constraint(taps, pltpu.HBM)

    parts = det_dev // DET_ROWS

    def own_detections(near):
        return pl.pallas_call(
            own_kernel,
            out_shape=(
                jax.ShapeDtypeStruct((parts, DET_FINE * DET_ROWS, DET_DEPTH), BF16),
                jax.ShapeDtypeStruct((det_dev, LANES), F32),
            ),
            in_specs=[vmem, vmem, vmem, after],
            compiler_params=pltpu.CompilerParams(vmem_limit_bytes=16 << 20),
            name="own",
        )(packed, time_row, station_row, near)

    def whole(*shape):
        return pl.BlockSpec(shape, lambda i: (0,) * len(shape))

    params = pltpu.CompilerParams(vmem_limit_bytes=(16 << 20) + groups * (1 << 17))

    def correlate(data, taps, start):
        count = data.shape[0]
        sums = (count * rows, FINE * LANES)
        first = start % half // 4
        series, win = pl.pallas_call(
            windows_kernel,
            out_shape=(
                jax.ShapeDtypeStruct((count, PACKED, LANES), F32),
                jax.ShapeDtypeStruct((count, STATIONS, FINE, LANES), F32),
            ),
            compiler_params=params,
            name="windows",
        )(data)
        return pl.pallas_call(
            functools.partial(correlate_kernel, start),
            grid=(count // 4,),
            in_specs=[
                whole(*series.shape),
                whole(*win.shape),
                pl.BlockSpec((height, depth), lambda i: (first + i, 0)),
                whole(*scale.shape),
            ],
            out_specs=(whole(*sums), whole(*sums)),
            out_shape=(jax.ShapeDtypeStruct(sums, BF16),) * 2,
            scratch_shapes=[pltpu.VMEM((BLOCKS * COARSE, CHANNELS * LANES), BF16)] * 8,
            compiler_params=params,
            name="correlate",
        )(series, win, taps, scale)

    near, taps = packed, []
    *first, last = rounds(ngx, ngy)
    for n, (axis, mask) in enumerate(first):
        other = swap(near, axis, mask)
        beside = near
        if n == 0:
            beside = scale
        elif n <= 2:
            taps.append(shifted(n - 1, near))
            beside = taps[-1]
        elif n == len(first) - 1:
            mine, mine_scale = own_detections(near)
            sums = [*correlate(near, taps[0], 0)]
            beside = sums[0]
        near = pl.pallas_call(
            join_kernel,
            out_shape=jax.ShapeDtypeStruct((2 * near.shape[0], PACKED, LANES), BF16),
            in_specs=[vmem, vmem, after, after],
            compiler_params=pltpu.CompilerParams(vmem_limit_bytes=16 << 20),
            name="join",
        )(near, other, beside, mine_scale if n == len(first) - 1 else beside)
    far = swap(near, *last)

    sums += [*correlate(other, taps[0], half // 2), *correlate(far, taps[1], half)]
    stack = pl.pallas_call(
        stack_kernel,
        out_shape=jax.ShapeDtypeStruct((tpl_dev, LAG_BLOCKS * LANES), F32),
        compiler_params=params,
        name="stack",
    )(owner, *sums)
    cuts = pl.pallas_call(
        functools.partial(cuts_kernel, ngx, ngy),
        out_shape=(
            jax.ShapeDtypeStruct((4, CHANNELS, KEEP + 1, det_dev, LANES), BF16),
            jax.ShapeDtypeStruct((4, det_dev, LANES), F32),
        ),
        compiler_params=params,
        name="cuts",
    )(near, far, mine_scale, partners)
    diff = pl.pallas_call(
        detect_kernel,
        out_shape=jax.ShapeDtypeStruct((4 * det_dev, DTLAG), F32),
        scratch_shapes=[
            pltpu.VMEM((4 * DET_COARSE * DET_ROWS, DET_DEPTH), BF16),
            pltpu.VMEM((4 * det_dev, DET_FINE * DET_ROWS), F32),
        ],
        compiler_params=params,
        name="detect",
    )(mine, *cuts)
    return stack, diff.reshape(det_dev, 4, DTLAG)


def solution(mesh):
    return jax.shard_map(
        functools.partial(on_device, mesh.shape["gx"], mesh.shape["gy"]),
        mesh=mesh,
        in_specs=(
            P(("gx", "gy"), None, None),
            P(("gx", "gy"), None, None),
            P(("gx", "gy"), None),
            P(("gx", "gy")),
            P(("gx", "gy")),
            P(("gx", "gy"), None),
        ),
        out_specs=(P(("gx", "gy"), None), P(("gx", "gy"), None, None)),
        check_vma=False,
    )
```

```python
import functools

import jax
import jax.numpy as jnp
from jax import lax
from jax.experimental import pallas as pl
from jax.experimental.pallas import tpu as pltpu
from jax.sharding import PartitionSpec as P

LANES = 128
CHANNELS = 3
STATIONS = 2
BLOCKS = 12
TAPS = 4
LAG_BLOCKS = BLOCKS - TAPS
SLOTS = 8
FINE = 8
COARSE = LANES // FINE
DET_FINE = 16
DET_COARSE = LANES // DET_FINE
DET_ROWS = 16
W = 256
DTLAG = 128
HALF = DTLAG // 2
KEEP = W // LANES
DET_DEPTH = CHANNELS * KEEP * LANES + LANES
SPAN = STATIONS * BLOCKS
ROWS = CHANNELS * SPAN
PACKED = ROWS + 8
MXU = 256
PARTS = [(0, j) for j in range(TAPS + 1)] + [(c, j) for c in (1, 2) for j in range(TAPS)] + [(CHANNELS, 0)]
PASSES = len(PARTS) // 2
EPS = 1e-06
F32 = jnp.float32
BF16 = jnp.bfloat16
NT = (((1,), (1,)), ((), ()))


def iota(shape, axis):
    return lax.broadcasted_iota(jnp.int32, shape, axis)


def rot(value, shift, axis=1):
    shift = shift % value.shape[axis]
    return pltpu.roll(value, shift, axis) if shift else value


def dot(a, b):
    return jnp.dot(a, b, preferred_element_type=F32)


def dot_nt(a, b):
    return lax.dot_general(a, b, NT, preferred_element_type=F32)


def ones_where(mask):
    return jnp.where(mask, 1.0, 0.0).astype(BF16)


def pieces(value, count):
    out = []
    for _ in range(count - 1):
        high = value.astype(BF16)
        out.append(high)
        value = value - high.astype(F32)
    out.append(value.astype(BF16))
    return out


def column(row):
    n = row.shape[1]
    diagonal = iota((n, n), 0) == iota((n, n), 1)
    return jnp.sum(jnp.where(diagonal, row, 0), axis=1, keepdims=True)


def pack_kernel(wave_ref, *refs):
    small_refs, out_ref, copy_refs, rows_ref = refs[:4], refs[4], refs[5:9], refs[9]
    for source_ref, copy_ref in zip(small_refs, copy_refs):
        copy_ref[...] = source_ref[...]
    time_ref, station_ref = small_refs[:2]
    start = time_ref[...] - HALF
    row = BLOCKS * station_ref[...] + start // LANES
    shift = start % LANES
    pad = jnp.zeros((1, LANES - row.shape[1]), F32)
    for c in range(CHANNELS):
        series = wave_ref[c].astype(F32)
        for s in range(STATIONS):
            for block in range(BLOCKS):
                at = c * SPAN + s * BLOCKS + block
                rows_ref[at : at + 1, :] = series[s : s + 1, block * LANES : (block + 1) * LANES]
    rows_ref[ROWS : ROWS + 1, :] = jnp.concatenate([row.astype(F32), pad], axis=1)
    rows_ref[ROWS + 1 : ROWS + 2, :] = jnp.concatenate([shift.astype(F32), pad], axis=1)
    rows_ref[ROWS + 2 : PACKED, :] = jnp.zeros((PACKED - ROWS - 2, LANES), F32)
    out_ref[0] = rows_ref[...].astype(BF16)


def join_kernel(near_ref, other_ref, *refs):
    out_ref = refs[-1]
    half = near_ref.shape[0]
    out_ref[0:half] = near_ref[...]
    out_ref[half:] = other_ref[...]


def rounds(ngx, ngy):
    masks = []
    for axis, size in (("gy", ngy), ("gx", ngx)):
        while size > 1:
            size //= 2
            masks.append((axis, size))
    return masks


def position(ngx, ngy, x, y):
    away = {"gx": x ^ lax.axis_index("gx"), "gy": y ^ lax.axis_index("gy")}
    return sum(((away[axis] // mask) & 1) << n for n, (axis, mask) in enumerate(rounds(ngx, ngy)))


def tile_kernel(ngx, ngy, templates_ref, station_ref, sorted_ref, scale_ref, owner_ref, tiles_ref, semaphore):
    copy = pltpu.make_async_copy(templates_ref, tiles_ref, semaphore)
    copy.start()
    tpl_dev, k_slots, row_len = tiles_ref.shape
    count = tpl_dev * k_slots
    total = sorted_ref.shape[0]
    station = station_ref[...].astype(F32).astype(BF16)
    home = ones_where(iota((count, tpl_dev), 0) // k_slots == iota((count, tpl_dev), 1))
    home_t = ones_where(iota((tpl_dev, count), 1) // k_slots == iota((tpl_dev, count), 0))
    by_row = dot_nt(home, station)
    by_col = dot(station, home_t)
    own_col = iota((count, k_slots), 0) % k_slots == iota((count, k_slots), 1)
    own_row = iota((k_slots, count), 1) % k_slots == iota((k_slots, count), 0)
    st_col = jnp.sum(jnp.where(own_col, by_row, 0.0), axis=1, keepdims=True)
    st_row = jnp.sum(jnp.where(own_row, by_col, 0.0), axis=0, keepdims=True)
    earlier = iota((count, count), 0) < iota((count, count), 1)
    rank = jnp.sum(jnp.where((st_col == st_row) & earlier, 1.0, 0.0), axis=0, keepdims=True)
    st = st_row.astype(jnp.int32)
    group = st // STATIONS
    place_of = position(ngx, ngy, group // ngy, group % ngy)
    slot = (place_of * STATIONS + st % STATIONS) * SLOTS + rank.astype(jnp.int32)
    copy.wait()
    tiles = tiles_ref[...].reshape(count, row_len)
    step = 128
    for first in range(0, total, step):
        place = ones_where(iota((step, count), 0) + first == slot)
        moved = dot(place, tiles)
        sorted_ref[first : first + step, :] = moved.astype(BF16)
        mean = jnp.sum(moved * moved, axis=1, keepdims=True) / row_len
        scale = lax.rsqrt(row_len * (mean + EPS))
        scale_ref[first : first + step, :] = jnp.broadcast_to(scale, (step, LANES))
        owner_ref[:, first : first + step] = dot_nt(home_t, place).astype(BF16)


def windows_kernel(data_ref, rows_ref, win_ref):
    groups = data_ref.shape[0]
    step = min(8, groups)
    column_of = iota((LANES, LANES), 1)
    sample = FINE * (COARSE - 1 - column_of % COARSE) + column_of // COARSE
    row = iota((LANES, LANES), 0)
    sums_of = ones_where(jnp.concatenate([row >= sample, row < sample, row >= 0], axis=1))
    major, chunk = iota((step, FINE, LANES), 1), iota((step, FINE, LANES), 2) // COARSE

    def body(q, carry):
        x = data_ref[pl.ds(q * step, step)].astype(F32)
        rows_ref[pl.ds(q * step, step)] = x
        energy = sum(x[:, SPAN * c : SPAN * (c + 1)] * x[:, SPAN * c : SPAN * (c + 1)] for c in range(CHANNELS))
        sums = sum(dot(part, sums_of) for part in pieces(energy.reshape(step * SPAN, LANES), 3))
        sums = sums.reshape(step, SPAN, 3 * LANES)
        for s in range(STATIONS):
            at = BLOCKS * s
            mean = sums[:, at : at + LAG_BLOCKS, 0:LANES]
            for j in range(1, TAPS):
                mean = mean + sums[:, at + j : at + j + LAG_BLOCKS, 2 * LANES :]
            mean = (mean + sums[:, at + TAPS : at + TAPS + LAG_BLOCKS, LANES : 2 * LANES]) / (
                CHANNELS * TAPS * LANES
            )
            value = lax.rsqrt(mean + EPS)
            for bit in range(3):
                size = 1 << bit
                up = (major // size) % 2
                other = (chunk // size) % 2
                later = rot(rot(value, -size, 1), size * COARSE, 2)
                earlier = rot(rot(value, size, 1), -size * COARSE, 2)
                value = jnp.where(up == other, value, jnp.where(up == 0, later, earlier))
            win_ref[pl.ds(q * step, step), s] = value
        return carry

    lax.fori_loop(0, groups // step, body, 0)


def build_data(rows_ref, g, s, c, out_ref):
    lane = iota((COARSE, LANES), 1)
    bound = FINE * (iota((COARSE, LANES), 0) + 1)
    now = None
    for block in range(BLOCKS):
        at = SPAN * c + BLOCKS * s + block
        row = rows_ref[g, pl.ds(at, FINE, stride=0), :]
        turned = [
            pltpu.roll(row, FINE * (1 + first), 1, stride=FINE, stride_axis=0) for first in range(0, COARSE, FINE)
        ]
        later = jnp.concatenate(turned, axis=0).astype(BF16)
        if block:
            out_ref[(block - 1) * COARSE : block * COARSE, c * LANES : (c + 1) * LANES] = jnp.where(
                lane < bound, now, later
            )
        now = later
        rows = slice((block - TAPS) * COARSE, (block - TAPS + 1) * COARSE)
        if c == 1 and block >= TAPS:
            out_ref[rows, CHANNELS * LANES :] = later
        if c == 2 and block >= TAPS:
            end = [pltpu.roll(row, FINE * first, 1, stride=FINE, stride_axis=0) for first in range(0, COARSE, FINE)]
            end = jnp.concatenate(end, axis=0).astype(BF16)
            out_ref[rows, CHANNELS * LANES :] = jnp.where(lane < LANES // 2, out_ref[rows, CHANNELS * LANES :], end)
    out_ref[(BLOCKS - 1) * COARSE : BLOCKS * COARSE, c * LANES : (c + 1) * LANES] = now


def build_taps(blocks_of, fine, height, out_ref, first, step):
    lane = iota((height, LANES), 1)
    zero = jnp.zeros((height, LANES), BF16)
    for b in range(fine):
        rows = slice(first + step * b, first + step * b + height)
        tail = zero
        at = 0
        for c, blocks in enumerate(blocks_of):
            before = zero
            for block in blocks:
                moved = rot(block, b)
                out_ref[rows, at : at + LANES] = jnp.where(lane < b, before, moved) if b else moved
                before = moved
                at += LANES
            if b:
                end = rot(blocks[-1], b + fine * c)
                tail = jnp.where((lane >= fine * c) & (lane < fine * c + b), end, tail)
        out_ref[rows, at : at + LANES] = tail


def taps_kernel(first, sorted_ref, after_ref, out_ref):
    height = FINE * STATIONS * SLOTS
    per_step = out_ref.shape[0] // height
    rows = STATIONS * SLOTS
    lane = iota((rows, LANES), 1)
    zero = jnp.zeros((rows, LANES), BF16)

    def body(i, carry):
        at = (first() * per_step + i) * rows
        tiles = sorted_ref[pl.ds(pl.multiple_of(at, rows), rows), :]
        out = out_ref.at[pl.ds(pl.multiple_of(i * height, height), height), :]
        for b in range(FINE):
            place = slice(b * rows, (b + 1) * rows)
            past = []
            block = 0
            for c in range(CHANNELS):
                before = zero
                for j in range(TAPS):
                    tile = tiles[:, (TAPS * c + j) * LANES : (TAPS * c + j + 1) * LANES]
                    moved = rot(tile, b)
                    lanes = slice(block * LANES, (block + 1) * LANES)
                    out[place, lanes] = jnp.where(lane < b, before, moved) if b else moved
                    before = moved
                    block += 1
                past.append(jnp.where(lane < b, before, zero) if b else zero)
                if c == 0:
                    out[place, block * LANES : (block + 1) * LANES] = past[0]
                    block += 1
            if b:
                end = rot(tile, b - FINE)
                past[1] = jnp.where((lane >= LANES - FINE) & (lane < LANES - FINE + b), end, past[1])
            out[place, block * LANES : (block + 1) * LANES] = past[1]
        return carry

    lax.fori_loop(0, per_step, body, 0)


def correlate_kernel(start, rows_ref, win_ref, taps_ref, scale_ref, high_ref, low_ref, *refs):
    x_refs = [[refs[4 * bank + 2 * n : 4 * bank + 2 * n + 2] for n in range(2)] for bank in range(2)]
    groups = rows_ref.shape[0]
    rows = STATIONS * SLOTS
    height = FINE * rows
    step = pl.program_id(0)

    def builds(first, bank):
        for n in range(2):
            for s in range(STATIONS):
                for c in range(CHANNELS):
                    yield lambda n=n, s=s, c=c: build_data(rows_ref, first + n, s, c, x_refs[bank][n][s])

    @pl.when(step == 0)
    def _():
        for write in builds(0, 0):
            write()

    def store_lags(i, raw):
        g = step * 4 + i
        scale = scale_ref[pl.ds(pl.multiple_of((start + g) * rows, rows), rows), :]
        at = pl.ds(pl.multiple_of(g * rows, rows), rows)
        for b in range(FINE):
            value, window = [], []
            for s in range(STATIONS):
                first = b * rows + s * SLOTS
                value.append(raw[first : first + SLOTS, s * LANES : (s + 1) * LANES])
                window.append(win_ref[g, s, pl.ds(b, SLOTS, stride=0), :])
            value = jnp.concatenate(value, axis=0) * scale * jnp.concatenate(window, axis=0)
            high, low = pieces(value, 2)
            high_ref[at, b * LANES : (b + 1) * LANES] = high
            low_ref[at, b * LANES : (b + 1) * LANES] = low

    def multiply(accs, bank, writes):
        for t in range(PASSES):
            for n in range(2):
                data = [
                    jnp.concatenate(
                        [ref[j * COARSE : j * COARSE + LANES, c * LANES : (c + 1) * LANES] for c, j in PARTS[2 * t : 2 * t + 2]],
                        axis=1,
                    )
                    for ref in x_refs[bank][n]
                ]
                pltpu.matmul_push_rhs(jnp.concatenate(data, axis=0), t % 2, n, transpose=True)
                first = (2 * bank + n) * height
                taps = taps_ref[first : first + height, t * MXU : (t + 1) * MXU]
                pltpu.matmul_acc_lhs(accs[n], taps, load_staged_rhs=t % 2)
            for write in writes[t::PASSES]:
                write()

    def four_groups(*accs):
        multiply(accs[:2], 0, list(builds(step * 4 + 2, 1)))
        finish = [lambda n=n: store_lags(n, pltpu.matmul_pop(accs[n])) for n in range(2)]
        multiply(accs[2:], 1, list(builds(jnp.minimum(step * 4 + 4, groups - 2), 0)) + finish)
        for n in range(2):
            store_lags(2 + n, pltpu.matmul_pop(accs[2 + n]))

    pl.run_scoped(four_groups, *[pltpu.ACC(n % 2)((height, MXU), F32) for n in range(4)])


def stack_kernel(owner_ref, *refs):
    stack_ref = refs[-1]
    total, first = 0.0, 0
    for high_ref, low_ref in zip(refs[0:-1:2], refs[1:-1:2]):
        owner = owner_ref[:, first : first + high_ref.shape[0]]
        total = total + dot(owner, high_ref[...]) + dot(owner, low_ref[...])
        first += high_ref.shape[0]
    tpl_dev = stack_ref.shape[0]
    block_of = iota((tpl_dev, FINE * LANES), 1) % LANES // COARSE
    place = iota((FINE * LANES, LANES), 0)
    spread = iota((FINE * LANES, LANES), 1) == FINE * (COARSE - 1 - place % COARSE) + place // LANES
    spread = ones_where(spread)
    out = 0.0
    for part in pieces(total, 2):
        part = part.astype(F32)
        masked = [jnp.where(block_of == block, part, 0.0) for block in range(LAG_BLOCKS)]
        out = out + dot(jnp.concatenate(masked, axis=0).astype(BF16), spread)
    for block in range(LAG_BLOCKS):
        rows = out[block * tpl_dev : (block + 1) * tpl_dev]
        stack_ref[:, block * LANES : (block + 1) * LANES] = rows * (1.0 / 8.0**0.5)


def cut(data, row, shift, blocks):
    det_dev = row.shape[0]
    row_iota, lane = iota((det_dev, PACKED), 1), iota((det_dev, LANES), 1)
    away = row_iota - row
    picks = [away == SPAN * c + j for c in range(CHANNELS) for j in range(blocks)]
    picks = jnp.concatenate([jnp.where(pick, 1.0, 0.0) for pick in picks], axis=0).astype(BF16)
    found = dot(picks, data).astype(BF16)
    found = [
        [found[(c * blocks + j) * det_dev : (c * blocks + j + 1) * det_dev] for j in range(blocks)]
        for c in range(CHANNELS)
    ]
    shift = jnp.broadcast_to(shift, (det_dev, LANES))
    for bit in range(7):
        size = 1 << bit
        moves = (shift & size) > 0
        found = [[jnp.where(moves, rot(block, -size), block) for block in row] for row in found]
    inside = lane < LANES - shift
    return [[jnp.where(inside, row[j], row[j + 1]) for j in range(blocks - 1)] for row in found]


def mean_square(blocks):
    total = 0.0
    for block, mask in blocks:
        block = block.astype(F32)
        square = block * block
        total = total + (square if mask is None else jnp.where(mask, square, 0.0))
    return jnp.sum(total, axis=1, keepdims=True) / (CHANNELS * W)


def own_windows(data, time_ref, station_ref):
    n = time_ref.shape[1]
    turned = iota((n, n), 0) ^ (DET_ROWS - 1) == iota((n, n), 1)
    start = jnp.sum(jnp.where(turned, time_ref[...], 0), axis=1, keepdims=True)
    station = jnp.sum(jnp.where(turned, station_ref[...], 0), axis=1, keepdims=True)
    mine = cut(data, station * BLOCKS + start // LANES, start % LANES, KEEP + 1)
    scale = lax.rsqrt(CHANNELS * W * (mean_square([(block, None) for blocks in mine for block in blocks]) + EPS))
    scale = jnp.sum(jnp.where(turned, scale, 0.0), axis=0, keepdims=True)
    return mine, column(scale)


def partner_windows(data, chosen_row):
    det_dev = chosen_row.shape[1]
    lane = iota((det_dev, LANES), 1)
    info = dot_nt(ones_where(lane == column(chosen_row)), data[PACKED - 16 : PACKED, :])
    pieces_of = cut(data, info[:, 8:9].astype(jnp.int32), info[:, 9:10].astype(jnp.int32), KEEP + 2)
    centre = []
    for first, middle, last in pieces_of:
        centre += [(first, lane >= HALF), (middle, None), (last, lane < HALF)]
    return pieces_of, lax.rsqrt(mean_square(centre) + EPS)


def differential(taps_ref, windows, x_ref, raw_ref, parts_ref):
    count = len(windows)
    height = count * DET_ROWS
    lane = iota((DET_ROWS, LANES), 1)
    wide = DET_FINE * DET_ROWS
    sub_lane = iota((8, LANES), 1) % DET_ROWS
    for q in range(taps_ref.shape[0]):
        rows = slice(q * DET_ROWS, (q + 1) * DET_ROWS)
        for d in range(count):
            source = [[block[rows] for block in blocks] for blocks in windows[d]]
            ends = {}
            for a in range(DET_COARSE):
                shift = DET_FINE * a
                out = slice((a * count + d) * DET_ROWS, (a * count + d + 1) * DET_ROWS)
                tail = None
                for c in range(CHANNELS):
                    moved = [rot(block, -shift) for block in source[c]]
                    ends[c, a] = moved[KEEP]
                    for j in range(KEEP):
                        block = jnp.where(lane < LANES - shift, moved[j], moved[j + 1]) if a else moved[j]
                        at = (c * KEEP + j) * LANES
                        x_ref[q % 2, out, at : at + LANES] = block
                    end = ends[c, a - c] if a >= c else rot(source[c][KEEP], DET_FINE * c - shift)
                    tail = end if tail is None else jnp.where(lane < DET_FINE * c, tail, end)
                x_ref[q % 2, out, DET_DEPTH - LANES : DET_DEPTH] = tail
        raw_ref[q] = dot_nt(x_ref[q % 2], taps_ref[q])
    for q in range(taps_ref.shape[0]):
        for half in range(2):
            for row in range(0, height, 8):
                upper = row % DET_ROWS // 8
                total = jnp.zeros((8, LANES), F32)
                for a in range(DET_COARSE):
                    part = raw_ref[q, a * height + row : a * height + row + 8, half * LANES : (half + 1) * LANES]
                    base = a + 1 if upper else a + LANES - DET_ROWS + 1
                    part = pltpu.roll(part, base, 1, stride=1, stride_axis=0)
                    total = jnp.where(sub_lane == 8 * upper + a, part, total)
                parts_ref[q * height + row : q * height + row + 8, half * LANES : (half + 1) * LANES] = total
    place, to = iota((wide, LANES), 0), iota((wide, LANES), 1)
    order = ones_where((to // DET_FINE == place % DET_COARSE) & (to % DET_FINE == place // DET_ROWS))
    return sum(dot(part, order) for part in pieces(parts_ref[...], 2))


def own_kernel(data_ref, time_ref, station_ref, after_ref, taps_ref, scale_ref):
    mine, scale = own_windows(data_ref[0], time_ref, station_ref)
    scale_ref[...] = jnp.broadcast_to(scale, scale_ref.shape)
    for q in range(taps_ref.shape[0]):
        rows = slice(q * DET_ROWS, (q + 1) * DET_ROWS)
        blocks = [[block[rows] for block in channel] for channel in mine]
        build_taps(blocks, DET_FINE, DET_ROWS, taps_ref.at[q], 0, DET_ROWS)


def cuts_kernel(ngx, ngy, near_ref, far_ref, scale_ref, partner_ref, windows_ref, scales_ref):
    gx, gy = lax.axis_index("gx"), lax.axis_index("gy")
    for d, (dx, dy) in enumerate(((1, 0), (-1, 0), (0, 1), (0, -1))):
        x, y = gx + dx, gy + dy
        valid = (x >= 0) & (x < ngx) & (y >= 0) & (y < ngy)
        at = position(ngx, ngy, jnp.clip(x, 0, ngx - 1), jnp.clip(y, 0, ngy - 1)) % near_ref.shape[0]
        data = (far_ref if dx else near_ref)[at]
        found, scale = partner_windows(data, partner_ref[d : d + 1, :])
        for c in range(CHANNELS):
            for j in range(KEEP + 1):
                windows_ref[d, c, j] = found[c][j]
        scales_ref[d] = jnp.where(valid, scale_ref[...] * scale, 0.0)


def detect_kernel(taps_ref, windows_ref, scales_ref, diff_ref, x_ref, raw_ref, parts_ref):
    windows = [[[windows_ref[d, c, j] for j in range(KEEP + 1)] for c in range(CHANNELS)] for d in range(4)]
    out = differential(taps_ref, windows, x_ref, raw_ref, parts_ref)
    for q in range(taps_ref.shape[0]):
        for d in range(4):
            at = (q * 4 + d) * DET_ROWS
            rows = slice(q * DET_ROWS, (q + 1) * DET_ROWS)
            diff_ref[pl.ds(q * DET_ROWS * 4 + d, DET_ROWS, stride=4), :] = (
                out[at : at + DET_ROWS] * scales_ref[d, rows, :]
            )


def on_device(ngx, ngy, waveforms, templates, tpl_stations, det_station, det_time, partner):
    tpl_dev, k_slots, row_len = templates.shape
    det_dev = det_station.shape[0]
    groups = ngx * ngy
    half = groups // 2
    rows = STATIONS * SLOTS
    total = groups * rows
    time_row, station_row = det_time.reshape(1, det_dev), det_station.reshape(1, det_dev)
    small = (time_row, station_row, partner.T, tpl_stations.T)
    packed, time_row, station_row, partners, tile_stations = pl.pallas_call(
        pack_kernel,
        out_shape=(pltpu.VMEM((1, PACKED, LANES), BF16),)
        + tuple(pltpu.VMEM(value.shape, value.dtype) for value in small),
        scratch_shapes=[pltpu.VMEM((PACKED, LANES), F32)],
        name="pack",
    )(waveforms.transpose(1, 0, 2), *small)

    def swap(value, axis, mask):
        size = {"gx": ngx, "gy": ngy}[axis]
        return lax.ppermute(value, axis, [(n, n ^ mask) for n in range(size)])

    vmem, after = pl.BlockSpec(memory_space=pltpu.VMEM), pl.BlockSpec(memory_space=pl.ANY)
    tiles, scale, owner = pl.pallas_call(
        functools.partial(tile_kernel, ngx, ngy),
        out_shape=(
            jax.ShapeDtypeStruct((total, row_len), BF16),
            jax.ShapeDtypeStruct((total, LANES), F32),
            jax.ShapeDtypeStruct((tpl_dev, total), BF16),
        ),
        in_specs=[after, vmem],
        scratch_shapes=[pltpu.VMEM(templates.shape, BF16), pltpu.SemaphoreType.DMA],
        compiler_params=pltpu.CompilerParams(vmem_limit_bytes=24 << 20),
        name="tiles",
    )(pltpu.with_memory_space_constraint(templates, pltpu.HBM), tile_stations)
    steps = groups // 4
    height = 4 * FINE * rows
    depth = MXU * PASSES
    def shifted(call, near):
        shape = (steps // 2 * height, depth)
        limit = pltpu.CompilerParams(vmem_limit_bytes=(8 << 20) + total * row_len * 4)
        if groups <= 32:
            taps = pl.pallas_call(
                functools.partial(taps_kernel, lambda: call),
                in_specs=[vmem, after],
                out_specs=vmem,
                out_shape=pltpu.VMEM(shape, BF16),
                compiler_params=limit,
                name="taps",
            )(tiles, near)
            return pltpu.with_memory_space_constraint(taps, pltpu.VMEM)
        taps = pl.pallas_call(
            functools.partial(taps_kernel, lambda: pl.program_id(0)),
            grid=(steps // 2,),
            in_specs=[pl.BlockSpec((total // 2, row_len), lambda i: (call, 0)), after],
            out_specs=pl.BlockSpec((height, depth), lambda i: (i, 0)),
            out_shape=pltpu.HBM(shape, BF16),
            compiler_params=limit,
            name="taps",
        )(tiles, near)
        return pltpu.with_memory_space_constraint(taps, pltpu.HBM)

    parts = det_dev // DET_ROWS

    def own_detections(near):
        return pl.pallas_call(
            own_kernel,
            out_shape=(
                jax.ShapeDtypeStruct((parts, DET_FINE * DET_ROWS, DET_DEPTH), BF16),
                jax.ShapeDtypeStruct((det_dev, LANES), F32),
            ),
            in_specs=[vmem, vmem, vmem, after],
            compiler_params=pltpu.CompilerParams(vmem_limit_bytes=16 << 20),
            name="own",
        )(packed, time_row, station_row, near)

    def whole(*shape):
        return pl.BlockSpec(shape, lambda i: (0,) * len(shape))

    params = pltpu.CompilerParams(vmem_limit_bytes=(16 << 20) + groups * (1 << 17))

    def correlate(data, taps, start):
        count = data.shape[0]
        sums = (count * rows, FINE * LANES)
        first = start % half // 4
        series, win = pl.pallas_call(
            windows_kernel,
            out_shape=(
                jax.ShapeDtypeStruct((count, PACKED, LANES), F32),
                jax.ShapeDtypeStruct((count, STATIONS, FINE, LANES), F32),
            ),
            compiler_params=params,
            name="windows",
        )(data)
        return pl.pallas_call(
            functools.partial(correlate_kernel, start),
            grid=(count // 4,),
            in_specs=[
                whole(*series.shape),
                whole(*win.shape),
                pl.BlockSpec((height, depth), lambda i: (first + i, 0)),
                whole(*scale.shape),
            ],
            out_specs=(whole(*sums), whole(*sums)),
            out_shape=(jax.ShapeDtypeStruct(sums, BF16),) * 2,
            scratch_shapes=[pltpu.VMEM((BLOCKS * COARSE, CHANNELS * LANES + LANES), BF16)] * 8,
            compiler_params=params,
            name="correlate",
        )(series, win, taps, scale)

    near, taps = packed, []
    *first, last = rounds(ngx, ngy)
    for n, (axis, mask) in enumerate(first):
        other = swap(near, axis, mask)
        beside = (near,)
        if n == 0:
            mine, mine_scale = own_detections(near)
            beside = (scale, mine_scale)
        elif n <= 2:
            taps.append(shifted(n - 1, near))
            beside = (taps[-1],)
        elif n == len(first) - 1:
            sums = [*correlate(near, taps[0], 0)]
            beside = (sums[0],)
        near = pl.pallas_call(
            join_kernel,
            out_shape=jax.ShapeDtypeStruct((2 * near.shape[0], PACKED, LANES), BF16),
            in_specs=[vmem, vmem] + [after] * len(beside),
            compiler_params=pltpu.CompilerParams(vmem_limit_bytes=16 << 20),
            name="join",
        )(near, other, *beside)
    far = swap(near, *last)

    sums += [*correlate(other, taps[0], half // 2), *correlate(far, taps[1], half)]
    stack = pl.pallas_call(
        stack_kernel,
        out_shape=jax.ShapeDtypeStruct((tpl_dev, LAG_BLOCKS * LANES), F32),
        compiler_params=params,
        name="stack",
    )(owner, *sums)
    cuts = pl.pallas_call(
        functools.partial(cuts_kernel, ngx, ngy),
        out_shape=(
            jax.ShapeDtypeStruct((4, CHANNELS, KEEP + 1, det_dev, LANES), BF16),
            jax.ShapeDtypeStruct((4, det_dev, LANES), F32),
        ),
        compiler_params=params,
        name="cuts",
    )(near, far, mine_scale, partners)
    diff = pl.pallas_call(
        detect_kernel,
        out_shape=jax.ShapeDtypeStruct((4 * det_dev, DTLAG), F32),
        scratch_shapes=[
            pltpu.VMEM((2, 4 * DET_COARSE * DET_ROWS, DET_DEPTH), BF16),
            pltpu.VMEM((parts, 4 * DET_COARSE * DET_ROWS, DET_FINE * DET_ROWS), F32),
            pltpu.VMEM((4 * det_dev, DET_FINE * DET_ROWS), F32),
        ],
        compiler_params=params,
        name="detect",
    )(mine, *cuts)
    return stack, diff.reshape(det_dev, 4, DTLAG)


def solution(mesh):
    return jax.shard_map(
        functools.partial(on_device, mesh.shape["gx"], mesh.shape["gy"]),
        mesh=mesh,
        in_specs=(
            P(("gx", "gy"), None, None),
            P(("gx", "gy"), None, None),
            P(("gx", "gy"), None),
            P(("gx", "gy")),
            P(("gx", "gy")),
            P(("gx", "gy"), None),
        ),
        out_specs=(P(("gx", "gy"), None), P(("gx", "gy"), None, None)),
        check_vma=False,
    )
```

```python
import functools

import jax
import jax.numpy as jnp
from jax import lax
from jax.experimental import pallas as pl
from jax.experimental.pallas import tpu as pltpu
from jax.sharding import PartitionSpec as P

LANES = 128
CHANNELS = 3
STATIONS = 2
BLOCKS = 12
TAPS = 4
LAG_BLOCKS = BLOCKS - TAPS
SLOTS = 8
FINE = 8
COARSE = LANES // FINE
DET_FINE = 16
DET_COARSE = LANES // DET_FINE
DET_ROWS = 16
W = 256
DTLAG = 128
HALF = DTLAG // 2
KEEP = W // LANES
DET_DEPTH = CHANNELS * KEEP * LANES + LANES
SPAN = STATIONS * BLOCKS
ROWS = CHANNELS * SPAN
PACKED = ROWS + 8
MXU = 256
PARTS = [(0, j) for j in range(TAPS + 1)] + [(c, j) for c in (1, 2) for j in range(TAPS)] + [(CHANNELS, 0)]
PASSES = len(PARTS) // 2
EPS = 1e-06
F32 = jnp.float32
BF16 = jnp.bfloat16
NT = (((1,), (1,)), ((), ()))


def iota(shape, axis):
    return lax.broadcasted_iota(jnp.int32, shape, axis)


def rot(value, shift, axis=1):
    shift = shift % value.shape[axis]
    return pltpu.roll(value, shift, axis) if shift else value


def dot(a, b):
    return jnp.dot(a, b, preferred_element_type=F32)


def dot_nt(a, b):
    return lax.dot_general(a, b, NT, preferred_element_type=F32)


def ones_where(mask):
    return jnp.where(mask, 1.0, 0.0).astype(BF16)


def pieces(value, count):
    out = []
    for _ in range(count - 1):
        high = value.astype(BF16)
        out.append(high)
        value = value - high.astype(F32)
    out.append(value.astype(BF16))
    return out


def column(row):
    n = row.shape[1]
    diagonal = iota((n, n), 0) == iota((n, n), 1)
    return jnp.sum(jnp.where(diagonal, row, 0), axis=1, keepdims=True)


def pack_kernel(wave_ref, *refs):
    small_refs, out_ref, copy_refs, rows_ref = refs[:4], refs[4], refs[5:9], refs[9]
    for source_ref, copy_ref in zip(small_refs, copy_refs):
        copy_ref[...] = source_ref[...]
    time_ref, station_ref = small_refs[:2]
    start = time_ref[...] - HALF
    row = BLOCKS * station_ref[...] + start // LANES
    shift = start % LANES
    pad = jnp.zeros((1, LANES - row.shape[1]), F32)
    for c in range(CHANNELS):
        series = wave_ref[c].astype(F32)
        for s in range(STATIONS):
            for block in range(BLOCKS):
                at = c * SPAN + s * BLOCKS + block
                rows_ref[at : at + 1, :] = series[s : s + 1, block * LANES : (block + 1) * LANES]
    rows_ref[ROWS : ROWS + 1, :] = jnp.concatenate([row.astype(F32), pad], axis=1)
    rows_ref[ROWS + 1 : ROWS + 2, :] = jnp.concatenate([shift.astype(F32), pad], axis=1)
    rows_ref[ROWS + 2 : PACKED, :] = jnp.zeros((PACKED - ROWS - 2, LANES), F32)
    out_ref[0] = rows_ref[...].astype(BF16)


def join_kernel(near_ref, other_ref, *refs):
    out_ref = refs[-1]
    half = near_ref.shape[0]
    out_ref[0:half] = near_ref[...]
    out_ref[half:] = other_ref[...]


def rounds(ngx, ngy):
    masks = []
    for axis, size in (("gy", ngy), ("gx", ngx)):
        while size > 1:
            size //= 2
            masks.append((axis, size))
    return masks


def position(ngx, ngy, x, y):
    away = {"gx": x ^ lax.axis_index("gx"), "gy": y ^ lax.axis_index("gy")}
    return sum(((away[axis] // mask) & 1) << n for n, (axis, mask) in enumerate(rounds(ngx, ngy)))


def tile_kernel(ngx, ngy, templates_ref, station_ref, sorted_ref, scale_ref, owner_ref, tiles_ref, semaphore):
    copy = pltpu.make_async_copy(templates_ref, tiles_ref, semaphore)
    copy.start()
    tpl_dev, k_slots, row_len = tiles_ref.shape
    count = tpl_dev * k_slots
    total = sorted_ref.shape[0]
    station = station_ref[...].astype(F32).astype(BF16)
    home = ones_where(iota((count, tpl_dev), 0) // k_slots == iota((count, tpl_dev), 1))
    home_t = ones_where(iota((tpl_dev, count), 1) // k_slots == iota((tpl_dev, count), 0))
    by_row = dot_nt(home, station)
    by_col = dot(station, home_t)
    own_col = iota((count, k_slots), 0) % k_slots == iota((count, k_slots), 1)
    own_row = iota((k_slots, count), 1) % k_slots == iota((k_slots, count), 0)
    st_col = jnp.sum(jnp.where(own_col, by_row, 0.0), axis=1, keepdims=True)
    st_row = jnp.sum(jnp.where(own_row, by_col, 0.0), axis=0, keepdims=True)
    earlier = iota((count, count), 0) < iota((count, count), 1)
    rank = jnp.sum(jnp.where((st_col == st_row) & earlier, 1.0, 0.0), axis=0, keepdims=True)
    st = st_row.astype(jnp.int32)
    group = st // STATIONS
    place_of = position(ngx, ngy, group // ngy, group % ngy)
    slot = (place_of * STATIONS + st % STATIONS) * SLOTS + rank.astype(jnp.int32)
    copy.wait()
    tiles = tiles_ref[...].reshape(count, row_len)
    step = 128
    for first in range(0, total, step):
        place = ones_where(iota((step, count), 0) + first == slot)
        moved = dot(place, tiles)
        sorted_ref[first : first + step, :] = moved.astype(BF16)
        mean = jnp.sum(moved * moved, axis=1, keepdims=True) / row_len
        scale = lax.rsqrt(row_len * (mean + EPS))
        scale_ref[first : first + step, :] = jnp.broadcast_to(scale, (step, LANES))
        owner_ref[:, first : first + step] = dot_nt(home_t, place).astype(BF16)


def windows_kernel(data_ref, rows_ref, win_ref):
    groups = data_ref.shape[0]
    step = min(16, groups)
    column_of = iota((LANES, LANES), 1)
    sample = FINE * (COARSE - 1 - column_of % COARSE) + column_of // COARSE
    row = iota((LANES, LANES), 0)
    sums_of = ones_where(jnp.concatenate([row >= sample, row < sample, row >= 0], axis=1))
    major, chunk = iota((step, FINE, LANES), 1), iota((step, FINE, LANES), 2) // COARSE

    def body(q, carry):
        x = data_ref[pl.ds(q * step, step)].astype(F32)
        rows_ref[pl.ds(q * step, step)] = x
        energy = sum(x[:, SPAN * c : SPAN * (c + 1)] * x[:, SPAN * c : SPAN * (c + 1)] for c in range(CHANNELS))
        count = step * SPAN
        sums = dot(jnp.concatenate(pieces(energy.reshape(count, LANES), 3), axis=0), sums_of)
        sums = sums[0:count] + sums[count : 2 * count] + sums[2 * count :]
        sums = sums.reshape(step, SPAN, 3 * LANES)
        for s in range(STATIONS):
            at = BLOCKS * s
            mean = sums[:, at : at + LAG_BLOCKS, 0:LANES]
            for j in range(1, TAPS):
                mean = mean + sums[:, at + j : at + j + LAG_BLOCKS, 2 * LANES :]
            mean = (mean + sums[:, at + TAPS : at + TAPS + LAG_BLOCKS, LANES : 2 * LANES]) / (
                CHANNELS * TAPS * LANES
            )
            value = lax.rsqrt(mean + EPS)
            for bit in range(3):
                size = 1 << bit
                up = (major // size) % 2
                other = (chunk // size) % 2
                later = rot(rot(value, -size, 1), size * COARSE, 2)
                earlier = rot(rot(value, size, 1), -size * COARSE, 2)
                value = jnp.where(up == other, value, jnp.where(up == 0, later, earlier))
            win_ref[pl.ds(q * step, step), s] = value
        return carry

    lax.fori_loop(0, groups // step, body, 0)


def build_data(rows_ref, g, s, c, out_ref):
    lane = iota((COARSE, LANES), 1)
    bound = FINE * (iota((COARSE, LANES), 0) + 1)
    now = None
    for block in range(BLOCKS):
        at = SPAN * c + BLOCKS * s + block
        row = rows_ref[g, pl.ds(at, FINE, stride=0), :]
        turned = [
            pltpu.roll(row, FINE * (1 + first), 1, stride=FINE, stride_axis=0) for first in range(0, COARSE, FINE)
        ]
        later = jnp.concatenate(turned, axis=0).astype(BF16)
        if block:
            out_ref[(block - 1) * COARSE : block * COARSE, c * LANES : (c + 1) * LANES] = jnp.where(
                lane < bound, now, later
            )
        now = later
        rows = slice((block - TAPS) * COARSE, (block - TAPS + 1) * COARSE)
        if c == 1 and block >= TAPS:
            out_ref[rows, CHANNELS * LANES :] = later
        if c == 2 and block >= TAPS:
            end = [pltpu.roll(row, FINE * first, 1, stride=FINE, stride_axis=0) for first in range(0, COARSE, FINE)]
            end = jnp.concatenate(end, axis=0).astype(BF16)
            out_ref[rows, CHANNELS * LANES :] = jnp.where(lane < LANES // 2, out_ref[rows, CHANNELS * LANES :], end)
    out_ref[(BLOCKS - 1) * COARSE : BLOCKS * COARSE, c * LANES : (c + 1) * LANES] = now


def build_taps(blocks_of, fine, height, out_ref, first, step):
    lane = iota((height, LANES), 1)
    zero = jnp.zeros((height, LANES), BF16)
    for b in range(fine):
        rows = slice(first + step * b, first + step * b + height)
        tail = zero
        at = 0
        for c, blocks in enumerate(blocks_of):
            before = zero
            for block in blocks:
                moved = rot(block, b)
                out_ref[rows, at : at + LANES] = jnp.where(lane < b, before, moved) if b else moved
                before = moved
                at += LANES
            if b:
                end = rot(blocks[-1], b + fine * c)
                tail = jnp.where((lane >= fine * c) & (lane < fine * c + b), end, tail)
        out_ref[rows, at : at + LANES] = tail


def taps_kernel(first, sorted_ref, after_ref, out_ref):
    height = FINE * STATIONS * SLOTS
    per_step = out_ref.shape[0] // height
    rows = STATIONS * SLOTS
    lane = iota((rows, LANES), 1)
    zero = jnp.zeros((rows, LANES), BF16)

    def body(i, carry):
        at = (first() * per_step + i) * rows
        tiles = sorted_ref[pl.ds(pl.multiple_of(at, rows), rows), :]
        out = out_ref.at[pl.ds(pl.multiple_of(i * height, height), height), :]
        for b in range(FINE):
            place = slice(b * rows, (b + 1) * rows)
            past = []
            block = 0
            for c in range(CHANNELS):
                before = zero
                for j in range(TAPS):
                    tile = tiles[:, (TAPS * c + j) * LANES : (TAPS * c + j + 1) * LANES]
                    moved = rot(tile, b)
                    lanes = slice(block * LANES, (block + 1) * LANES)
                    out[place, lanes] = jnp.where(lane < b, before, moved) if b else moved
                    before = moved
                    block += 1
                past.append(jnp.where(lane < b, before, zero) if b else zero)
                if c == 0:
                    out[place, block * LANES : (block + 1) * LANES] = past[0]
                    block += 1
            if b:
                end = rot(tile, b - FINE)
                past[1] = jnp.where((lane >= LANES - FINE) & (lane < LANES - FINE + b), end, past[1])
            out[place, block * LANES : (block + 1) * LANES] = past[1]
        return carry

    lax.fori_loop(0, per_step, body, 0)


def correlate_kernel(start, rows_ref, win_ref, taps_ref, scale_ref, high_ref, low_ref, *refs):
    x_refs = [[refs[4 * bank + 2 * n : 4 * bank + 2 * n + 2] for n in range(2)] for bank in range(2)]
    groups = rows_ref.shape[0]
    rows = STATIONS * SLOTS
    height = FINE * rows
    step = pl.program_id(0)

    def builds(first, bank):
        for n in range(2):
            for s in range(STATIONS):
                for c in range(CHANNELS):
                    yield lambda n=n, s=s, c=c: build_data(rows_ref, first + n, s, c, x_refs[bank][n][s])

    @pl.when(step == 0)
    def _():
        for write in builds(0, 0):
            write()

    def store_lags(i, raw):
        g = step * 4 + i
        scale = scale_ref[pl.ds(pl.multiple_of((start + g) * rows, rows), rows), :]
        at = pl.ds(pl.multiple_of(g * rows, rows), rows)
        for b in range(FINE):
            value, window = [], []
            for s in range(STATIONS):
                first = b * rows + s * SLOTS
                value.append(raw[first : first + SLOTS, s * LANES : (s + 1) * LANES])
                window.append(win_ref[g, s, pl.ds(b, SLOTS, stride=0), :])
            value = jnp.concatenate(value, axis=0) * scale * jnp.concatenate(window, axis=0)
            high, low = pieces(value, 2)
            high_ref[at, b * LANES : (b + 1) * LANES] = high
            low_ref[at, b * LANES : (b + 1) * LANES] = low

    def multiply(accs, bank, writes):
        for t in range(PASSES):
            for n in range(2):
                data = [
                    jnp.concatenate(
                        [ref[j * COARSE : j * COARSE + LANES, c * LANES : (c + 1) * LANES] for c, j in PARTS[2 * t : 2 * t + 2]],
                        axis=1,
                    )
                    for ref in x_refs[bank][n]
                ]
                pltpu.matmul_push_rhs(jnp.concatenate(data, axis=0), t % 2, n, transpose=True)
                first = (2 * bank + n) * height
                taps = taps_ref[first : first + height, t * MXU : (t + 1) * MXU]
                pltpu.matmul_acc_lhs(accs[n], taps, load_staged_rhs=t % 2)
            for write in writes[t::PASSES]:
                write()

    def four_groups(*accs):
        multiply(accs[:2], 0, list(builds(step * 4 + 2, 1)))
        finish = [lambda n=n: store_lags(n, pltpu.matmul_pop(accs[n])) for n in range(2)]
        multiply(accs[2:], 1, list(builds(jnp.minimum(step * 4 + 4, groups - 2), 0)) + finish)
        for n in range(2):
            store_lags(2 + n, pltpu.matmul_pop(accs[2 + n]))

    pl.run_scoped(four_groups, *[pltpu.ACC(n % 2)((height, MXU), F32) for n in range(4)])


def stack_kernel(owner_ref, *refs):
    stack_ref = refs[-1]
    total, first = 0.0, 0
    for high_ref, low_ref in zip(refs[0:-1:2], refs[1:-1:2]):
        owner = owner_ref[:, first : first + high_ref.shape[0]]
        total = total + dot(owner, high_ref[...]) + dot(owner, low_ref[...])
        first += high_ref.shape[0]
    tpl_dev = stack_ref.shape[0]
    block_of = iota((tpl_dev, FINE * LANES), 1) % LANES // COARSE
    place = iota((FINE * LANES, LANES), 0)
    spread = iota((FINE * LANES, LANES), 1) == FINE * (COARSE - 1 - place % COARSE) + place // LANES
    spread = ones_where(spread)
    out = 0.0
    for part in pieces(total, 2):
        part = part.astype(F32)
        masked = [jnp.where(block_of == block, part, 0.0) for block in range(LAG_BLOCKS)]
        out = out + dot(jnp.concatenate(masked, axis=0).astype(BF16), spread)
    for block in range(LAG_BLOCKS):
        rows = out[block * tpl_dev : (block + 1) * tpl_dev]
        stack_ref[:, block * LANES : (block + 1) * LANES] = rows * (1.0 / 8.0**0.5)


def cut(data, row, shift, blocks):
    det_dev = row.shape[0]
    row_iota, lane = iota((det_dev, PACKED), 1), iota((det_dev, LANES), 1)
    away = row_iota - row
    picks = [away == SPAN * c + j for c in range(CHANNELS) for j in range(blocks)]
    picks = jnp.concatenate([jnp.where(pick, 1.0, 0.0) for pick in picks], axis=0).astype(BF16)
    found = dot(picks, data).astype(BF16)
    found = [
        [found[(c * blocks + j) * det_dev : (c * blocks + j + 1) * det_dev] for j in range(blocks)]
        for c in range(CHANNELS)
    ]
    shift = jnp.broadcast_to(shift, (det_dev, LANES))
    for bit in range(7):
        size = 1 << bit
        moves = (shift & size) > 0
        found = [[jnp.where(moves, rot(block, -size), block) for block in row] for row in found]
    inside = lane < LANES - shift
    return [[jnp.where(inside, row[j], row[j + 1]) for j in range(blocks - 1)] for row in found]


def mean_square(blocks):
    total = 0.0
    for block, mask in blocks:
        block = block.astype(F32)
        square = block * block
        total = total + (square if mask is None else jnp.where(mask, square, 0.0))
    return jnp.sum(total, axis=1, keepdims=True) / (CHANNELS * W)


def own_windows(data, time_ref, station_ref):
    n = time_ref.shape[1]
    turned = iota((n, n), 0) ^ (DET_ROWS - 1) == iota((n, n), 1)
    start = jnp.sum(jnp.where(turned, time_ref[...], 0), axis=1, keepdims=True)
    station = jnp.sum(jnp.where(turned, station_ref[...], 0), axis=1, keepdims=True)
    mine = cut(data, station * BLOCKS + start // LANES, start % LANES, KEEP + 1)
    scale = lax.rsqrt(CHANNELS * W * (mean_square([(block, None) for blocks in mine for block in blocks]) + EPS))
    scale = jnp.sum(jnp.where(turned, scale, 0.0), axis=0, keepdims=True)
    return mine, column(scale)


def partner_windows(data, chosen_row):
    det_dev = chosen_row.shape[1]
    lane = iota((det_dev, LANES), 1)
    info = dot_nt(ones_where(lane == column(chosen_row)), data[PACKED - 16 : PACKED, :])
    pieces_of = cut(data, info[:, 8:9].astype(jnp.int32), info[:, 9:10].astype(jnp.int32), KEEP + 2)
    centre = []
    for first, middle, last in pieces_of:
        centre += [(first, lane >= HALF), (middle, None), (last, lane < HALF)]
    return pieces_of, lax.rsqrt(mean_square(centre) + EPS)


def differential(taps_ref, windows, x_ref, raw_ref, parts_ref):
    count = len(windows)
    height = count * DET_ROWS
    lane = iota((DET_ROWS, LANES), 1)
    wide = DET_FINE * DET_ROWS
    sub_lane = iota((8, LANES), 1) % DET_ROWS
    for q in range(taps_ref.shape[0]):
        rows = slice(q * DET_ROWS, (q + 1) * DET_ROWS)
        for d in range(count):
            source = [[block[rows] for block in blocks] for blocks in windows[d]]
            ends = {}
            for a in range(DET_COARSE):
                shift = DET_FINE * a
                out = slice((a * count + d) * DET_ROWS, (a * count + d + 1) * DET_ROWS)
                tail = None
                for c in range(CHANNELS):
                    moved = [rot(block, -shift) for block in source[c]]
                    ends[c, a] = moved[KEEP]
                    for j in range(KEEP):
                        block = jnp.where(lane < LANES - shift, moved[j], moved[j + 1]) if a else moved[j]
                        at = (c * KEEP + j) * LANES
                        x_ref[q % 2, out, at : at + LANES] = block
                    end = ends[c, a - c] if a >= c else rot(source[c][KEEP], DET_FINE * c - shift)
                    tail = end if tail is None else jnp.where(lane < DET_FINE * c, tail, end)
                x_ref[q % 2, out, DET_DEPTH - LANES : DET_DEPTH] = tail
        raw_ref[q] = dot_nt(x_ref[q % 2], taps_ref[q])
    for q in range(taps_ref.shape[0]):
        for half in range(2):
            for row in range(0, height, 8):
                upper = row % DET_ROWS // 8
                total = jnp.zeros((8, LANES), F32)
                for a in range(DET_COARSE):
                    part = raw_ref[q, a * height + row : a * height + row + 8, half * LANES : (half + 1) * LANES]
                    base = a + 1 if upper else a + LANES - DET_ROWS + 1
                    part = pltpu.roll(part, base, 1, stride=1, stride_axis=0)
                    total = jnp.where(sub_lane == 8 * upper + a, part, total)
                parts_ref[q * height + row : q * height + row + 8, half * LANES : (half + 1) * LANES] = total
    place, to = iota((wide, LANES), 0), iota((wide, LANES), 1)
    order = ones_where((to // DET_FINE == place % DET_COARSE) & (to % DET_FINE == place // DET_ROWS))
    return sum(dot(part, order) for part in pieces(parts_ref[...], 2))


def own_kernel(data_ref, time_ref, station_ref, after_ref, taps_ref, scale_ref):
    mine, scale = own_windows(data_ref[0], time_ref, station_ref)
    scale_ref[...] = jnp.broadcast_to(scale, scale_ref.shape)
    for q in range(taps_ref.shape[0]):
        rows = slice(q * DET_ROWS, (q + 1) * DET_ROWS)
        blocks = [[block[rows] for block in channel] for channel in mine]
        build_taps(blocks, DET_FINE, DET_ROWS, taps_ref.at[q], 0, DET_ROWS)


MOVES = ((1, 0), (-1, 0), (0, 1), (0, -1))


def cuts_kernel(ngx, ngy, directions, data_ref, scale_ref, partner_ref, *refs):
    windows_ref, scales_ref = refs[-2:]
    gx, gy = lax.axis_index("gx"), lax.axis_index("gy")
    for n, d in enumerate(directions):
        x, y = gx + MOVES[d][0], gy + MOVES[d][1]
        valid = (x >= 0) & (x < ngx) & (y >= 0) & (y < ngy)
        at = position(ngx, ngy, jnp.clip(x, 0, ngx - 1), jnp.clip(y, 0, ngy - 1)) % data_ref.shape[0]
        found, scale = partner_windows(data_ref[at], partner_ref[d : d + 1, :])
        for c in range(CHANNELS):
            for j in range(KEEP + 1):
                windows_ref[n, c, j] = found[c][j]
        scales_ref[n] = jnp.where(valid, scale_ref[...] * scale, 0.0)


def detect_kernel(taps_ref, *refs):
    cuts, (diff_ref, x_ref, raw_ref, parts_ref) = refs[:4], refs[4:]
    windows, scales = [], []
    for windows_ref, scales_ref in (cuts[0:2], cuts[2:4]):
        for n in range(2):
            windows.append([[windows_ref[n, c, j] for j in range(KEEP + 1)] for c in range(CHANNELS)])
            scales.append(scales_ref.at[n])
    out = differential(taps_ref, windows, x_ref, raw_ref, parts_ref)
    for q in range(taps_ref.shape[0]):
        for d in range(4):
            at = (q * 4 + d) * DET_ROWS
            rows = slice(q * DET_ROWS, (q + 1) * DET_ROWS)
            diff_ref[pl.ds(q * DET_ROWS * 4 + d, DET_ROWS, stride=4), :] = (
                out[at : at + DET_ROWS] * scales[d][rows, :]
            )


def on_device(ngx, ngy, waveforms, templates, tpl_stations, det_station, det_time, partner):
    tpl_dev, k_slots, row_len = templates.shape
    det_dev = det_station.shape[0]
    groups = ngx * ngy
    half = groups // 2
    rows = STATIONS * SLOTS
    total = groups * rows
    time_row, station_row = det_time.reshape(1, det_dev), det_station.reshape(1, det_dev)
    small = (time_row, station_row, partner.T, tpl_stations.T)
    packed, time_row, station_row, partners, tile_stations = pl.pallas_call(
        pack_kernel,
        out_shape=(pltpu.VMEM((1, PACKED, LANES), BF16),)
        + tuple(pltpu.VMEM(value.shape, value.dtype) for value in small),
        scratch_shapes=[pltpu.VMEM((PACKED, LANES), F32)],
        name="pack",
    )(waveforms.transpose(1, 0, 2), *small)

    def swap(value, axis, mask):
        size = {"gx": ngx, "gy": ngy}[axis]
        return lax.ppermute(value, axis, [(n, n ^ mask) for n in range(size)])

    vmem, after = pl.BlockSpec(memory_space=pltpu.VMEM), pl.BlockSpec(memory_space=pl.ANY)
    tiles, scale, owner = pl.pallas_call(
        functools.partial(tile_kernel, ngx, ngy),
        out_shape=(
            jax.ShapeDtypeStruct((total, row_len), BF16),
            jax.ShapeDtypeStruct((total, LANES), F32),
            jax.ShapeDtypeStruct((tpl_dev, total), BF16),
        ),
        in_specs=[after, vmem],
        scratch_shapes=[pltpu.VMEM(templates.shape, BF16), pltpu.SemaphoreType.DMA],
        compiler_params=pltpu.CompilerParams(vmem_limit_bytes=24 << 20),
        name="tiles",
    )(pltpu.with_memory_space_constraint(templates, pltpu.HBM), tile_stations)
    steps = groups // 4
    height = 4 * FINE * rows
    depth = MXU * PASSES
    def shifted(call, near):
        shape = (steps // 2 * height, depth)
        limit = pltpu.CompilerParams(vmem_limit_bytes=(8 << 20) + total * row_len * 4)
        if groups <= 32:
            taps = pl.pallas_call(
                functools.partial(taps_kernel, lambda: call),
                in_specs=[vmem, after],
                out_specs=vmem,
                out_shape=pltpu.VMEM(shape, BF16),
                compiler_params=limit,
                name="taps",
            )(tiles, near)
            return pltpu.with_memory_space_constraint(taps, pltpu.VMEM)
        taps = pl.pallas_call(
            functools.partial(taps_kernel, lambda: pl.program_id(0)),
            grid=(steps // 2,),
            in_specs=[pl.BlockSpec((total // 2, row_len), lambda i: (call, 0)), after],
            out_specs=pl.BlockSpec((height, depth), lambda i: (i, 0)),
            out_shape=pltpu.HBM(shape, BF16),
            compiler_params=limit,
            name="taps",
        )(tiles, near)
        return pltpu.with_memory_space_constraint(taps, pltpu.HBM)

    parts = det_dev // DET_ROWS

    def own_detections(near):
        return pl.pallas_call(
            own_kernel,
            out_shape=(
                jax.ShapeDtypeStruct((parts, DET_FINE * DET_ROWS, DET_DEPTH), BF16),
                jax.ShapeDtypeStruct((det_dev, LANES), F32),
            ),
            in_specs=[vmem, vmem, vmem, after],
            compiler_params=pltpu.CompilerParams(vmem_limit_bytes=16 << 20),
            name="own",
        )(packed, time_row, station_row, near)

    def whole(*shape):
        return pl.BlockSpec(shape, lambda i: (0,) * len(shape))

    params = pltpu.CompilerParams(vmem_limit_bytes=(16 << 20) + groups * (1 << 17))

    def correlate(data, taps, start):
        count = data.shape[0]
        sums = (count * rows, FINE * LANES)
        first = start % half // 4
        series, win = pl.pallas_call(
            windows_kernel,
            out_shape=(
                jax.ShapeDtypeStruct((count, PACKED, LANES), F32),
                jax.ShapeDtypeStruct((count, STATIONS, FINE, LANES), F32),
            ),
            compiler_params=params,
            name="windows",
        )(data)
        return pl.pallas_call(
            functools.partial(correlate_kernel, start),
            grid=(count // 4,),
            in_specs=[
                whole(*series.shape),
                whole(*win.shape),
                pl.BlockSpec((height, depth), lambda i: (first + i, 0)),
                whole(*scale.shape),
            ],
            out_specs=(whole(*sums), whole(*sums)),
            out_shape=(jax.ShapeDtypeStruct(sums, BF16),) * 2,
            scratch_shapes=[pltpu.VMEM((BLOCKS * COARSE, CHANNELS * LANES + LANES), BF16)] * 8,
            compiler_params=params,
            name="correlate",
        )(series, win, taps, scale)

    def cut_windows(directions, data):
        count = len(directions)
        return pl.pallas_call(
            functools.partial(cuts_kernel, ngx, ngy, directions),
            out_shape=(
                jax.ShapeDtypeStruct((count, CHANNELS, KEEP + 1, det_dev, LANES), BF16),
                jax.ShapeDtypeStruct((count, det_dev, LANES), F32),
            ),
            compiler_params=params,
            name="cuts",
        )(data, mine_scale, partners)

    near, taps = packed, []
    *first, last = rounds(ngx, ngy)
    for n, (axis, mask) in enumerate(first):
        other = swap(near, axis, mask)
        beside = (near,)
        if n == 0:
            mine, mine_scale = own_detections(near)
            beside = (scale, mine_scale)
        elif n <= 2:
            taps.append(shifted(n - 1, near))
            beside = (taps[-1],)
        elif n == len(first) - 1:
            sums = [*correlate(near, taps[0], 0)]
            near_cuts = cut_windows((2, 3), near)
            beside = (sums[0], near_cuts[0])
        near = pl.pallas_call(
            join_kernel,
            out_shape=jax.ShapeDtypeStruct((2 * near.shape[0], PACKED, LANES), BF16),
            in_specs=[vmem, vmem] + [after] * len(beside),
            compiler_params=pltpu.CompilerParams(vmem_limit_bytes=16 << 20),
            name="join",
        )(near, other, *beside)
    far = swap(near, *last)

    sums += [*correlate(other, taps[0], half // 2), *correlate(far, taps[1], half)]
    stack = pl.pallas_call(
        stack_kernel,
        out_shape=jax.ShapeDtypeStruct((tpl_dev, LAG_BLOCKS * LANES), F32),
        compiler_params=params,
        name="stack",
    )(owner, *sums)
    far_cuts = cut_windows((0, 1), far)
    diff = pl.pallas_call(
        detect_kernel,
        out_shape=jax.ShapeDtypeStruct((4 * det_dev, DTLAG), F32),
        scratch_shapes=[
            pltpu.VMEM((2, 4 * DET_COARSE * DET_ROWS, DET_DEPTH), BF16),
            pltpu.VMEM((parts, 4 * DET_COARSE * DET_ROWS, DET_FINE * DET_ROWS), F32),
            pltpu.VMEM((4 * det_dev, DET_FINE * DET_ROWS), F32),
        ],
        compiler_params=params,
        name="detect",
    )(mine, *far_cuts, *near_cuts)
    return stack, diff.reshape(det_dev, 4, DTLAG)


def solution(mesh):
    return jax.shard_map(
        functools.partial(on_device, mesh.shape["gx"], mesh.shape["gy"]),
        mesh=mesh,
        in_specs=(
            P(("gx", "gy"), None, None),
            P(("gx", "gy"), None, None),
            P(("gx", "gy"), None),
            P(("gx", "gy")),
            P(("gx", "gy")),
            P(("gx", "gy"), None),
        ),
        out_specs=(P(("gx", "gy"), None), P(("gx", "gy"), None, None)),
        check_vma=False,
    )
```

```python
import functools

import jax
import jax.numpy as jnp
from jax import lax
from jax.experimental import pallas as pl
from jax.experimental.pallas import tpu as pltpu
from jax.sharding import PartitionSpec as P

LANES = 128
CHANNELS = 3
STATIONS = 2
BLOCKS = 12
TAPS = 4
LAG_BLOCKS = BLOCKS - TAPS
SLOTS = 8
FINE = 8
COARSE = LANES // FINE
DET_FINE = 16
DET_COARSE = LANES // DET_FINE
DET_ROWS = 16
W = 256
DTLAG = 128
HALF = DTLAG // 2
KEEP = W // LANES
DET_DEPTH = CHANNELS * KEEP * LANES + LANES
SPAN = STATIONS * BLOCKS
ROWS = CHANNELS * SPAN
PACKED = ROWS + 8
MXU = 256
PARTS = [(0, j) for j in range(TAPS + 1)] + [(c, j) for c in (1, 2) for j in range(TAPS)] + [(CHANNELS, 0)]
PASSES = len(PARTS) // 2
EPS = 1e-06
F32 = jnp.float32
BF16 = jnp.bfloat16
NT = (((1,), (1,)), ((), ()))


def iota(shape, axis):
    return lax.broadcasted_iota(jnp.int32, shape, axis)


def rot(value, shift, axis=1):
    shift = shift % value.shape[axis]
    return pltpu.roll(value, shift, axis) if shift else value


def dot(a, b):
    return jnp.dot(a, b, preferred_element_type=F32)


def dot_nt(a, b):
    return lax.dot_general(a, b, NT, preferred_element_type=F32)


def ones_where(mask):
    return jnp.where(mask, 1.0, 0.0).astype(BF16)


def pieces(value, count):
    out = []
    for _ in range(count - 1):
        high = value.astype(BF16)
        out.append(high)
        value = value - high.astype(F32)
    out.append(value.astype(BF16))
    return out


def column(row):
    n = row.shape[1]
    diagonal = iota((n, n), 0) == iota((n, n), 1)
    return jnp.sum(jnp.where(diagonal, row, 0), axis=1, keepdims=True)


def pack_kernel(wave_ref, *refs):
    small_refs, out_ref, copy_refs, rows_ref = refs[:4], refs[4], refs[5:9], refs[9]
    for source_ref, copy_ref in zip(small_refs, copy_refs):
        copy_ref[...] = source_ref[...]
    time_ref, station_ref = small_refs[:2]
    start = time_ref[...] - HALF
    row = BLOCKS * station_ref[...] + start // LANES
    shift = start % LANES
    pad = jnp.zeros((1, LANES - row.shape[1]), F32)
    for c in range(CHANNELS):
        series = wave_ref[c].astype(F32)
        for s in range(STATIONS):
            for block in range(BLOCKS):
                at = c * SPAN + s * BLOCKS + block
                rows_ref[at : at + 1, :] = series[s : s + 1, block * LANES : (block + 1) * LANES]
    rows_ref[ROWS : ROWS + 1, :] = jnp.concatenate([row.astype(F32), pad], axis=1)
    rows_ref[ROWS + 1 : ROWS + 2, :] = jnp.concatenate([shift.astype(F32), pad], axis=1)
    rows_ref[ROWS + 2 : PACKED, :] = jnp.zeros((PACKED - ROWS - 2, LANES), F32)
    out_ref[0] = rows_ref[...].astype(BF16)


def join_kernel(near_ref, other_ref, *refs):
    out_ref = refs[-1]
    half = near_ref.shape[0]
    out_ref[0:half] = near_ref[...]
    out_ref[half:] = other_ref[...]


def rounds(ngx, ngy):
    masks = []
    for axis, size in (("gy", ngy), ("gx", ngx)):
        while size > 1:
            size //= 2
            masks.append((axis, size))
    return masks


def position(ngx, ngy, x, y):
    away = {"gx": x ^ lax.axis_index("gx"), "gy": y ^ lax.axis_index("gy")}
    return sum(((away[axis] // mask) & 1) << n for n, (axis, mask) in enumerate(rounds(ngx, ngy)))


def tile_kernel(ngx, ngy, templates_ref, station_ref, sorted_ref, scale_ref, owner_ref, tiles_ref, semaphore):
    copy = pltpu.make_async_copy(templates_ref, tiles_ref, semaphore)
    copy.start()
    tpl_dev, k_slots, row_len = tiles_ref.shape
    count = tpl_dev * k_slots
    total = sorted_ref.shape[0]
    station = station_ref[...].astype(F32).astype(BF16)
    home = ones_where(iota((count, tpl_dev), 0) // k_slots == iota((count, tpl_dev), 1))
    home_t = ones_where(iota((tpl_dev, count), 1) // k_slots == iota((tpl_dev, count), 0))
    by_row = dot_nt(home, station)
    by_col = dot(station, home_t)
    own_col = iota((count, k_slots), 0) % k_slots == iota((count, k_slots), 1)
    own_row = iota((k_slots, count), 1) % k_slots == iota((k_slots, count), 0)
    st_col = jnp.sum(jnp.where(own_col, by_row, 0.0), axis=1, keepdims=True)
    st_row = jnp.sum(jnp.where(own_row, by_col, 0.0), axis=0, keepdims=True)
    earlier = iota((count, count), 0) < iota((count, count), 1)
    rank = jnp.sum(jnp.where((st_col == st_row) & earlier, 1.0, 0.0), axis=0, keepdims=True)
    st = st_row.astype(jnp.int32)
    group = st // STATIONS
    place_of = position(ngx, ngy, group // ngy, group % ngy)
    slot = (place_of * STATIONS + st % STATIONS) * SLOTS + rank.astype(jnp.int32)
    copy.wait()
    tiles = tiles_ref[...].reshape(count, row_len)
    step = 128
    for first in range(0, total, step):
        place = ones_where(iota((step, count), 0) + first == slot)
        moved = dot(place, tiles)
        sorted_ref[first : first + step, :] = moved.astype(BF16)
        mean = jnp.sum(moved * moved, axis=1, keepdims=True) / row_len
        scale = lax.rsqrt(row_len * (mean + EPS))
        scale_ref[first : first + step, :] = jnp.broadcast_to(scale, (step, LANES))
        owner_ref[:, first : first + step] = dot_nt(home_t, place).astype(BF16)


def windows_kernel(data_ref, rows_ref, win_ref):
    groups = data_ref.shape[0]
    step = min(16, groups)
    column_of = iota((LANES, LANES), 1)
    sample = FINE * (COARSE - 1 - column_of % COARSE) + column_of // COARSE
    row = iota((LANES, LANES), 0)
    sums_of = ones_where(jnp.concatenate([row >= sample, row < sample, row >= 0], axis=1))
    major, chunk = iota((step, FINE, LANES), 1), iota((step, FINE, LANES), 2) // COARSE

    def body(q, carry):
        x = data_ref[pl.ds(q * step, step)].astype(F32)
        rows_ref[pl.ds(q * step, step)] = x
        energy = sum(x[:, SPAN * c : SPAN * (c + 1)] * x[:, SPAN * c : SPAN * (c + 1)] for c in range(CHANNELS))
        count = step * SPAN
        sums = dot(jnp.concatenate(pieces(energy.reshape(count, LANES), 3), axis=0), sums_of)
        sums = sums[0:count] + sums[count : 2 * count] + sums[2 * count :]
        sums = sums.reshape(step, SPAN, 3 * LANES)
        for s in range(STATIONS):
            at = BLOCKS * s
            mean = sums[:, at : at + LAG_BLOCKS, 0:LANES]
            for j in range(1, TAPS):
                mean = mean + sums[:, at + j : at + j + LAG_BLOCKS, 2 * LANES :]
            mean = (mean + sums[:, at + TAPS : at + TAPS + LAG_BLOCKS, LANES : 2 * LANES]) / (
                CHANNELS * TAPS * LANES
            )
            value = lax.rsqrt(mean + EPS)
            for bit in range(3):
                size = 1 << bit
                up = (major // size) % 2
                other = (chunk // size) % 2
                later = rot(rot(value, -size, 1), size * COARSE, 2)
                earlier = rot(rot(value, size, 1), -size * COARSE, 2)
                value = jnp.where(up == other, value, jnp.where(up == 0, later, earlier))
            win_ref[pl.ds(q * step, step), s] = value
        return carry

    lax.fori_loop(0, groups // step, body, 0)


def build_data(rows_ref, g, s, c, out_ref):
    lane = iota((COARSE, LANES), 1)
    bound = FINE * (iota((COARSE, LANES), 0) + 1)
    now = None
    for block in range(BLOCKS):
        at = SPAN * c + BLOCKS * s + block
        row = rows_ref[g, pl.ds(at, FINE, stride=0), :]
        turned = [
            pltpu.roll(row, FINE * (1 + first), 1, stride=FINE, stride_axis=0) for first in range(0, COARSE, FINE)
        ]
        later = jnp.concatenate(turned, axis=0).astype(BF16)
        if block:
            out_ref[(block - 1) * COARSE : block * COARSE, c * LANES : (c + 1) * LANES] = jnp.where(
                lane < bound, now, later
            )
        now = later
        rows = slice((block - TAPS) * COARSE, (block - TAPS + 1) * COARSE)
        if c == 1 and block >= TAPS:
            out_ref[rows, CHANNELS * LANES :] = later
        if c == 2 and block >= TAPS:
            end = [pltpu.roll(row, FINE * first, 1, stride=FINE, stride_axis=0) for first in range(0, COARSE, FINE)]
            end = jnp.concatenate(end, axis=0).astype(BF16)
            out_ref[rows, CHANNELS * LANES :] = jnp.where(lane < LANES // 2, out_ref[rows, CHANNELS * LANES :], end)
    out_ref[(BLOCKS - 1) * COARSE : BLOCKS * COARSE, c * LANES : (c + 1) * LANES] = now


def build_taps(blocks_of, fine, height, out_ref, first, step):
    lane = iota((height, LANES), 1)
    zero = jnp.zeros((height, LANES), BF16)
    for b in range(fine):
        rows = slice(first + step * b, first + step * b + height)
        tail = zero
        at = 0
        for c, blocks in enumerate(blocks_of):
            before = zero
            for block in blocks:
                moved = rot(block, b)
                out_ref[rows, at : at + LANES] = jnp.where(lane < b, before, moved) if b else moved
                before = moved
                at += LANES
            if b:
                end = rot(blocks[-1], b + fine * c)
                tail = jnp.where((lane >= fine * c) & (lane < fine * c + b), end, tail)
        out_ref[rows, at : at + LANES] = tail


def taps_kernel(first, sorted_ref, after_ref, out_ref):
    height = FINE * STATIONS * SLOTS
    per_step = out_ref.shape[0] // height
    rows = STATIONS * SLOTS
    lane = iota((rows, LANES), 1)
    zero = jnp.zeros((rows, LANES), BF16)

    def body(i, carry):
        at = (first() * per_step + i) * rows
        tiles = sorted_ref[pl.ds(pl.multiple_of(at, rows), rows), :]
        out = out_ref.at[pl.ds(pl.multiple_of(i * height, height), height), :]
        for b in range(FINE):
            place = slice(b * rows, (b + 1) * rows)
            past = []
            block = 0
            for c in range(CHANNELS):
                before = zero
                for j in range(TAPS):
                    tile = tiles[:, (TAPS * c + j) * LANES : (TAPS * c + j + 1) * LANES]
                    moved = rot(tile, b)
                    lanes = slice(block * LANES, (block + 1) * LANES)
                    out[place, lanes] = jnp.where(lane < b, before, moved) if b else moved
                    before = moved
                    block += 1
                past.append(jnp.where(lane < b, before, zero) if b else zero)
                if c == 0:
                    out[place, block * LANES : (block + 1) * LANES] = past[0]
                    block += 1
            if b:
                end = rot(tile, b - FINE)
                past[1] = jnp.where((lane >= LANES - FINE) & (lane < LANES - FINE + b), end, past[1])
            out[place, block * LANES : (block + 1) * LANES] = past[1]
        return carry

    lax.fori_loop(0, per_step, body, 0)


def correlate_kernel(start, rows_ref, win_ref, taps_ref, scale_ref, high_ref, low_ref, *refs):
    x_refs = [[refs[4 * bank + 2 * n : 4 * bank + 2 * n + 2] for n in range(2)] for bank in range(2)]
    groups = rows_ref.shape[0]
    rows = STATIONS * SLOTS
    height = FINE * rows
    step = pl.program_id(0)

    def builds(first, bank):
        for n in range(2):
            for s in range(STATIONS):
                for c in range(CHANNELS):
                    yield lambda n=n, s=s, c=c: build_data(rows_ref, first + n, s, c, x_refs[bank][n][s])

    @pl.when(step == 0)
    def _():
        for write in builds(0, 0):
            write()

    def store_lags(i, raw):
        g = step * 4 + i
        scale = scale_ref[pl.ds(pl.multiple_of((start + g) * rows, rows), rows), :]
        at = pl.ds(pl.multiple_of(g * rows, rows), rows)
        for b in range(FINE):
            value, window = [], []
            for s in range(STATIONS):
                first = b * rows + s * SLOTS
                value.append(raw[first : first + SLOTS, s * LANES : (s + 1) * LANES])
                window.append(win_ref[g, s, pl.ds(b, SLOTS, stride=0), :])
            value = jnp.concatenate(value, axis=0) * scale * jnp.concatenate(window, axis=0)
            high, low = pieces(value, 2)
            high_ref[at, b * LANES : (b + 1) * LANES] = high
            low_ref[at, b * LANES : (b + 1) * LANES] = low

    def multiply(accs, bank, writes):
        for t in range(PASSES):
            for n in range(2):
                data = [
                    jnp.concatenate(
                        [ref[j * COARSE : j * COARSE + LANES, c * LANES : (c + 1) * LANES] for c, j in PARTS[2 * t : 2 * t + 2]],
                        axis=1,
                    )
                    for ref in x_refs[bank][n]
                ]
                pltpu.matmul_push_rhs(jnp.concatenate(data, axis=0), t % 2, n, transpose=True)
                first = (2 * bank + n) * height
                taps = taps_ref[first : first + height, t * MXU : (t + 1) * MXU]
                pltpu.matmul_acc_lhs(accs[n], taps, load_staged_rhs=t % 2)
            for write in writes[t::PASSES]:
                write()

    def four_groups(*accs):
        multiply(accs[:2], 0, list(builds(step * 4 + 2, 1)))
        finish = [lambda n=n: store_lags(n, pltpu.matmul_pop(accs[n])) for n in range(2)]
        multiply(accs[2:], 1, list(builds(jnp.minimum(step * 4 + 4, groups - 2), 0)) + finish)
        for n in range(2):
            store_lags(2 + n, pltpu.matmul_pop(accs[2 + n]))

    pl.run_scoped(four_groups, *[pltpu.ACC(n % 2)((height, MXU), F32) for n in range(4)])


def stack_kernel(owner_ref, *refs):
    stack_ref = refs[-1]
    total, first = 0.0, 0
    for high_ref, low_ref in zip(refs[0:-1:2], refs[1:-1:2]):
        owner = owner_ref[:, first : first + high_ref.shape[0]]
        total = total + dot(owner, high_ref[...]) + dot(owner, low_ref[...])
        first += high_ref.shape[0]
    tpl_dev = stack_ref.shape[0]
    block_of = iota((tpl_dev, FINE * LANES), 1) % LANES // COARSE
    place = iota((FINE * LANES, LANES), 0)
    spread = iota((FINE * LANES, LANES), 1) == FINE * (COARSE - 1 - place % COARSE) + place // LANES
    spread = ones_where(spread)
    out = 0.0
    for part in pieces(total, 2):
        part = part.astype(F32)
        masked = [jnp.where(block_of == block, part, 0.0) for block in range(LAG_BLOCKS)]
        out = out + dot(jnp.concatenate(masked, axis=0).astype(BF16), spread)
    for block in range(LAG_BLOCKS):
        rows = out[block * tpl_dev : (block + 1) * tpl_dev]
        stack_ref[:, block * LANES : (block + 1) * LANES] = rows * (1.0 / 8.0**0.5)


def cut(data, row, shift, blocks):
    det_dev = row.shape[0]
    row_iota, lane = iota((det_dev, PACKED), 1), iota((det_dev, LANES), 1)
    away = row_iota - row
    picks = [away == SPAN * c + j for c in range(CHANNELS) for j in range(blocks)]
    picks = jnp.concatenate([jnp.where(pick, 1.0, 0.0) for pick in picks], axis=0).astype(BF16)
    found = dot(picks, data).astype(BF16)
    found = [
        [found[(c * blocks + j) * det_dev : (c * blocks + j + 1) * det_dev] for j in range(blocks)]
        for c in range(CHANNELS)
    ]
    shift = jnp.broadcast_to(shift, (det_dev, LANES))
    for bit in range(7):
        size = 1 << bit
        moves = (shift & size) > 0
        found = [[jnp.where(moves, rot(block, -size), block) for block in row] for row in found]
    inside = lane < LANES - shift
    return [[jnp.where(inside, row[j], row[j + 1]) for j in range(blocks - 1)] for row in found]


def mean_square(blocks):
    total = 0.0
    for block, mask in blocks:
        block = block.astype(F32)
        square = block * block
        total = total + (square if mask is None else jnp.where(mask, square, 0.0))
    return jnp.sum(total, axis=1, keepdims=True) / (CHANNELS * W)


def own_windows(data, time_ref, station_ref):
    n = time_ref.shape[1]
    turned = iota((n, n), 0) ^ (DET_ROWS - 1) == iota((n, n), 1)
    start = jnp.sum(jnp.where(turned, time_ref[...], 0), axis=1, keepdims=True)
    station = jnp.sum(jnp.where(turned, station_ref[...], 0), axis=1, keepdims=True)
    mine = cut(data, station * BLOCKS + start // LANES, start % LANES, KEEP + 1)
    scale = lax.rsqrt(CHANNELS * W * (mean_square([(block, None) for blocks in mine for block in blocks]) + EPS))
    scale = jnp.sum(jnp.where(turned, scale, 0.0), axis=0, keepdims=True)
    return mine, column(scale)


def partner_windows(data, chosen_row):
    det_dev = chosen_row.shape[1]
    lane = iota((det_dev, LANES), 1)
    info = dot_nt(ones_where(lane == column(chosen_row)), data[PACKED - 16 : PACKED, :])
    pieces_of = cut(data, info[:, 8:9].astype(jnp.int32), info[:, 9:10].astype(jnp.int32), KEEP + 2)
    centre = []
    for first, middle, last in pieces_of:
        centre += [(first, lane >= HALF), (middle, None), (last, lane < HALF)]
    return pieces_of, lax.rsqrt(mean_square(centre) + EPS)


def differential(taps_ref, windows, x_ref, raw_ref, parts_ref):
    count = len(windows)
    height = count * DET_ROWS
    lane = iota((DET_ROWS, LANES), 1)
    wide = DET_FINE * DET_ROWS
    sub_lane = iota((8, LANES), 1) % DET_ROWS
    for q in range(taps_ref.shape[0]):
        rows = slice(q * DET_ROWS, (q + 1) * DET_ROWS)
        for d in range(count):
            source = [[block[rows] for block in blocks] for blocks in windows[d]]
            ends = {}
            for a in range(DET_COARSE):
                shift = DET_FINE * a
                out = slice((a * count + d) * DET_ROWS, (a * count + d + 1) * DET_ROWS)
                tail = None
                for c in range(CHANNELS):
                    moved = [rot(block, -shift) for block in source[c]]
                    ends[c, a] = moved[KEEP]
                    for j in range(KEEP):
                        block = jnp.where(lane < LANES - shift, moved[j], moved[j + 1]) if a else moved[j]
                        at = (c * KEEP + j) * LANES
                        x_ref[q % 2, out, at : at + LANES] = block
                    end = ends[c, a - c] if a >= c else rot(source[c][KEEP], DET_FINE * c - shift)
                    tail = end if tail is None else jnp.where(lane < DET_FINE * c, tail, end)
                x_ref[q % 2, out, DET_DEPTH - LANES : DET_DEPTH] = tail
        raw_ref[q] = dot_nt(x_ref[q % 2], taps_ref[q])
    for q in range(taps_ref.shape[0]):
        for half in range(2):
            for row in range(0, height, 8):
                upper = row % DET_ROWS // 8
                total = jnp.zeros((8, LANES), F32)
                for a in range(DET_COARSE):
                    part = raw_ref[q, a * height + row : a * height + row + 8, half * LANES : (half + 1) * LANES]
                    base = a + 1 if upper else a + LANES - DET_ROWS + 1
                    part = pltpu.roll(part, base, 1, stride=1, stride_axis=0)
                    total = jnp.where(sub_lane == 8 * upper + a, part, total)
                parts_ref[q * height + row : q * height + row + 8, half * LANES : (half + 1) * LANES] = total
    place, to = iota((wide, LANES), 0), iota((wide, LANES), 1)
    order = ones_where((to // DET_FINE == place % DET_COARSE) & (to % DET_FINE == place // DET_ROWS))
    return sum(dot(part, order) for part in pieces(parts_ref[...], 2))


def own_kernel(data_ref, time_ref, station_ref, after_ref, taps_ref, scale_ref):
    mine, scale = own_windows(data_ref[0], time_ref, station_ref)
    scale_ref[...] = jnp.broadcast_to(scale, scale_ref.shape)
    for q in range(taps_ref.shape[0]):
        rows = slice(q * DET_ROWS, (q + 1) * DET_ROWS)
        blocks = [[block[rows] for block in channel] for channel in mine]
        build_taps(blocks, DET_FINE, DET_ROWS, taps_ref.at[q], 0, DET_ROWS)


MOVES = ((1, 0), (-1, 0), (0, 1), (0, -1))


def cuts_kernel(ngx, ngy, directions, data_ref, scale_ref, partner_ref, *refs):
    windows_ref, scales_ref = refs[-2:]
    gx, gy = lax.axis_index("gx"), lax.axis_index("gy")
    for n, d in enumerate(directions):
        x, y = gx + MOVES[d][0], gy + MOVES[d][1]
        valid = (x >= 0) & (x < ngx) & (y >= 0) & (y < ngy)
        at = position(ngx, ngy, jnp.clip(x, 0, ngx - 1), jnp.clip(y, 0, ngy - 1)) % data_ref.shape[0]
        found, scale = partner_windows(data_ref[at], partner_ref[d : d + 1, :])
        for c in range(CHANNELS):
            for j in range(KEEP + 1):
                windows_ref[n, c, j] = found[c][j]
        scales_ref[n] = jnp.where(valid, scale_ref[...] * scale, 0.0)


def detect_kernel(last, taps_ref, windows_ref, scales_ref, *refs):
    out_ref, x_ref, raw_ref, parts_ref = refs[-4:]
    windows = [[[windows_ref[n, c, j] for j in range(KEEP + 1)] for c in range(CHANNELS)] for n in range(2)]
    out = differential(taps_ref, windows, x_ref, raw_ref, parts_ref)
    for q in range(taps_ref.shape[0]):
        for n in range(2):
            at = (q * 2 + n) * DET_ROWS
            value = out[at : at + DET_ROWS] * scales_ref[n, q * DET_ROWS : (q + 1) * DET_ROWS, :]
            if last:
                first = q * DET_ROWS * 4 + n
                out_ref[pl.ds(first, DET_ROWS, stride=4), :] = value
                out_ref[pl.ds(first + 2, DET_ROWS, stride=4), :] = refs[0][at : at + DET_ROWS, :]
            else:
                out_ref[at : at + DET_ROWS, :] = value


def on_device(ngx, ngy, waveforms, templates, tpl_stations, det_station, det_time, partner):
    tpl_dev, k_slots, row_len = templates.shape
    det_dev = det_station.shape[0]
    groups = ngx * ngy
    half = groups // 2
    rows = STATIONS * SLOTS
    total = groups * rows
    time_row, station_row = det_time.reshape(1, det_dev), det_station.reshape(1, det_dev)
    small = (time_row, station_row, partner.T, tpl_stations.T)
    packed, time_row, station_row, partners, tile_stations = pl.pallas_call(
        pack_kernel,
        out_shape=(pltpu.VMEM((1, PACKED, LANES), BF16),)
        + tuple(pltpu.VMEM(value.shape, value.dtype) for value in small),
        scratch_shapes=[pltpu.VMEM((PACKED, LANES), F32)],
        name="pack",
    )(waveforms.transpose(1, 0, 2), *small)

    def swap(value, axis, mask):
        size = {"gx": ngx, "gy": ngy}[axis]
        return lax.ppermute(value, axis, [(n, n ^ mask) for n in range(size)])

    vmem, after = pl.BlockSpec(memory_space=pltpu.VMEM), pl.BlockSpec(memory_space=pl.ANY)
    tiles, scale, owner = pl.pallas_call(
        functools.partial(tile_kernel, ngx, ngy),
        out_shape=(
            jax.ShapeDtypeStruct((total, row_len), BF16),
            jax.ShapeDtypeStruct((total, LANES), F32),
            jax.ShapeDtypeStruct((tpl_dev, total), BF16),
        ),
        in_specs=[after, vmem],
        scratch_shapes=[pltpu.VMEM(templates.shape, BF16), pltpu.SemaphoreType.DMA],
        compiler_params=pltpu.CompilerParams(vmem_limit_bytes=24 << 20),
        name="tiles",
    )(pltpu.with_memory_space_constraint(templates, pltpu.HBM), tile_stations)
    steps = groups // 4
    height = 4 * FINE * rows
    depth = MXU * PASSES
    def shifted(call, near):
        shape = (steps // 2 * height, depth)
        limit = pltpu.CompilerParams(vmem_limit_bytes=(8 << 20) + total * row_len * 4)
        if groups <= 32:
            taps = pl.pallas_call(
                functools.partial(taps_kernel, lambda: call),
                in_specs=[vmem, after],
                out_specs=vmem,
                out_shape=pltpu.VMEM(shape, BF16),
                compiler_params=limit,
                name="taps",
            )(tiles, near)
            return pltpu.with_memory_space_constraint(taps, pltpu.VMEM)
        taps = pl.pallas_call(
            functools.partial(taps_kernel, lambda: pl.program_id(0)),
            grid=(steps // 2,),
            in_specs=[pl.BlockSpec((total // 2, row_len), lambda i: (call, 0)), after],
            out_specs=pl.BlockSpec((height, depth), lambda i: (i, 0)),
            out_shape=pltpu.HBM(shape, BF16),
            compiler_params=limit,
            name="taps",
        )(tiles, near)
        return pltpu.with_memory_space_constraint(taps, pltpu.HBM)

    parts = det_dev // DET_ROWS

    def own_detections(near):
        return pl.pallas_call(
            own_kernel,
            out_shape=(
                jax.ShapeDtypeStruct((parts, DET_FINE * DET_ROWS, DET_DEPTH), BF16),
                jax.ShapeDtypeStruct((det_dev, LANES), F32),
            ),
            in_specs=[vmem, vmem, vmem, after],
            compiler_params=pltpu.CompilerParams(vmem_limit_bytes=16 << 20),
            name="own",
        )(packed, time_row, station_row, near)

    def whole(*shape):
        return pl.BlockSpec(shape, lambda i: (0,) * len(shape))

    params = pltpu.CompilerParams(vmem_limit_bytes=(16 << 20) + groups * (1 << 17))

    def correlate(data, taps, start):
        count = data.shape[0]
        sums = (count * rows, FINE * LANES)
        first = start % half // 4
        series, win = pl.pallas_call(
            windows_kernel,
            out_shape=(
                jax.ShapeDtypeStruct((count, PACKED, LANES), F32),
                jax.ShapeDtypeStruct((count, STATIONS, FINE, LANES), F32),
            ),
            compiler_params=params,
            name="windows",
        )(data)
        return pl.pallas_call(
            functools.partial(correlate_kernel, start),
            grid=(count // 4,),
            in_specs=[
                whole(*series.shape),
                whole(*win.shape),
                pl.BlockSpec((height, depth), lambda i: (first + i, 0)),
                whole(*scale.shape),
            ],
            out_specs=(whole(*sums), whole(*sums)),
            out_shape=(jax.ShapeDtypeStruct(sums, BF16),) * 2,
            scratch_shapes=[pltpu.VMEM((BLOCKS * COARSE, CHANNELS * LANES + LANES), BF16)] * 8,
            compiler_params=params,
            name="correlate",
        )(series, win, taps, scale)

    def cut_windows(directions, data):
        count = len(directions)
        return pl.pallas_call(
            functools.partial(cuts_kernel, ngx, ngy, directions),
            out_shape=(
                jax.ShapeDtypeStruct((count, CHANNELS, KEEP + 1, det_dev, LANES), BF16),
                jax.ShapeDtypeStruct((count, det_dev, LANES), F32),
            ),
            compiler_params=params,
            name="cuts",
        )(data, mine_scale, partners)

    def detect(cuts, *done):
        high = 2 * DET_COARSE * DET_ROWS
        return pl.pallas_call(
            functools.partial(detect_kernel, len(done)),
            out_shape=jax.ShapeDtypeStruct(((4 if done else 2) * det_dev, DTLAG), F32),
            scratch_shapes=[
                pltpu.VMEM((2, high, DET_DEPTH), BF16),
                pltpu.VMEM((parts, high, DET_FINE * DET_ROWS), F32),
                pltpu.VMEM((2 * det_dev, DET_FINE * DET_ROWS), F32),
            ],
            compiler_params=params,
            name="detect",
        )(mine, *cuts, *done)

    near, taps = packed, []
    *first, last = rounds(ngx, ngy)
    for n, (axis, mask) in enumerate(first):
        other = swap(near, axis, mask)
        beside = (near,)
        if n == 0:
            mine, mine_scale = own_detections(near)
            beside = (scale, mine_scale)
        elif n <= 2:
            taps.append(shifted(n - 1, near))
            beside = (taps[-1],)
        elif n == len(first) - 1:
            sums = [*correlate(near, taps[0], 0)]
            near_lags = detect(near_cuts)
            beside = (sums[0], near_lags)
        if near.shape[0] == ngy:
            near_cuts = cut_windows((2, 3), near)
            beside += (near_cuts[0],)
        near = pl.pallas_call(
            join_kernel,
            out_shape=jax.ShapeDtypeStruct((2 * near.shape[0], PACKED, LANES), BF16),
            in_specs=[vmem, vmem] + [after] * len(beside),
            compiler_params=pltpu.CompilerParams(vmem_limit_bytes=16 << 20),
            name="join",
        )(near, other, *beside)
    far = swap(near, *last)

    sums += [*correlate(other, taps[0], half // 2), *correlate(far, taps[1], half)]
    stack = pl.pallas_call(
        stack_kernel,
        out_shape=jax.ShapeDtypeStruct((tpl_dev, LAG_BLOCKS * LANES), F32),
        compiler_params=params,
        name="stack",
    )(owner, *sums)
    far_cuts = cut_windows((0, 1), far)
    diff = detect(far_cuts, near_lags)
    return stack, diff.reshape(det_dev, 4, DTLAG)


def solution(mesh):
    return jax.shard_map(
        functools.partial(on_device, mesh.shape["gx"], mesh.shape["gy"]),
        mesh=mesh,
        in_specs=(
            P(("gx", "gy"), None, None),
            P(("gx", "gy"), None, None),
            P(("gx", "gy"), None),
            P(("gx", "gy")),
            P(("gx", "gy")),
            P(("gx", "gy"), None),
        ),
        out_specs=(P(("gx", "gy"), None), P(("gx", "gy"), None, None)),
        check_vma=False,
    )
```
